32 devices in a mesh: groups: 2 (over y), blk: 4 (over z), comp: 2 (over x), lat: 2 (over core).
Axes of the slice: x: 2, y: 2, z: 4, core: 2. Of those that a mesh axis runs over, the one named last changes fastest.
Arguments:
- rhs: float32 [96, 2, 4, 2048], P(('groups', 'comp'), None, 'blk'), parts along dimension 0, may hold values from -6 to 6
- legendre: bfloat16 [4, 2048, 32], P('blk', None, 'lat'), may hold values from -0.03125 to 0.03125
- beam: float32 [24, 2048], replicated, may hold values from 0.3 to 1
- mixing: float32 [24, 48], P(None, 'comp'), may hold values from -0.875 to 0.875
- prior: float32 [48, 2048], P('comp'), may hold values from 0.5 to 4
- inv_noise: float32 [24, 32, 4096], P('comp', ('blk', 'lat')), may hold values from 0.25 to 4
- mask_flags: int32 [24, 32], P('comp', ('blk', 'lat')), may hold values 0 or 1
- cycle_len: int32 [32], P('lat'), may hold values from 16 to 4096, as said below
- cycle_slot: int32 [32], P('lat'), may hold values from 0 to 15, as said below
- m_values: int32 [4], replicated, may hold values from 0 to 2047, as said below
Outputs:
- solution: float32 [96, 2, 4, 2048], P(('groups', 'comp'), None, 'blk'), parts along dimension 0
- residual: float32 [96, 2, 4, 2048], P(('groups', 'comp'), None, 'blk'), parts along dimension 0
The draws below stay inside these ranges and needn't reach their ends.
There are 2 independent parts, one for each index of `groups`. The reference program is written for one: setup_inputs(seed, part) draws one part's arguments, and reference() takes and returns one part's arrays. A program takes and returns all parts, laid end to end along the dimension named above; an argument that names none is the same for every part. Nothing has to cross between parts.
Inputs may be any that keep to these rules, and one draw needn't show every extreme that they name: `cycle_len`: lengths are multiples of 4; each band (aligned block of 16 entries) holds a cycle of exactly 4096 pixels. `cycle_slot`: each aligned block of 16 entries is a permutation of 0 to 15. `m_values`: the m values are distinct, and both 0 and 2047 occur.
All inputs are finite; a program needn't handle non-finite values. No bound on the sum of `mask_flags` on one device may be relied on, other than what follows from the above.
Results may differ from the reference program's by a relative error of at most 0.023.
Values may be sent and summed in bfloat16 or wider, within the bound.
No kernel may reach another device: no remote copies, remote signals or barrier semaphores. Data moves between devices by JAX's collectives and lax.ppermute only.
A program may use at most 64 MiB of HBM per device.

```python
import math
import jax
import jax.numpy as jnp
from jax import lax

L = 2048
C = 48
F = 24
PMAX = 4096
R_DEV = 4
ITERS = 3
RB = 16
CYCLES = 32
M_TOT = 4
N_LAT = 2


def draw_cycle_len(key, part):
    quarter = PMAX // 4
    draw_one = jax.random.randint(jax.random.fold_in(key, 11), (CYCLES,), 1, quarter + 1)
    draw_two = jax.random.randint(jax.random.fold_in(key, 12), (CYCLES,), 1, quarter + 1)
    lengths = 4 * jnp.maximum(4, jnp.maximum(draw_one, draw_two))
    longest = jax.random.randint(jax.random.fold_in(key, 13), (CYCLES // RB,), 0, RB)
    positions = jnp.arange(CYCLES, dtype=jnp.int32)
    chosen = positions % RB == jnp.repeat(longest, RB, total_repeat_length=CYCLES)
    return jnp.where(chosen, PMAX, lengths).astype(jnp.int32)


def band_order(band_key):
    return jax.random.permutation(band_key, RB)


def draw_cycle_slot(key, part):
    band_keys = jax.random.split(jax.random.fold_in(key, 21), CYCLES // RB)
    orders = jax.vmap(band_order)(band_keys)
    return orders.reshape(CYCLES).astype(jnp.int32)


def draw_m_values(key, part):
    middle = jax.random.permutation(jax.random.fold_in(key, 31), L - 2)[:M_TOT] + 1
    lowest_at = jax.random.randint(jax.random.fold_in(key, 32), (), 0, M_TOT)
    offset = jax.random.randint(jax.random.fold_in(key, 33), (), 1, M_TOT)
    highest_at = (lowest_at + offset) % M_TOT
    positions = jnp.arange(M_TOT, dtype=jnp.int32)
    values = jnp.where(positions == lowest_at, 0, middle)
    values = jnp.where(positions == highest_at, L - 1, values)
    return values.astype(jnp.int32)


def set_ends(values, stream_key, least, largest):
    spot = [jax.random.randint(jax.random.fold_in(stream_key, axis), (), 0, length) for axis, length in enumerate(values.shape)]
    main_axis = values.shape.index(max(values.shape))
    next_to = spot[:main_axis] + [(spot[main_axis] + 1) % values.shape[main_axis]] + spot[main_axis + 1:]
    return values.at[tuple(spot)].set(least).at[tuple(next_to)].set(largest)


def block_scale(own_key, dims, shards, least, largest):
    level = 1.0
    for dim, parts in shards:
        draws = jax.random.uniform(jax.random.fold_in(jax.random.fold_in(own_key, 6), dim), (parts,), jnp.float32, least / len(shards), largest / len(shards))
        level = level * jnp.repeat(jnp.exp(draws), dims[dim] // parts).reshape((-1,) + (1,) * (len(dims) - 1 - dim))
    return level


def bell_draw(own_key, extent, spread, reach, shards=(), kind=jnp.bfloat16):
    array = spread * jax.random.normal(own_key, extent, jnp.float32)
    if shards:
        array = array * block_scale(own_key, extent, shards, -0.22, 0.18)
    return jnp.clip(array, -reach, reach).astype(kind)


def setup_inputs(seed: int = 0, part: int = 0) -> dict:
    splits = jax.random.split(jax.random.key(seed), 11)
    part_keys = jax.random.split(jax.random.fold_in(splits[10], part), 11)
    rhs = bell_draw(part_keys[0], (C, 2, M_TOT, L), 1.0, 6.0, ((0, 2), (2, 4)), jnp.float32)
    legendre = bell_draw(splits[1], (M_TOT, L, CYCLES), (CYCLES * PMAX // 4) ** -0.5, 0.03125, ((0, 4), (2, 2)))
    beam = jnp.clip(jnp.exp(jax.random.uniform(splits[2], (F, L), jnp.float32, math.log(0.3), math.log(1.0))), 0.3, 1.0)
    mixing = bell_draw(splits[3], (F, C), C ** -0.5, 0.875, ((1, 2),), jnp.float32)
    prior = jnp.clip(jnp.exp(math.log(4.0) - 2.0794415 * jax.random.uniform(splits[4], (C, L), jnp.float32) ** block_scale(splits[4], (C, L), ((0, 2),), -0.2, 0.2)), 0.5, 4.0)
    inv_noise = jnp.clip(jnp.exp(math.log(4.0) - 2.7725887 * jax.random.uniform(splits[5], (F, CYCLES, PMAX), jnp.float32) ** block_scale(splits[5], (F, CYCLES, PMAX), ((0, 2), (1, 8)), -0.2, 0.2)), 0.25, 4.0)
    mask_flags = set_ends((jax.random.randint(splits[6], (F, CYCLES), 0, 8) < 7).astype(jnp.int32), jax.random.fold_in(splits[6], 1), 0, 1)
    cycle_len = draw_cycle_len(jax.random.fold_in(splits[10], 71), part)
    cycle_slot = draw_cycle_slot(jax.random.fold_in(splits[10], 71), part)
    m_values = draw_m_values(jax.random.fold_in(splits[10], 71), part)
    return {"rhs": rhs, "legendre": legendre, "beam": beam, "mixing": mixing, "prior": prior, "inv_noise": inv_noise, "mask_flags": mask_flags, "cycle_len": cycle_len, "cycle_slot": cycle_slot, "m_values": m_values}


HIGHEST_PRECISION = lax.Precision.HIGHEST


def cycle_table(m_values, length):
    pixels = jnp.arange(PMAX, dtype=jnp.int32)
    phase_ids = (m_values[:, None] * (2 * pixels[None, :] + 1)) % (2 * length)
    angles = math.pi * phase_ids.astype(jnp.float32) / length.astype(jnp.float32)
    inside = (pixels < length)[None, :]
    cosine = jnp.where(inside, jnp.cos(angles), jnp.float32(0.0))
    sine_part = jnp.where(inside, -jnp.sin(angles), jnp.float32(0.0))
    return jnp.stack([cosine, sine_part]).astype(jnp.bfloat16)


def slot_columns(cycle_len, cycle_slot):
    slot_ids = jnp.arange(CYCLES, dtype=jnp.int32)
    owners = slot_ids // (N_LAT * R_DEV)
    band_ids = (slot_ids // R_DEV) % N_LAT
    places = slot_ids % R_DEV
    cycle_ids = cycle_slot[band_ids * RB + owners * R_DEV + places]
    columns = (band_ids * RB + cycle_ids).astype(jnp.int32)
    return columns, cycle_len[columns]


def apply_operator(vector, mixing, beam, prior, legendre_slot, inv_noise, mask_flags, lengths, m_values):
    blended = jnp.einsum('fc,ckml->fkml', mixing, vector, precision=HIGHEST_PRECISION)
    blended = (blended * beam[:, None, None, :]).astype(jnp.bfloat16)
    legendre_wide = legendre_slot.astype(jnp.float32)
    coeffs = jnp.einsum('fkml,mlg->fkmg', blended.astype(jnp.float32), legendre_wide,
                        precision=HIGHEST_PRECISION).astype(jnp.bfloat16)

    def one_slot(slot_items):
        coeff_slot, noise_slot, mask_slot, length = slot_items
        trig_table = cycle_table(m_values, length).astype(jnp.float32)
        sky_map = jnp.einsum('fkm,kmp->fp', coeff_slot.astype(jnp.float32), trig_table,
                             precision=HIGHEST_PRECISION)
        weighted = (mask_slot.astype(jnp.float32)[:, None] * noise_slot * sky_map).astype(jnp.bfloat16)
        return jnp.einsum('fp,kmp->fkm', weighted.astype(jnp.float32), trig_table,
                          precision=HIGHEST_PRECISION).astype(jnp.bfloat16)

    projected = lax.map(one_slot, (jnp.moveaxis(coeffs, 3, 0), jnp.moveaxis(inv_noise, 1, 0),
                                   jnp.moveaxis(mask_flags, 1, 0), lengths))
    projected = jnp.moveaxis(projected, 0, 3)
    harmonic = jnp.einsum('fkmg,mlg->fkml', projected.astype(jnp.float32), legendre_wide,
                          precision=HIGHEST_PRECISION)
    backward = jnp.einsum('fc,fkml->ckml', mixing, harmonic * beam[:, None, None, :],
                          precision=HIGHEST_PRECISION)
    return prior[:, None, None, :] * vector + backward


def reference(rhs, legendre, beam, mixing, prior, inv_noise, mask_flags, cycle_len, cycle_slot, m_values):
    columns, lengths = slot_columns(cycle_len, cycle_slot)
    legendre_slot = legendre[:, :, columns]
    solution = jnp.zeros_like(rhs)
    residual = rhs
    direction = rhs
    for iteration in range(ITERS):
        applied = apply_operator(direction, mixing, beam, prior, legendre_slot, inv_noise,
                                 mask_flags, lengths, m_values)
        curvature = jnp.sum(direction * applied)
        cross_term = jnp.sum(residual * applied)
        square = jnp.sum(applied * applied)
        norm_now = jnp.sum(residual * residual)
        step_size = norm_now / curvature
        solution = solution + step_size * direction
        residual = residual - step_size * applied
        norm_next = norm_now - 2.0 * step_size * cross_term + step_size * step_size * square
        direction = residual + (norm_next / norm_now) * direction
    return solution, residual
```

```python
import math

import jax
import jax.numpy as jnp
from jax import lax
from jax.experimental import pallas as pl
from jax.experimental.pallas import tpu as pltpu
from jax.sharding import PartitionSpec as P

ITERS = 3
LANES = 128
SUBLANES = 8
WIDE = 512
MOMENTS = 2 * ITERS
POWERS = 2 * ITERS - 1
HIGHEST_PRECISION = lax.Precision.HIGHEST
F32 = jnp.float32
BF16 = jnp.bfloat16


def nt_dot(a, b):
    return lax.dot_general(a, b, (((1,), (1,)), ((), ())), preferred_element_type=F32)


def nn_dot(a, b):
    return jnp.dot(a, b, preferred_element_type=F32)


def iota(shape, dim):
    return lax.broadcasted_iota(jnp.int32, shape, dim)


def halves(x):
    high = x.astype(BF16)
    return high, (x - high.astype(F32)).astype(BF16)


def half_turn_sine(u):
    square = u * u
    total = jnp.full_like(u, -(math.pi**11) / math.factorial(11))
    for power in (9, 7, 5, 3, 1):
        sign = 1.0 if power % 4 == 1 else -1.0
        total = total * square + sign * math.pi**power / math.factorial(power)
    return total * u


def gather_kernel(
    rhs_ref, legendre_ref, beam_ref, mixing_ref, prior_ref, noise_ref, mask_ref, len_ref, slot_ref, m_ref,
    out_ref, gram_ref,
):
    channel_width, cycle_count, pixel_count = noise_ref.shape
    comp_count, l_count = prior_ref.shape
    channel_count = beam_ref.shape[0]
    m_count = m_ref.shape[0]
    band_cycles = legendre_ref.shape[0]
    rows = 2 * m_count
    owner = lax.axis_index("blk")
    band = lax.axis_index("lat")
    bands = lax.axis_size("lat")

    row_ids = iota((rows, 1), 0)
    m_column = jnp.zeros((rows, 1), F32)
    for i in range(m_count):
        m_column = jnp.where(row_ids % m_count == i, m_ref[i].astype(F32), m_column)
    quarter = jnp.where(row_ids < m_count, 0.0, 0.25).astype(F32)
    lane_ids = iota((1, LANES), 1)
    chunk = min(WIDE, pixel_count)
    lengths = [len_ref[slot_ref[owner * cycle_count + q]] for q in range(cycle_count)]
    doubles = [jnp.full((rows, 1), (2 * n).astype(F32), F32) for n in lengths]
    inverses = [1.0 / double for double in doubles]
    sums = [jnp.zeros((rows, LANES), F32) for q in range(cycle_count)]
    padding = jnp.zeros((LANES - channel_width * rows, chunk), F32)
    for start in range(0, pixel_count, chunk):
        pixels = iota((rows, chunk), 1) + start
        phases = m_column * (2 * pixels + 1).astype(F32)
        for q in range(cycle_count):
            rest = phases - jnp.floor(phases * inverses[q] + 0.5) * doubles[q]
            turns = rest * inverses[q] + quarter
            turns = turns - jnp.floor(turns + 0.5)
            sine = half_turn_sine(turns)
            table = jnp.where(pixels < lengths[q], 1.0 - 2.0 * sine * sine, 0.0).astype(BF16)
            wide = table.astype(F32)
            weighted = [noise_ref[f, q : q + 1, start : start + chunk] * wide for f in range(channel_width)]
            weighted = jnp.concatenate(weighted + [padding], axis=0).astype(BF16)
            sums[q] = sums[q] + nt_dot(table, weighted)
    for q in range(cycle_count):
        flags = jnp.zeros((1, LANES), F32)
        for f in range(channel_width):
            flags = jnp.where(lane_ids // rows == f, mask_ref[q, f].astype(F32), flags)
        gram = sums[q] * flags
        gram_ref[q * m_count : (q + 1) * m_count, :LANES] = gram[:m_count]
        gram_ref[q * m_count : (q + 1) * m_count, LANES:] = gram[m_count:]

    mixing = mixing_ref[...].astype(BF16)
    groups = l_count // LANES
    moments = [jnp.zeros((comp_count, 2 * LANES), F32) for n in range(MOMENTS)]
    used = POWERS * 2 * channel_count
    images = jnp.zeros((band_cycles, 2 * LANES), F32)
    filler = jnp.zeros((2 * LANES - used, 2 * LANES), F32)
    for pair in range(0, groups, 2):
        parts = []
        for group in (pair, pair + 1):
            lanes = slice(group * LANES, (group + 1) * LANES)
            vector = jnp.concatenate(
                [rhs_ref[pl.ds(k * groups + group, comp_count, stride=2 * groups), :] for k in range(2)], axis=1
            )
            prior = jnp.concatenate([prior_ref[:, lanes]] * 2, axis=1)
            powers = [vector]
            for n in range(1, POWERS):
                powers.append(prior * powers[-1])
            for n in range(MOMENTS):
                moments[n] = moments[n] + powers[n // 2] * powers[n - n // 2]
            mixed = nn_dot(mixing, jnp.concatenate(powers, axis=1).astype(BF16))
            beam = beam_ref[:, lanes]
            parts.append([mixed[:, i * LANES : (i + 1) * LANES] * beam for i in range(2 * POWERS)])
        blended = jnp.concatenate(
            [jnp.concatenate([parts[0][i], parts[1][i]], axis=1) for i in range(2 * POWERS)] + [filler], axis=0
        )
        images = images + nt_dot(
            legendre_ref[:, pair * LANES : (pair + 2) * LANES], blended.astype(BF16)
        )

    count = cycle_count * m_count
    message_rows = iota((count, LANES), 0)
    lanes = iota((count, LANES), 1)
    slots = jnp.zeros((count, LANES), jnp.int32)
    for q in range(cycle_count):
        slots = jnp.where(message_rows // m_count == q, slot_ref[owner * cycle_count + q], slots)
    wanted = (message_rows % m_count * bands + band) * band_cycles + slots
    held = (owner * bands + band) * band_cycles + message_rows
    first = gram_ref[:, :LANES]
    base = channel_width * rows
    first = jnp.where(lanes == base, wanted.astype(F32), first)
    first = jnp.where(lanes == base + 1, held.astype(F32), first)
    totals = jnp.zeros((count, LANES), F32)
    for n in range(MOMENTS):
        total = jnp.sum(jnp.sum(moments[n], axis=0, keepdims=True), axis=1, keepdims=True)
        totals = jnp.where(message_rows == n, total, totals)
    for piece in range(3):
        part = totals.astype(BF16).astype(F32)
        first = jnp.where(lanes == base + 2 + piece, part, first)
        totals = totals - part
    out_ref[:count, :LANES] = first.astype(BF16)
    out_ref[:count, LANES : 2 * LANES] = gram_ref[:, LANES:].astype(BF16)
    out_ref[:count, 2 * LANES :] = images.astype(BF16)
    for piece in range(l_count // WIDE):
        out_ref[count * (piece + 1) : count * (piece + 2), :] = legendre_ref[:, piece * WIDE : (piece + 1) * WIDE]


def iterate_kernel(
    near_ref, far_ref, rhs_ref, beam_ref, own_mixing_ref, other_mixing_ref, own_prior_ref, other_prior_ref,
    solution_ref, residual_ref, legendre_ref, doubled_ref, channel_width, m_count, block_count,
):
    comp_count, l_count = own_prior_ref.shape
    channel_count = beam_ref.shape[0]
    rows = 2 * m_count
    pieces = l_count // WIDE
    count = near_ref.shape[0] // (block_count * (2 + pieces))
    stride = count * (1 + pieces)
    cycles = 2 * block_count * count
    small = channel_count * rows
    base = channel_width * rows
    owner = lax.axis_index("blk")
    comp = lax.axis_index("comp")

    own_rows, other_rows = [], []
    for ref in (near_ref, far_ref):
        for i in range(block_count):
            own_rows.append(ref[i * stride : i * stride + count, :])
        for i in range(block_count):
            begin = block_count * stride + i * count
            other_rows.append(ref[begin : begin + count, :])
    own_rows = jnp.concatenate(own_rows, axis=0).astype(F32)
    other_rows = jnp.concatenate(other_rows, axis=0).astype(F32)

    pieces_sum = own_rows[:, :LANES] + other_rows[:, :LANES]
    scalars = []
    for n in range(MOMENTS):
        total = jnp.zeros((1, LANES), F32)
        for i in range(block_count):
            total = total + pieces_sum[i * count + n : i * count + n + 1, :]
        lane = iota((1, LANES), 1)
        keep = (lane >= base + 2) & (lane < base + 5)
        scalars.append(jnp.sum(jnp.where(keep, total, 0.0), axis=1, keepdims=True))

    wanted = own_rows[:, base : base + 1]
    held = jnp.transpose(jnp.broadcast_to(own_rows[:, base + 1 : base + 2], (cycles, cycles)))
    pick = jnp.where(wanted == held, 1.0, 0.0).astype(BF16)
    for piece in range(pieces):
        blocks = []
        for ref in (near_ref, far_ref):
            for i in range(block_count):
                begin = i * stride + count * (piece + 1)
                blocks.append(ref[begin : begin + count, :])
        legendre_ref[:, piece * WIDE : (piece + 1) * WIDE] = nn_dot(pick, jnp.concatenate(blocks, axis=0)).astype(BF16)

    row = iota((small, cycles), 0)
    lane = iota((small, cycles), 1)
    same_m = row % m_count == lane % m_count
    summed = jnp.transpose((own_rows + other_rows)[:, 2 * LANES :])
    high, low = halves(summed)
    images = nt_dot(jnp.concatenate([high, low], axis=1), jnp.concatenate([pick, pick], axis=1))
    width = 2 * channel_count
    images = jnp.concatenate([images[n * width : (n + 1) * width] for n in range(POWERS)], axis=1)
    high, low = halves(images)
    spread_row = iota((small, width), 0)
    spread_lane = iota((small, width), 1)
    spread = (spread_row // rows == spread_lane % channel_count) & (
        spread_row % rows // m_count == spread_lane // channel_count
    )
    spread = jnp.where(spread, 1.0, 0.0).astype(BF16)
    images = nn_dot(spread, high) + nn_dot(spread, low)
    y = [jnp.where(same_m, images[:, n * cycles : (n + 1) * cycles], 0.0) for n in range(POWERS)]

    own_gram = jnp.transpose(own_rows[:, : 2 * LANES])
    other_gram = jnp.transpose(other_rows[:, : 2 * LANES])
    first_gram = jnp.where(comp == 0, own_gram, other_gram)
    second_gram = jnp.where(comp == 0, other_gram, own_gram)
    grams = []
    for k in range(2):
        gram = jnp.concatenate(
            [first_gram[k * LANES : k * LANES + base], second_gram[k * LANES : k * LANES + base]], axis=0
        )
        grams.append(gram.reshape(channel_count, rows, cycles))
    group = jnp.where(
        iota((2 * cycles, cycles), 0) % cycles // m_count == iota((2 * cycles, cycles), 1) // m_count, 1.0, 0.0
    ).astype(BF16)

    def sky(image):
        image = image.reshape(channel_count, rows, cycles)
        cosine = jnp.sum(image[:, :m_count], axis=1, keepdims=True)
        sine = jnp.sum(image[:, m_count:], axis=1, keepdims=True)
        product = (grams[0] * cosine + grams[1] * sine).reshape(small, cycles)
        high, low = halves(product)
        result = nn_dot(jnp.concatenate([high, low], axis=1), group)
        return jnp.where(same_m, result, 0.0)

    expand = jnp.where(iota((small, channel_count), 0) // rows == iota((small, channel_count), 1), 1.0, 0.0)
    expand = expand.astype(BF16)
    same_row = iota((small, small), 0) % rows == iota((small, small), 1) % rows

    def spread_matrix(matrix):
        tall = nn_dot(expand, matrix).astype(BF16)
        return jnp.where(same_row, nt_dot(tall, expand), 0.0).astype(BF16)

    def spread_transpose(matrix):
        tall = nt_dot(expand, matrix).astype(BF16)
        return jnp.where(same_row, nt_dot(tall, expand), 0.0).astype(BF16)

    own_mixing = own_mixing_ref[...].astype(BF16)
    other_mixing = other_mixing_ref[...].astype(BF16)
    both = (nt_dot(own_mixing, own_mixing) + nt_dot(other_mixing, other_mixing)).astype(BF16)
    square_matrix = spread_matrix(both)
    forward = [spread_matrix(own_mixing), spread_matrix(other_mixing)]
    backward = [spread_transpose(own_mixing), spread_transpose(other_mixing)]
    priors = (own_prior_ref, other_prior_ref)

    def dot(a, b):
        return jnp.sum(jnp.sum(a * b, axis=0, keepdims=True), axis=1, keepdims=True)

    chunk = 2 * LANES
    starts = range(0, l_count, chunk)

    def harmonic(z, start):
        table = legendre_ref[:, start : start + chunk]
        beam = beam_ref[:, start : start + chunk][:, None, :]
        value = nn_dot(z, table).reshape(channel_count, rows, chunk) * beam
        return table, beam, value.reshape(small, chunk).astype(BF16)

    def analyse(value, table, beam):
        value = value.reshape(channel_count, rows, chunk) * beam
        return nt_dot(value.reshape(small, chunk).astype(BF16), table)

    def first_pass(z):
        z = z.astype(BF16)
        plain = jnp.zeros((small, cycles), F32)
        primed = jnp.zeros((small, cycles), F32)
        second = jnp.zeros((rows, chunk), F32)
        third = jnp.zeros((rows, chunk), F32)
        for start in starts:
            table, beam, value = harmonic(z, start)
            plain = plain + analyse(nn_dot(square_matrix, value), table, beam)
            mixed = jnp.zeros((small, chunk), F32)
            for side in range(2):
                prior = priors[side][:, start : start + chunk][:, None, :]
                once = nn_dot(backward[side], value).reshape(comp_count, rows, chunk) * prior
                twice = once * prior
                second = second + jnp.sum(once * once, axis=0)
                third = third + jnp.sum(once * twice, axis=0)
                mixed = mixed + nn_dot(forward[side], once.reshape(small, chunk).astype(BF16))
                doubled_ref[side, :, start : start + chunk] = twice.reshape(small, chunk).astype(BF16)
            primed = primed + analyse(mixed, table, beam)
        return (
            jnp.where(same_m, plain, 0.0),
            jnp.where(same_m, primed, 0.0),
            jnp.sum(jnp.sum(second, axis=0, keepdims=True), axis=1, keepdims=True),
            jnp.sum(jnp.sum(third, axis=0, keepdims=True), axis=1, keepdims=True),
        )

    def second_pass(z):
        z = z.astype(BF16)
        plain = jnp.zeros((small, cycles), F32)
        cross = jnp.zeros((rows, chunk), F32)
        own = jnp.zeros((rows, chunk), F32)
        for start in starts:
            table, beam, value = harmonic(z, start)
            plain = plain + analyse(nn_dot(square_matrix, value), table, beam)
            for side in range(2):
                prior = priors[side][:, start : start + chunk][:, None, :]
                vector = nn_dot(backward[side], value).reshape(comp_count, rows, chunk)
                twice = doubled_ref[side, :, start : start + chunk].astype(F32).reshape(comp_count, rows, chunk)
                cross = cross + jnp.sum(vector * twice, axis=0)
                own = own + jnp.sum(vector * vector * prior, axis=0)
        return (
            jnp.where(same_m, plain, 0.0),
            jnp.sum(jnp.sum(cross, axis=0, keepdims=True), axis=1, keepdims=True),
            jnp.sum(jnp.sum(own, axis=0, keepdims=True), axis=1, keepdims=True),
        )

    s = scalars
    z0 = sky(y[0])
    y_plain0, y_prime0, pp00, ppp00 = first_pass(z0)
    norm0 = s[0]
    step0 = norm0 / (s[1] + dot(y[0], z0))
    p00, uu00 = dot(z0, y_prime0), dot(z0, y_plain0)
    by0, by1, by2, by3, by4 = [dot(y[n], z0) for n in range(5)]
    norm1 = s[0] - 2.0 * step0 * (s[1] + by0) + step0 * step0 * (s[2] + 2.0 * by1 + uu00)
    ratio0 = norm1 / norm0
    y_r1 = y[0] - step0 * (y[1] + y_plain0)
    y_d1 = y_r1 + ratio0 * y[0]
    e0, e1, e2 = 1.0 + ratio0, -step0, -step0
    z1 = sky(y_d1)
    y_plain1, p2_01, p_11 = second_pass(z1)
    quadratic1 = (
        e0 * e0 * s[1] + 2.0 * e0 * e1 * s[2] + e1 * e1 * s[3]
        + 2.0 * e0 * e2 * by1 + 2.0 * e1 * e2 * by2 + e2 * e2 * p00
    )
    step1 = norm1 / (quadratic1 + dot(y_d1, z1))
    y_pd1 = e0 * y[1] + e1 * y[2] + e2 * y_prime0
    h0, h1, h2 = 1.0 + 0.0 * step1, -step0 - step1 * e0, -step1 * e1
    h3, h4, h5 = -step0, -step1 * e2, -step1
    b1y = [dot(y[n], z1) for n in range(4)]
    uu01, p01, uu11 = dot(z1, y_plain0), dot(z1, y_prime0), dot(z1, y_plain1)
    norm2 = (
        h0 * h0 * s[0] + 2.0 * h0 * h1 * s[1] + (h1 * h1 + 2.0 * h0 * h2) * s[2]
        + 2.0 * h1 * h2 * s[3] + h2 * h2 * s[4]
        + 2.0 * h3 * (h0 * by0 + h1 * by1 + h2 * by2)
        + 2.0 * h4 * (h0 * by1 + h1 * by2 + h2 * by3)
        + 2.0 * h5 * (h0 * b1y[0] + h1 * b1y[1] + h2 * b1y[2])
        + h3 * h3 * uu00 + 2.0 * h3 * h4 * p00 + h4 * h4 * pp00
        + 2.0 * h3 * h5 * uu01 + 2.0 * h4 * h5 * p01 + h5 * h5 * uu11
    )
    ratio1 = norm2 / norm1
    y_d2 = y_r1 - step1 * (y_pd1 + y_plain1) + ratio1 * y_d1
    z2 = sky(y_d2)
    h0, h1, h3 = h0 + ratio1 * e0, h1 + ratio1 * e1, h3 + ratio1 * e2
    quadratic2 = (
        h0 * h0 * s[1] + 2.0 * h0 * h1 * s[2] + (h1 * h1 + 2.0 * h0 * h2) * s[3]
        + 2.0 * h1 * h2 * s[4] + h2 * h2 * s[5]
        + 2.0 * h3 * (h0 * by1 + h1 * by2 + h2 * by3)
        + 2.0 * h4 * (h0 * by2 + h1 * by3 + h2 * by4)
        + 2.0 * h5 * (h0 * b1y[1] + h1 * b1y[2] + h2 * b1y[3])
        + h3 * h3 * p00 + 2.0 * h3 * h4 * pp00 + h4 * h4 * ppp00
        + 2.0 * h3 * h5 * p01 + 2.0 * h4 * h5 * p2_01 + h5 * h5 * p_11
    )
    step2 = norm2 / (quadratic2 + dot(y_d2, z2))

    mine_row = iota((width, small), 0)
    mine_lane = iota((width, small), 1)
    mine = (mine_lane // rows == mine_row % channel_count) & (
        mine_lane % rows == mine_row // channel_count * m_count + owner
    )
    mine = jnp.where(mine, 1.0, 0.0).astype(BF16)
    stacked = jnp.concatenate([z.astype(BF16) for z in (z0, z1, z2)], axis=1)
    stacked = nn_dot(mine, stacked).astype(BF16)
    stacked = jnp.concatenate([stacked[:, i * cycles : (i + 1) * cycles] for i in range(ITERS)], axis=0)
    groups = l_count // LANES
    for start in starts:
        table = legendre_ref[:, start : start + chunk]
        beam = beam_ref[:, start : start + chunk]
        value = nn_dot(stacked, table)
        value = [value[i * channel_count : (i + 1) * channel_count] * beam for i in range(2 * ITERS)]
        value = jnp.concatenate(value, axis=1).astype(BF16)
        vectors = lax.dot_general(own_mixing, value, (((0,), (0,)), ((), ())), preferred_element_type=F32)
        for part in range(chunk // LANES):
            prior = own_prior_ref[:, start + part * LANES : start + (part + 1) * LANES]
            for k in range(2):
                place = pl.ds(k * groups + start // LANES + part, comp_count, stride=2 * groups)
                u = []
                for i in range(ITERS):
                    begin = (2 * i + k) * chunk + part * LANES
                    u.append(vectors[:, begin : begin + LANES])
                b = rhs_ref[place, :]
                r1 = b - step0 * (prior * b + u[0])
                d1 = r1 + ratio0 * b
                r2 = r1 - step1 * (prior * d1 + u[1])
                d2 = r2 + ratio1 * d1
                solution_ref[place, :] = step0 * b + step1 * d1 + step2 * d2
                residual_ref[place, :] = r2 - step2 * (prior * d2 + u[2])


def swap(x, axis):
    return lax.ppermute(x, axis, [(0, 1), (1, 0)])


def compact(
    rhs, legendre, beam, mixing, prior, inv_noise, mask_flags, cycle_len, cycle_slot, m_values
):
    comp_count, parts, m_own, l_count = rhs.shape
    block_count = lax.axis_size("blk")
    m_count = m_values.shape[0]
    channel_width, cycle_count = mask_flags.shape
    channel_count = beam.shape[0]
    count = cycle_count * m_count
    vmem = pl.BlockSpec(memory_space=pltpu.VMEM)
    smem = pl.BlockSpec(memory_space=pltpu.SMEM)
    flat = rhs.reshape(comp_count * parts * l_count // LANES, LANES)
    message = pl.pallas_call(
        gather_kernel,
        out_shape=jax.ShapeDtypeStruct((count * (1 + l_count // WIDE), WIDE), BF16),
        in_specs=[vmem] * 6 + [smem] * 4,
        out_specs=vmem,
        scratch_shapes=[pltpu.VMEM((count, 2 * LANES), F32)],
        compiler_params=pltpu.CompilerParams(vmem_limit_bytes=48 * 1024 * 1024),
        name="gather_kernel",
    )(
        flat, jnp.transpose(legendre[0]), beam, mixing, prior, inv_noise, jnp.transpose(mask_flags),
        cycle_len, cycle_slot, m_values,
    )
    other_prior = swap(prior, "comp")
    other_mixing = swap(mixing, "comp")
    blocks = [message]
    for shift in range(1, block_count):
        blocks.append(lax.ppermute(message, "blk", [(i, (i + shift) % block_count) for i in range(block_count)]))
    crossing = swap(jnp.concatenate([block[:count] for block in blocks], axis=0), "comp")
    near = jnp.concatenate(blocks + [crossing], axis=0)
    far = swap(near, "lat")

    def kernel(*refs):
        iterate_kernel(*refs, channel_width, m_count, block_count)

    small = channel_count * 2 * m_count
    cycles = 2 * block_count * count
    answers = pl.pallas_call(
        kernel,
        out_shape=[jax.ShapeDtypeStruct(flat.shape, F32)] * 2,
        in_specs=[vmem] * 8,
        out_specs=[vmem] * 2,
        scratch_shapes=[pltpu.VMEM((cycles, l_count), BF16), pltpu.VMEM((2, small, l_count), BF16)],
        compiler_params=pltpu.CompilerParams(vmem_limit_bytes=48 * 1024 * 1024),
        name="iterate_kernel",
    )(near, far, flat, beam, mixing, other_mixing, prior, other_prior)
    return tuple(answer.reshape(rhs.shape) for answer in answers)


def cycle_table(m_values, length, pixel_count):
    pixels = jnp.arange(pixel_count, dtype=jnp.int32)
    phase_ids = m_values[:, None] * (2 * pixels[None, :] + 1) % (2 * length)
    angles = math.pi * phase_ids.astype(jnp.float32) / length.astype(jnp.float32)
    inside = (pixels < length)[None, :]
    cosine = jnp.where(inside, jnp.cos(angles), jnp.float32(0.0))
    sine_part = jnp.where(inside, -jnp.sin(angles), jnp.float32(0.0))
    return jnp.stack([cosine, sine_part]).astype(jnp.bfloat16)


def distributed(
    rhs, legendre, beam, mixing, prior, inv_noise, mask_flags, cycle_len, cycle_slot, m_values
):
    cycle_count = inv_noise.shape[1]
    pixel_count = inv_noise.shape[2]
    channel_width = inv_noise.shape[0]
    owner_index = lax.axis_index("blk")
    comp_index = lax.axis_index("comp")
    local_ids = lax.dynamic_slice_in_dim(cycle_slot, owner_index * cycle_count, cycle_count)
    local_lengths = cycle_len[local_ids]
    legendre_slot = legendre[:, :, cycle_slot]
    weights = mask_flags.astype(jnp.float32)
    own_beam = lax.dynamic_slice_in_dim(beam, comp_index * channel_width, channel_width, 0)
    stored = jax.vmap(cycle_table, in_axes=(None, 0, None))(m_values, local_lengths, pixel_count)
    solution = jnp.zeros_like(rhs)
    residual = rhs
    direction = rhs
    for iteration in range(ITERS):
        local_mix = jnp.einsum("fc,ckml->fkml", mixing, direction, precision=HIGHEST_PRECISION)
        summed = lax.psum(local_mix.astype(jnp.bfloat16), "comp").astype(jnp.float32)
        own_part = lax.dynamic_slice_in_dim(summed, comp_index * channel_width, channel_width, 0)
        blended = (own_part * own_beam[:, None, None, :]).astype(jnp.bfloat16)
        coeffs = jnp.einsum(
            "fkml,mlr->fkmr", blended, legendre_slot, preferred_element_type=jnp.float32
        ).astype(jnp.bfloat16)
        arrived = lax.all_to_all(coeffs, "blk", split_axis=3, concat_axis=2, tiled=True)
        sky_map = jnp.einsum("fkmq,qkmp->fqp", arrived, stored, preferred_element_type=jnp.float32)
        weighted = (weights[:, :, None] * inv_noise * sky_map).astype(jnp.bfloat16)
        projected = jnp.einsum(
            "fqp,qkmp->fkmq", weighted, stored, preferred_element_type=jnp.float32
        ).astype(jnp.bfloat16)
        returned = lax.all_to_all(projected, "blk", split_axis=2, concat_axis=3, tiled=True)
        harmonic = jnp.einsum(
            "fkms,mls->fkml", returned, legendre_slot, preferred_element_type=jnp.float32
        )
        everyone = lax.all_gather(
            harmonic.astype(jnp.bfloat16), ("comp", "lat"), axis=0, tiled=True
        ).astype(harmonic.dtype)
        stacked = everyone.reshape(
            (lax.axis_size("comp"), lax.axis_size("lat"), channel_width) + harmonic.shape[1:]
        )
        summed_bands = jnp.sum(stacked, axis=1).reshape((-1,) + harmonic.shape[1:])
        backward = jnp.einsum(
            "fc,fkml->ckml",
            mixing,
            summed_bands * beam[:, None, None, :],
            precision=HIGHEST_PRECISION,
        )
        applied = prior[:, None, None, :] * direction + backward
        totals = lax.psum(
            (
                jnp.sum(direction * applied),
                jnp.sum(residual * applied),
                jnp.sum(applied * applied),
                jnp.sum(residual * residual),
            ),
            ("blk", "comp"),
        )
        curvature, cross_term, square, norm_now = totals
        step_size = norm_now / curvature
        solution = solution + step_size * direction
        residual = residual - step_size * applied
        norm_next = norm_now - 2.0 * step_size * cross_term + step_size * step_size * square
        direction = residual + norm_next / norm_now * direction
    return (solution, residual)


def fits(mesh, rhs, legendre, beam, mixing, inv_noise, m_values):
    sizes = dict(mesh.shape)
    m_count = m_values.shape[0]
    cycles = legendre.shape[2]
    slots = cycles // (sizes["blk"] * sizes["lat"])
    channels = beam.shape[0]
    width = channels // sizes["comp"]
    comps = mixing.shape[1] // sizes["comp"]
    l_count = legendre.shape[1]
    return (
        sizes["comp"] == 2
        and sizes["lat"] == 2
        and m_count == sizes["blk"]
        and 2 * m_count == SUBLANES
        and cycles * m_count == LANES
        and slots * m_count == cycles // sizes["lat"] == 16
        and comps == channels
        and channels % SUBLANES == 0
        and width * SUBLANES + 5 <= LANES
        and 2 * POWERS * channels <= 2 * LANES
        and l_count % WIDE == 0
        and inv_noise.shape[2] % WIDE == 0
        and rhs.shape[1] == 2
        and MOMENTS <= 16
    )


def solution(mesh):
    in_specs = (
        P(("groups", "comp"), None, "blk", None),
        P("blk", None, "lat"),
        P(),
        P(None, "comp"),
        P("comp", None),
        P("comp", ("blk", "lat"), None),
        P("comp", ("blk", "lat")),
        P("lat"),
        P("lat"),
        P(),
    )
    out_specs = (P(("groups", "comp"), None, "blk", None), P(("groups", "comp"), None, "blk", None))

    def whole(rhs, legendre, beam, mixing, prior, inv_noise, mask_flags, cycle_len, cycle_slot, m_values):
        small = fits(mesh, rhs, legendre, beam, mixing, inv_noise, m_values)
        local = compact if small else distributed
        mapped = jax.shard_map(local, mesh=mesh, in_specs=in_specs, out_specs=out_specs, check_vma=False)
        return mapped(
            rhs, legendre, beam, mixing, prior, inv_noise, mask_flags, cycle_len, cycle_slot, m_values
        )

    return whole
```

```python
import math

import jax
import jax.numpy as jnp
from jax import lax
from jax.experimental import pallas as pl
from jax.experimental.pallas import tpu as pltpu
from jax.sharding import PartitionSpec as P

ITERS = 3
LANES = 128
SUBLANES = 8
WIDE = 512
SIDE_ROWS = 32
MOMENTS = 2 * ITERS
POWERS = 2 * ITERS - 1
HIGHEST_PRECISION = lax.Precision.HIGHEST
F32 = jnp.float32
BF16 = jnp.bfloat16


def nt_dot(a, b):
    return lax.dot_general(a, b, (((1,), (1,)), ((), ())), preferred_element_type=F32)


def nn_dot(a, b):
    return jnp.dot(a, b, preferred_element_type=F32)


def iota(shape, dim):
    return lax.broadcasted_iota(jnp.int32, shape, dim)


def halves(x):
    high = x.astype(BF16)
    return high, (x - high.astype(F32)).astype(BF16)


def half_turn_sine(u):
    square = u * u
    total = jnp.full_like(u, -(math.pi**11) / math.factorial(11))
    for power in (9, 7, 5, 3, 1):
        sign = 1.0 if power % 4 == 1 else -1.0
        total = total * square + sign * math.pi**power / math.factorial(power)
    return total * u


def project(rhs_ref, legendre_ref, beam_ref, mixing_ref, prior_ref):
    comp_count, l_count = prior_ref.shape
    channel_count = beam_ref.shape[0]
    band_cycles = legendre_ref.shape[0]
    mixing = mixing_ref[...].astype(BF16)
    groups = l_count // LANES
    moments = [jnp.zeros((comp_count, 2 * LANES), F32) for n in range(MOMENTS)]
    used = POWERS * 2 * channel_count
    images = jnp.zeros((band_cycles, 2 * LANES), F32)
    filler = jnp.zeros((2 * LANES - used, 2 * LANES), F32)
    for pair in range(0, groups, 2):
        parts = []
        for group in (pair, pair + 1):
            lanes = slice(group * LANES, (group + 1) * LANES)
            vector = jnp.concatenate(
                [rhs_ref[pl.ds(k * groups + group, comp_count, stride=2 * groups), :] for k in range(2)], axis=1
            )
            prior = jnp.concatenate([prior_ref[:, lanes]] * 2, axis=1)
            powers = [vector]
            for n in range(1, POWERS):
                powers.append(prior * powers[-1])
            for n in range(MOMENTS):
                moments[n] = moments[n] + powers[n // 2] * powers[n - n // 2]
            mixed = nn_dot(mixing, jnp.concatenate(powers, axis=1).astype(BF16))
            beam = beam_ref[:, lanes]
            parts.append([mixed[:, i * LANES : (i + 1) * LANES] * beam for i in range(2 * POWERS)])
        blended = jnp.concatenate(
            [jnp.concatenate([parts[0][i], parts[1][i]], axis=1) for i in range(2 * POWERS)] + [filler], axis=0
        )
        images = images + nt_dot(
            legendre_ref[:, pair * LANES : (pair + 2) * LANES], blended.astype(BF16)
        )
    return images, moments


def gather_kernel(
    rhs_in, legendre_in, beam_in, mixing_in, prior_in, noise_in, mask_in, len_in, slot_in, m_in,
    out_ref, side_ref,
    rhs_ref, legendre_ref, beam_ref, mixing_ref, prior_ref, noise_ref, mask_ref, len_ref, slot_ref, m_ref,
    gram_ref, sems,
):
    sources = (slot_in, len_in, m_in, mask_in, mixing_in, prior_in, rhs_in, beam_in, legendre_in, noise_in)
    targets = (slot_ref, len_ref, m_ref, mask_ref, mixing_ref, prior_ref, rhs_ref, beam_ref, legendre_ref, noise_ref)
    copies = [pltpu.make_async_copy(a, b, sems.at[i]) for i, (a, b) in enumerate(zip(sources, targets))]
    for copy in copies:
        copy.start()
    channel_width, cycle_count, pixel_count = noise_ref.shape
    comp_count, l_count = prior_ref.shape
    m_count = m_ref.shape[0]
    band_cycles = legendre_ref.shape[0]
    rows = 2 * m_count
    owner = lax.axis_index("blk")
    band = lax.axis_index("lat")
    bands = lax.axis_size("lat")

    for copy in copies[:-1]:
        copy.wait()
    images, moments = project(rhs_ref, legendre_ref, beam_ref, mixing_ref, prior_ref)
    copies[-1].wait()

    row_ids = iota((rows, 1), 0)
    m_column = jnp.zeros((rows, 1), F32)
    for i in range(m_count):
        m_column = jnp.where(row_ids % m_count == i, m_ref[i].astype(F32), m_column)
    quarter = jnp.where(row_ids < m_count, 0.0, 0.25).astype(F32)
    chunk = min(WIDE, pixel_count)
    lengths = [len_ref[slot_ref[owner * cycle_count + q]] for q in range(cycle_count)]
    doubles = [jnp.full((rows, 1), (2 * n).astype(F32), F32) for n in lengths]
    inverses = [1.0 / double for double in doubles]
    sums = [jnp.zeros((rows, LANES), F32) for q in range(cycle_count)]
    padding = jnp.zeros((LANES - channel_width * rows, chunk), F32)
    for start in range(0, pixel_count, chunk):
        pixels = iota((rows, chunk), 1) + start
        phases = m_column * (2 * pixels + 1).astype(F32)
        for q in range(cycle_count):
            rest = phases - jnp.floor(phases * inverses[q] + 0.5) * doubles[q]
            turns = rest * inverses[q] + quarter
            turns = turns - jnp.floor(turns + 0.5)
            sine = half_turn_sine(turns)
            table = jnp.where(pixels < lengths[q], 1.0 - 2.0 * sine * sine, 0.0).astype(BF16)
            wide = table.astype(F32)
            weighted = [noise_ref[f, q : q + 1, start : start + chunk] * wide for f in range(channel_width)]
            weighted = jnp.concatenate(weighted + [padding], axis=0).astype(BF16)
            sums[q] = sums[q] + nt_dot(table, weighted)
    spread = jnp.where(iota((channel_width, LANES), 1) // rows == iota((channel_width, LANES), 0), 1.0, 0.0)
    flags = nn_dot(mask_ref[...].astype(F32).astype(BF16), spread.astype(BF16))
    for q in range(cycle_count):
        gram = sums[q] * flags[q : q + 1]
        gram_ref[q * m_count : (q + 1) * m_count, :LANES] = gram[:m_count]
        gram_ref[q * m_count : (q + 1) * m_count, LANES:] = gram[m_count:]

    count = cycle_count * m_count
    message_rows = iota((count, LANES), 0)
    lanes = iota((count, LANES), 1)
    slots = jnp.zeros((count, LANES), jnp.int32)
    for q in range(cycle_count):
        slots = jnp.where(message_rows // m_count == q, slot_ref[owner * cycle_count + q], slots)
    wanted = (message_rows % m_count * bands + band) * band_cycles + slots
    held = (owner * bands + band) * band_cycles + message_rows
    first = gram_ref[:, :LANES]
    base = channel_width * rows
    first = jnp.where(lanes == base, wanted.astype(F32), first)
    first = jnp.where(lanes == base + 1, held.astype(F32), first)
    totals = jnp.zeros((count, LANES), F32)
    for n in range(MOMENTS):
        total = jnp.sum(jnp.sum(moments[n], axis=0, keepdims=True), axis=1, keepdims=True)
        totals = jnp.where(message_rows == n, total, totals)
    for piece in range(3):
        part = totals.astype(BF16).astype(F32)
        first = jnp.where(lanes == base + 2 + piece, part, first)
        totals = totals - part
    out_ref[:count, :LANES] = first.astype(BF16)
    out_ref[:count, LANES : 2 * LANES] = gram_ref[:, LANES:].astype(BF16)
    out_ref[:count, 2 * LANES :] = images.astype(BF16)
    for piece in range(l_count // WIDE):
        out_ref[count * (piece + 1) : count * (piece + 2), :] = legendre_ref[:, piece * WIDE : (piece + 1) * WIDE]
    half = l_count // 2
    spare = side_ref.shape[0] // (half // WIDE) - comp_count
    for piece in range(half // WIDE):
        lanes = pl.ds(pl.multiple_of(band * half + piece * WIDE, WIDE), WIDE)
        block = [prior_ref[:, lanes]]
        strips = []
        for i in range(WIDE // LANES):
            begin = i * spare
            if piece == 0 and begin < mixing_ref.shape[0]:
                strip = jnp.concatenate(
                    [mixing_ref[begin : begin + spare, :], jnp.zeros((spare, LANES - comp_count), F32)], axis=1
                )
            else:
                strip = jnp.zeros((spare, LANES), F32)
            strips.append(strip)
        block.append(jnp.concatenate(strips, axis=1))
        side_ref[piece * (comp_count + spare) : (piece + 1) * (comp_count + spare), :] = jnp.concatenate(
            block, axis=0
        ).astype(BF16)


def iterate_kernel(
    near_ref, far_ref, rhs_ref, beam_ref, own_mixing_ref, own_prior_ref,
    solution_ref, residual_ref, legendre_ref, doubled_ref, other_prior_ref, channel_width, m_count, block_count,
    side_rows,
):
    comp_count, l_count = own_prior_ref.shape
    channel_count = beam_ref.shape[0]
    rows = 2 * m_count
    pieces = l_count // WIDE
    count = (near_ref.shape[0] - side_rows) // (block_count * (2 + pieces))
    stride = count * (1 + pieces)
    cycles = 2 * block_count * count
    small = channel_count * rows
    base = channel_width * rows
    owner = lax.axis_index("blk")
    comp = lax.axis_index("comp")
    band = lax.axis_index("lat")

    half = l_count // 2
    step = side_rows // (half // WIDE)
    side_begin = near_ref.shape[0] - side_rows
    for ref, place in ((near_ref, band), (far_ref, 1 - band)):
        for piece in range(half // WIDE):
            lanes = pl.ds(pl.multiple_of(place * half + piece * WIDE, WIDE), WIDE)
            block = ref[side_begin + piece * step : side_begin + (piece + 1) * step, :].astype(F32)
            other_prior_ref[:, lanes] = block[:comp_count]
    block = near_ref[side_begin : side_begin + step, :].astype(F32)[comp_count:]
    strips = [block[:, i * LANES : i * LANES + comp_count] for i in range(channel_count // (step - comp_count))]
    other_mixing = jnp.concatenate(strips, axis=0).astype(BF16)

    own_rows, other_rows = [], []
    for ref in (near_ref, far_ref):
        for i in range(block_count):
            own_rows.append(ref[i * stride : i * stride + count, :])
        for i in range(block_count):
            begin = block_count * stride + i * count
            other_rows.append(ref[begin : begin + count, :])
    own_rows = jnp.concatenate(own_rows, axis=0).astype(F32)
    other_rows = jnp.concatenate(other_rows, axis=0).astype(F32)

    pieces_sum = own_rows[:, :LANES] + other_rows[:, :LANES]
    scalars = []
    for n in range(MOMENTS):
        total = jnp.zeros((1, LANES), F32)
        for i in range(block_count):
            total = total + pieces_sum[i * count + n : i * count + n + 1, :]
        lane = iota((1, LANES), 1)
        keep = (lane >= base + 2) & (lane < base + 5)
        scalars.append(jnp.sum(jnp.where(keep, total, 0.0), axis=1, keepdims=True))

    wanted = own_rows[:, base : base + 1]
    held = jnp.transpose(jnp.broadcast_to(own_rows[:, base + 1 : base + 2], (cycles, cycles)))
    pick = jnp.where(wanted == held, 1.0, 0.0).astype(BF16)
    for piece in range(pieces):
        blocks = []
        for ref in (near_ref, far_ref):
            for i in range(block_count):
                begin = i * stride + count * (piece + 1)
                blocks.append(ref[begin : begin + count, :])
        legendre_ref[:, piece * WIDE : (piece + 1) * WIDE] = nn_dot(pick, jnp.concatenate(blocks, axis=0)).astype(BF16)

    row = iota((small, cycles), 0)
    lane = iota((small, cycles), 1)
    same_m = row % m_count == lane % m_count
    summed = jnp.transpose((own_rows + other_rows)[:, 2 * LANES :])
    high, low = halves(summed)
    images = nt_dot(jnp.concatenate([high, low], axis=1), jnp.concatenate([pick, pick], axis=1))
    width = 2 * channel_count
    images = jnp.concatenate([images[n * width : (n + 1) * width] for n in range(POWERS)], axis=1)
    high, low = halves(images)
    spread_row = iota((small, width), 0)
    spread_lane = iota((small, width), 1)
    spread = (spread_row // rows == spread_lane % channel_count) & (
        spread_row % rows // m_count == spread_lane // channel_count
    )
    spread = jnp.where(spread, 1.0, 0.0).astype(BF16)
    images = nn_dot(spread, high) + nn_dot(spread, low)
    y = [jnp.where(same_m, images[:, n * cycles : (n + 1) * cycles], 0.0) for n in range(POWERS)]

    own_gram = jnp.transpose(own_rows[:, : 2 * LANES])
    other_gram = jnp.transpose(other_rows[:, : 2 * LANES])
    first_gram = jnp.where(comp == 0, own_gram, other_gram)
    second_gram = jnp.where(comp == 0, other_gram, own_gram)
    grams = []
    for k in range(2):
        gram = jnp.concatenate(
            [first_gram[k * LANES : k * LANES + base], second_gram[k * LANES : k * LANES + base]], axis=0
        )
        grams.append(gram.reshape(channel_count, rows, cycles))
    group = jnp.where(
        iota((2 * cycles, cycles), 0) % cycles // m_count == iota((2 * cycles, cycles), 1) // m_count, 1.0, 0.0
    ).astype(BF16)

    def sky(image):
        image = image.reshape(channel_count, rows, cycles)
        cosine = jnp.sum(image[:, :m_count], axis=1, keepdims=True)
        sine = jnp.sum(image[:, m_count:], axis=1, keepdims=True)
        product = (grams[0] * cosine + grams[1] * sine).reshape(small, cycles)
        high, low = halves(product)
        result = nn_dot(jnp.concatenate([high, low], axis=1), group)
        return jnp.where(same_m, result, 0.0)

    expand = jnp.where(iota((small, channel_count), 0) // rows == iota((small, channel_count), 1), 1.0, 0.0)
    expand = expand.astype(BF16)
    same_row = iota((small, small), 0) % rows == iota((small, small), 1) % rows

    def spread_matrix(matrix):
        tall = nn_dot(expand, matrix).astype(BF16)
        return jnp.where(same_row, nt_dot(tall, expand), 0.0).astype(BF16)

    def spread_transpose(matrix):
        tall = nt_dot(expand, matrix).astype(BF16)
        return jnp.where(same_row, nt_dot(tall, expand), 0.0).astype(BF16)

    own_mixing = own_mixing_ref[...].astype(BF16)
    both = (nt_dot(own_mixing, own_mixing) + nt_dot(other_mixing, other_mixing)).astype(BF16)
    square_matrix = spread_matrix(both)
    forward = [spread_matrix(own_mixing), spread_matrix(other_mixing)]
    backward = [spread_transpose(own_mixing), spread_transpose(other_mixing)]
    priors = (own_prior_ref, other_prior_ref)

    def dot(a, b):
        return jnp.sum(jnp.sum(a * b, axis=0, keepdims=True), axis=1, keepdims=True)

    chunk = 2 * LANES
    starts = range(0, l_count, chunk)

    def harmonic(z, start):
        table = legendre_ref[:, start : start + chunk]
        beam = beam_ref[:, start : start + chunk][:, None, :]
        value = nn_dot(z, table).reshape(channel_count, rows, chunk) * beam
        return table, beam, value.reshape(small, chunk).astype(BF16)

    def analyse(value, table, beam):
        value = value.reshape(channel_count, rows, chunk) * beam
        return nt_dot(value.reshape(small, chunk).astype(BF16), table)

    def first_pass(z):
        z = z.astype(BF16)
        plain = jnp.zeros((small, cycles), F32)
        primed = jnp.zeros((small, cycles), F32)
        second = jnp.zeros((rows, chunk), F32)
        third = jnp.zeros((rows, chunk), F32)
        for start in starts:
            table, beam, value = harmonic(z, start)
            plain = plain + analyse(nn_dot(square_matrix, value), table, beam)
            mixed = jnp.zeros((small, chunk), F32)
            for side in range(2):
                prior = priors[side][:, start : start + chunk][:, None, :]
                once = nn_dot(backward[side], value).reshape(comp_count, rows, chunk) * prior
                twice = once * prior
                second = second + jnp.sum(once * once, axis=0)
                third = third + jnp.sum(once * twice, axis=0)
                mixed = mixed + nn_dot(forward[side], once.reshape(small, chunk).astype(BF16))
                doubled_ref[side, :, start : start + chunk] = twice.reshape(small, chunk).astype(BF16)
            primed = primed + analyse(mixed, table, beam)
        return (
            jnp.where(same_m, plain, 0.0),
            jnp.where(same_m, primed, 0.0),
            jnp.sum(jnp.sum(second, axis=0, keepdims=True), axis=1, keepdims=True),
            jnp.sum(jnp.sum(third, axis=0, keepdims=True), axis=1, keepdims=True),
        )

    def second_pass(z):
        z = z.astype(BF16)
        plain = jnp.zeros((small, cycles), F32)
        cross = jnp.zeros((rows, chunk), F32)
        own = jnp.zeros((rows, chunk), F32)
        for start in starts:
            table, beam, value = harmonic(z, start)
            plain = plain + analyse(nn_dot(square_matrix, value), table, beam)
            for side in range(2):
                prior = priors[side][:, start : start + chunk][:, None, :]
                vector = nn_dot(backward[side], value).reshape(comp_count, rows, chunk)
                twice = doubled_ref[side, :, start : start + chunk].astype(F32).reshape(comp_count, rows, chunk)
                cross = cross + jnp.sum(vector * twice, axis=0)
                own = own + jnp.sum(vector * vector * prior, axis=0)
        return (
            jnp.where(same_m, plain, 0.0),
            jnp.sum(jnp.sum(cross, axis=0, keepdims=True), axis=1, keepdims=True),
            jnp.sum(jnp.sum(own, axis=0, keepdims=True), axis=1, keepdims=True),
        )

    s = scalars
    z0 = sky(y[0])
    y_plain0, y_prime0, pp00, ppp00 = first_pass(z0)
    norm0 = s[0]
    step0 = norm0 / (s[1] + dot(y[0], z0))
    p00, uu00 = dot(z0, y_prime0), dot(z0, y_plain0)
    by0, by1, by2, by3, by4 = [dot(y[n], z0) for n in range(5)]
    norm1 = s[0] - 2.0 * step0 * (s[1] + by0) + step0 * step0 * (s[2] + 2.0 * by1 + uu00)
    ratio0 = norm1 / norm0
    y_r1 = y[0] - step0 * (y[1] + y_plain0)
    y_d1 = y_r1 + ratio0 * y[0]
    e0, e1, e2 = 1.0 + ratio0, -step0, -step0
    z1 = sky(y_d1)
    y_plain1, p2_01, p_11 = second_pass(z1)
    quadratic1 = (
        e0 * e0 * s[1] + 2.0 * e0 * e1 * s[2] + e1 * e1 * s[3]
        + 2.0 * e0 * e2 * by1 + 2.0 * e1 * e2 * by2 + e2 * e2 * p00
    )
    step1 = norm1 / (quadratic1 + dot(y_d1, z1))
    y_pd1 = e0 * y[1] + e1 * y[2] + e2 * y_prime0
    h0, h1, h2 = 1.0 + 0.0 * step1, -step0 - step1 * e0, -step1 * e1
    h3, h4, h5 = -step0, -step1 * e2, -step1
    b1y = [dot(y[n], z1) for n in range(4)]
    uu01, p01, uu11 = dot(z1, y_plain0), dot(z1, y_prime0), dot(z1, y_plain1)
    norm2 = (
        h0 * h0 * s[0] + 2.0 * h0 * h1 * s[1] + (h1 * h1 + 2.0 * h0 * h2) * s[2]
        + 2.0 * h1 * h2 * s[3] + h2 * h2 * s[4]
        + 2.0 * h3 * (h0 * by0 + h1 * by1 + h2 * by2)
        + 2.0 * h4 * (h0 * by1 + h1 * by2 + h2 * by3)
        + 2.0 * h5 * (h0 * b1y[0] + h1 * b1y[1] + h2 * b1y[2])
        + h3 * h3 * uu00 + 2.0 * h3 * h4 * p00 + h4 * h4 * pp00
        + 2.0 * h3 * h5 * uu01 + 2.0 * h4 * h5 * p01 + h5 * h5 * uu11
    )
    ratio1 = norm2 / norm1
    y_d2 = y_r1 - step1 * (y_pd1 + y_plain1) + ratio1 * y_d1
    z2 = sky(y_d2)
    h0, h1, h3 = h0 + ratio1 * e0, h1 + ratio1 * e1, h3 + ratio1 * e2
    quadratic2 = (
        h0 * h0 * s[1] + 2.0 * h0 * h1 * s[2] + (h1 * h1 + 2.0 * h0 * h2) * s[3]
        + 2.0 * h1 * h2 * s[4] + h2 * h2 * s[5]
        + 2.0 * h3 * (h0 * by1 + h1 * by2 + h2 * by3)
        + 2.0 * h4 * (h0 * by2 + h1 * by3 + h2 * by4)
        + 2.0 * h5 * (h0 * b1y[1] + h1 * b1y[2] + h2 * b1y[3])
        + h3 * h3 * p00 + 2.0 * h3 * h4 * pp00 + h4 * h4 * ppp00
        + 2.0 * h3 * h5 * p01 + 2.0 * h4 * h5 * p2_01 + h5 * h5 * p_11
    )
    step2 = norm2 / (quadratic2 + dot(y_d2, z2))

    mine_row = iota((width, small), 0)
    mine_lane = iota((width, small), 1)
    mine = (mine_lane // rows == mine_row % channel_count) & (
        mine_lane % rows == mine_row // channel_count * m_count + owner
    )
    mine = jnp.where(mine, 1.0, 0.0).astype(BF16)
    stacked = jnp.concatenate([z.astype(BF16) for z in (z0, z1, z2)], axis=1)
    stacked = nn_dot(mine, stacked).astype(BF16)
    stacked = jnp.concatenate([stacked[:, i * cycles : (i + 1) * cycles] for i in range(ITERS)], axis=0)
    groups = l_count // LANES
    for start in starts:
        table = legendre_ref[:, start : start + chunk]
        beam = beam_ref[:, start : start + chunk]
        value = nn_dot(stacked, table)
        value = [value[i * channel_count : (i + 1) * channel_count] * beam for i in range(2 * ITERS)]
        value = jnp.concatenate(value, axis=1).astype(BF16)
        vectors = lax.dot_general(own_mixing, value, (((0,), (0,)), ((), ())), preferred_element_type=F32)
        for part in range(chunk // LANES):
            prior = own_prior_ref[:, start + part * LANES : start + (part + 1) * LANES]
            for k in range(2):
                place = pl.ds(k * groups + start // LANES + part, comp_count, stride=2 * groups)
                u = []
                for i in range(ITERS):
                    begin = (2 * i + k) * chunk + part * LANES
                    u.append(vectors[:, begin : begin + LANES])
                b = rhs_ref[place, :]
                r1 = b - step0 * (prior * b + u[0])
                d1 = r1 + ratio0 * b
                r2 = r1 - step1 * (prior * d1 + u[1])
                d2 = r2 + ratio1 * d1
                solution_ref[place, :] = step0 * b + step1 * d1 + step2 * d2
                residual_ref[place, :] = r2 - step2 * (prior * d2 + u[2])


def swap(x, axis):
    return lax.ppermute(x, axis, [(0, 1), (1, 0)])


def compact(
    rhs, legendre, beam, mixing, prior, inv_noise, mask_flags, cycle_len, cycle_slot, m_values
):
    comp_count, parts, m_own, l_count = rhs.shape
    block_count = lax.axis_size("blk")
    m_count = m_values.shape[0]
    channel_width, cycle_count = mask_flags.shape
    channel_count = beam.shape[0]
    count = cycle_count * m_count
    vmem = pl.BlockSpec(memory_space=pltpu.VMEM)
    flat = rhs.reshape(comp_count * parts * l_count // LANES, LANES)
    half = l_count // 2
    side_rows = half // WIDE * SIDE_ROWS
    hbm = pl.BlockSpec(memory_space=pltpu.HBM)
    operands = (
        flat, jnp.transpose(legendre[0]), beam, mixing, prior, inv_noise, jnp.transpose(mask_flags),
        cycle_len, cycle_slot, m_values,
    )
    spaces = [pltpu.VMEM] * 7 + [pltpu.SMEM] * 3
    message, side = pl.pallas_call(
        gather_kernel,
        out_shape=[
            jax.ShapeDtypeStruct((count * (1 + l_count // WIDE), WIDE), BF16),
            jax.ShapeDtypeStruct((side_rows, WIDE), BF16),
        ],
        in_specs=[hbm] * len(operands),
        out_specs=[vmem] * 2,
        scratch_shapes=[space(x.shape, x.dtype) for space, x in zip(spaces, operands)]
        + [pltpu.VMEM((count, 2 * LANES), F32), pltpu.SemaphoreType.DMA((len(operands),))],
        compiler_params=pltpu.CompilerParams(vmem_limit_bytes=63 * 1024 * 1024),
        name="gather_kernel",
    )(*operands)
    blocks = [message]
    for shift in range(1, block_count):
        blocks.append(lax.ppermute(message, "blk", [(i, (i + shift) % block_count) for i in range(block_count)]))
    crossing = swap(jnp.concatenate([block[:count] for block in blocks] + [side], axis=0), "comp")
    near = jnp.concatenate(blocks + [crossing], axis=0)
    far = swap(near, "lat")

    def kernel(*refs):
        iterate_kernel(*refs, channel_width, m_count, block_count, side_rows)

    small = channel_count * 2 * m_count
    cycles = 2 * block_count * count
    answers = pl.pallas_call(
        kernel,
        out_shape=[jax.ShapeDtypeStruct(flat.shape, F32)] * 2,
        in_specs=[vmem] * 6,
        out_specs=[vmem] * 2,
        scratch_shapes=[
            pltpu.VMEM((cycles, l_count), BF16),
            pltpu.VMEM((2, small, l_count), BF16),
            pltpu.VMEM(prior.shape, F32),
        ],
        compiler_params=pltpu.CompilerParams(vmem_limit_bytes=48 * 1024 * 1024),
        name="iterate_kernel",
    )(near, far, flat, beam, mixing, prior)
    return tuple(answer.reshape(rhs.shape) for answer in answers)


def cycle_table(m_values, length, pixel_count):
    pixels = jnp.arange(pixel_count, dtype=jnp.int32)
    phase_ids = m_values[:, None] * (2 * pixels[None, :] + 1) % (2 * length)
    angles = math.pi * phase_ids.astype(jnp.float32) / length.astype(jnp.float32)
    inside = (pixels < length)[None, :]
    cosine = jnp.where(inside, jnp.cos(angles), jnp.float32(0.0))
    sine_part = jnp.where(inside, -jnp.sin(angles), jnp.float32(0.0))
    return jnp.stack([cosine, sine_part]).astype(jnp.bfloat16)


def distributed(
    rhs, legendre, beam, mixing, prior, inv_noise, mask_flags, cycle_len, cycle_slot, m_values
):
    cycle_count = inv_noise.shape[1]
    pixel_count = inv_noise.shape[2]
    channel_width = inv_noise.shape[0]
    owner_index = lax.axis_index("blk")
    comp_index = lax.axis_index("comp")
    local_ids = lax.dynamic_slice_in_dim(cycle_slot, owner_index * cycle_count, cycle_count)
    local_lengths = cycle_len[local_ids]
    legendre_slot = legendre[:, :, cycle_slot]
    weights = mask_flags.astype(jnp.float32)
    own_beam = lax.dynamic_slice_in_dim(beam, comp_index * channel_width, channel_width, 0)
    stored = jax.vmap(cycle_table, in_axes=(None, 0, None))(m_values, local_lengths, pixel_count)
    solution = jnp.zeros_like(rhs)
    residual = rhs
    direction = rhs
    for iteration in range(ITERS):
        local_mix = jnp.einsum("fc,ckml->fkml", mixing, direction, precision=HIGHEST_PRECISION)
        summed = lax.psum(local_mix.astype(jnp.bfloat16), "comp").astype(jnp.float32)
        own_part = lax.dynamic_slice_in_dim(summed, comp_index * channel_width, channel_width, 0)
        blended = (own_part * own_beam[:, None, None, :]).astype(jnp.bfloat16)
        coeffs = jnp.einsum(
            "fkml,mlr->fkmr", blended, legendre_slot, preferred_element_type=jnp.float32
        ).astype(jnp.bfloat16)
        arrived = lax.all_to_all(coeffs, "blk", split_axis=3, concat_axis=2, tiled=True)
        sky_map = jnp.einsum("fkmq,qkmp->fqp", arrived, stored, preferred_element_type=jnp.float32)
        weighted = (weights[:, :, None] * inv_noise * sky_map).astype(jnp.bfloat16)
        projected = jnp.einsum(
            "fqp,qkmp->fkmq", weighted, stored, preferred_element_type=jnp.float32
        ).astype(jnp.bfloat16)
        returned = lax.all_to_all(projected, "blk", split_axis=2, concat_axis=3, tiled=True)
        harmonic = jnp.einsum(
            "fkms,mls->fkml", returned, legendre_slot, preferred_element_type=jnp.float32
        )
        everyone = lax.all_gather(
            harmonic.astype(jnp.bfloat16), ("comp", "lat"), axis=0, tiled=True
        ).astype(harmonic.dtype)
        stacked = everyone.reshape(
            (lax.axis_size("comp"), lax.axis_size("lat"), channel_width) + harmonic.shape[1:]
        )
        summed_bands = jnp.sum(stacked, axis=1).reshape((-1,) + harmonic.shape[1:])
        backward = jnp.einsum(
            "fc,fkml->ckml",
            mixing,
            summed_bands * beam[:, None, None, :],
            precision=HIGHEST_PRECISION,
        )
        applied = prior[:, None, None, :] * direction + backward
        totals = lax.psum(
            (
                jnp.sum(direction * applied),
                jnp.sum(residual * applied),
                jnp.sum(applied * applied),
                jnp.sum(residual * residual),
            ),
            ("blk", "comp"),
        )
        curvature, cross_term, square, norm_now = totals
        step_size = norm_now / curvature
        solution = solution + step_size * direction
        residual = residual - step_size * applied
        norm_next = norm_now - 2.0 * step_size * cross_term + step_size * step_size * square
        direction = residual + norm_next / norm_now * direction
    return (solution, residual)


def fits(mesh, rhs, legendre, beam, mixing, inv_noise, m_values):
    sizes = dict(mesh.shape)
    m_count = m_values.shape[0]
    cycles = legendre.shape[2]
    slots = cycles // (sizes["blk"] * sizes["lat"])
    channels = beam.shape[0]
    width = channels // sizes["comp"]
    comps = mixing.shape[1] // sizes["comp"]
    l_count = legendre.shape[1]
    return (
        sizes["comp"] == 2
        and sizes["lat"] == 2
        and m_count == sizes["blk"]
        and 2 * m_count == SUBLANES
        and cycles * m_count == LANES
        and slots * m_count == cycles // sizes["lat"] == 16
        and comps == channels
        and SIDE_ROWS - comps >= SUBLANES
        and (SIDE_ROWS - comps) * (WIDE // LANES) >= channels
        and channels % (SIDE_ROWS - comps) == 0
        and l_count % (2 * WIDE) == 0
        and channels % SUBLANES == 0
        and width * SUBLANES + 5 <= LANES
        and 2 * POWERS * channels <= 2 * LANES
        and l_count % WIDE == 0
        and inv_noise.shape[2] % WIDE == 0
        and rhs.shape[1] == 2
        and MOMENTS <= 16
    )


def solution(mesh):
    in_specs = (
        P(("groups", "comp"), None, "blk", None),
        P("blk", None, "lat"),
        P(),
        P(None, "comp"),
        P("comp", None),
        P("comp", ("blk", "lat"), None),
        P("comp", ("blk", "lat")),
        P("lat"),
        P("lat"),
        P(),
    )
    out_specs = (P(("groups", "comp"), None, "blk", None), P(("groups", "comp"), None, "blk", None))

    def whole(rhs, legendre, beam, mixing, prior, inv_noise, mask_flags, cycle_len, cycle_slot, m_values):
        small = fits(mesh, rhs, legendre, beam, mixing, inv_noise, m_values)
        local = compact if small else distributed
        mapped = jax.shard_map(local, mesh=mesh, in_specs=in_specs, out_specs=out_specs, check_vma=False)
        return mapped(
            rhs, legendre, beam, mixing, prior, inv_noise, mask_flags, cycle_len, cycle_slot, m_values
        )

    return whole
```

```python
import math

import jax
import jax.numpy as jnp
from jax import lax
from jax.experimental import pallas as pl
from jax.experimental.pallas import tpu as pltpu
from jax.sharding import PartitionSpec as P

ITERS = 3
LANES = 128
SUBLANES = 8
WIDE = 512
SIDE_ROWS = 32
MOMENTS = 2 * ITERS
POWERS = 2 * ITERS - 1
HIGHEST_PRECISION = lax.Precision.HIGHEST
F32 = jnp.float32
BF16 = jnp.bfloat16


def nt_dot(a, b):
    return lax.dot_general(a, b, (((1,), (1,)), ((), ())), preferred_element_type=F32)


def nn_dot(a, b):
    return jnp.dot(a, b, preferred_element_type=F32)


def iota(shape, dim):
    return lax.broadcasted_iota(jnp.int32, shape, dim)


def halves(x):
    high = x.astype(BF16)
    return high, (x - high.astype(F32)).astype(BF16)


def half_turn_sine(u):
    square = u * u
    total = jnp.full_like(u, -(math.pi**11) / math.factorial(11))
    for power in (9, 7, 5, 3, 1):
        sign = 1.0 if power % 4 == 1 else -1.0
        total = total * square + sign * math.pi**power / math.factorial(power)
    return total * u


def project(rhs_ref, legendre_ref, beam_ref, mixing_ref, prior_ref):
    comp_count, l_count = prior_ref.shape
    channel_count = beam_ref.shape[0]
    band_cycles = legendre_ref.shape[0]
    mixing = mixing_ref[...].astype(BF16)
    groups = l_count // LANES
    moments = [jnp.zeros((comp_count, 2 * LANES), F32) for n in range(MOMENTS)]
    used = POWERS * 2 * channel_count
    images = jnp.zeros((band_cycles, 2 * LANES), F32)
    filler = jnp.zeros((2 * LANES - used, 2 * LANES), F32)
    for pair in range(0, groups, 2):
        parts = []
        for group in (pair, pair + 1):
            lanes = slice(group * LANES, (group + 1) * LANES)
            vector = jnp.concatenate(
                [rhs_ref[pl.ds(k * groups + group, comp_count, stride=2 * groups), :] for k in range(2)], axis=1
            )
            prior = jnp.concatenate([prior_ref[:, lanes]] * 2, axis=1)
            powers = [vector]
            for n in range(1, POWERS):
                powers.append(prior * powers[-1])
            for n in range(MOMENTS):
                moments[n] = moments[n] + powers[n // 2] * powers[n - n // 2]
            mixed = nn_dot(mixing, jnp.concatenate(powers, axis=1).astype(BF16))
            beam = beam_ref[:, lanes]
            parts.append([mixed[:, i * LANES : (i + 1) * LANES] * beam for i in range(2 * POWERS)])
        blended = jnp.concatenate(
            [jnp.concatenate([parts[0][i], parts[1][i]], axis=1) for i in range(2 * POWERS)] + [filler], axis=0
        )
        images = images + nt_dot(
            legendre_ref[:, pair * LANES : (pair + 2) * LANES], blended.astype(BF16)
        )
    return images, moments


def gather_kernel(
    rhs_in, legendre_in, beam_in, mixing_in, prior_in, noise_in, mask_in, len_in, slot_in, m_in,
    out_ref, side_ref,
    rhs_ref, legendre_ref, beam_ref, mixing_ref, prior_ref, noise_ref, mask_ref, len_ref, slot_ref, m_ref,
    gram_ref, sems,
):
    sources = (slot_in, len_in, m_in, mask_in, mixing_in, prior_in, rhs_in, beam_in, legendre_in, noise_in)
    targets = (slot_ref, len_ref, m_ref, mask_ref, mixing_ref, prior_ref, rhs_ref, beam_ref, legendre_ref, noise_ref)
    copies = [pltpu.make_async_copy(a, b, sems.at[i]) for i, (a, b) in enumerate(zip(sources, targets))]
    for copy in copies:
        copy.start()
    channel_width, cycle_count, pixel_count = noise_ref.shape
    comp_count, l_count = prior_ref.shape
    m_count = m_ref.shape[0]
    band_cycles = legendre_ref.shape[0]
    rows = 2 * m_count
    owner = lax.axis_index("blk")
    band = lax.axis_index("lat")
    bands = lax.axis_size("lat")

    for copy in copies[:-1]:
        copy.wait()
    images, moments = project(rhs_ref, legendre_ref, beam_ref, mixing_ref, prior_ref)
    copies[-1].wait()

    row_ids = iota((rows, 1), 0)
    m_column = jnp.zeros((rows, 1), F32)
    for i in range(m_count):
        m_column = jnp.where(row_ids % m_count == i, m_ref[i].astype(F32), m_column)
    quarter = jnp.where(row_ids < m_count, 0.0, 0.25).astype(F32)
    chunk = min(WIDE, pixel_count)
    lengths = [len_ref[slot_ref[owner * cycle_count + q]] for q in range(cycle_count)]
    doubles = [jnp.full((rows, 1), (2 * n).astype(F32), F32) for n in lengths]
    inverses = [1.0 / double for double in doubles]
    sums = [jnp.zeros((rows, LANES), F32) for q in range(cycle_count)]
    padding = jnp.zeros((LANES - channel_width * rows, chunk), F32)
    for start in range(0, pixel_count, chunk):
        pixels = iota((rows, chunk), 1) + start
        phases = m_column * (2 * pixels + 1).astype(F32)
        for q in range(cycle_count):
            rest = phases - jnp.floor(phases * inverses[q] + 0.5) * doubles[q]
            turns = rest * inverses[q] + quarter
            turns = turns - jnp.floor(turns + 0.5)
            sine = half_turn_sine(turns)
            table = jnp.where(pixels < lengths[q], 1.0 - 2.0 * sine * sine, 0.0).astype(BF16)
            wide = table.astype(F32)
            weighted = [noise_ref[f, q : q + 1, start : start + chunk] * wide for f in range(channel_width)]
            weighted = jnp.concatenate(weighted + [padding], axis=0).astype(BF16)
            sums[q] = sums[q] + nt_dot(table, weighted)
    spread = jnp.where(iota((channel_width, LANES), 1) // rows == iota((channel_width, LANES), 0), 1.0, 0.0)
    flags = nn_dot(mask_ref[...].astype(F32).astype(BF16), spread.astype(BF16))
    for q in range(cycle_count):
        gram = sums[q] * flags[q : q + 1]
        gram_ref[q * m_count : (q + 1) * m_count, :LANES] = gram[:m_count]
        gram_ref[q * m_count : (q + 1) * m_count, LANES:] = gram[m_count:]

    count = cycle_count * m_count
    message_rows = iota((count, LANES), 0)
    lanes = iota((count, LANES), 1)
    slots = jnp.zeros((count, LANES), jnp.int32)
    for q in range(cycle_count):
        slots = jnp.where(message_rows // m_count == q, slot_ref[owner * cycle_count + q], slots)
    wanted = (message_rows % m_count * bands + band) * band_cycles + slots
    held = (owner * bands + band) * band_cycles + message_rows
    first = gram_ref[:, :LANES]
    base = channel_width * rows
    first = jnp.where(lanes == base, wanted.astype(F32), first)
    first = jnp.where(lanes == base + 1, held.astype(F32), first)
    totals = jnp.zeros((count, LANES), F32)
    for n in range(MOMENTS):
        total = jnp.sum(jnp.sum(moments[n], axis=0, keepdims=True), axis=1, keepdims=True)
        totals = jnp.where(message_rows == n, total, totals)
    for piece in range(3):
        part = totals.astype(BF16).astype(F32)
        first = jnp.where(lanes == base + 2 + piece, part, first)
        totals = totals - part
    out_ref[:, :LANES] = first.astype(BF16)
    out_ref[:, LANES : 2 * LANES] = gram_ref[:, LANES:].astype(BF16)
    out_ref[:, 2 * LANES :] = images.astype(BF16)
    half = l_count // 2
    spare = side_ref.shape[0] // (half // WIDE) - comp_count
    for piece in range(half // WIDE):
        lanes = pl.ds(pl.multiple_of(band * half + piece * WIDE, WIDE), WIDE)
        block = [prior_ref[:, lanes]]
        strips = []
        for i in range(WIDE // LANES):
            begin = i * spare
            if piece == 0 and begin < mixing_ref.shape[0]:
                strip = jnp.concatenate(
                    [mixing_ref[begin : begin + spare, :], jnp.zeros((spare, LANES - comp_count), F32)], axis=1
                )
            else:
                strip = jnp.zeros((spare, LANES), F32)
            strips.append(strip)
        block.append(jnp.concatenate(strips, axis=1))
        side_ref[piece * (comp_count + spare) : (piece + 1) * (comp_count + spare), :] = jnp.concatenate(
            block, axis=0
        ).astype(BF16)


def iterate_kernel(
    near_ref, far_ref, near_legendre_ref, far_legendre_ref, rhs_ref, beam_ref, own_mixing_ref, own_prior_ref,
    solution_ref, residual_ref, legendre_ref, doubled_ref, other_prior_ref, channel_width, m_count, block_count,
    side_rows,
):
    comp_count, l_count = own_prior_ref.shape
    channel_count = beam_ref.shape[0]
    rows = 2 * m_count
    count = (near_ref.shape[0] - side_rows) // (block_count * 2)
    cycles = 2 * block_count * count
    small = channel_count * rows
    base = channel_width * rows
    owner = lax.axis_index("blk")
    comp = lax.axis_index("comp")
    band = lax.axis_index("lat")

    half = l_count // 2
    step = side_rows // (half // WIDE)
    side_begin = near_ref.shape[0] - side_rows
    for ref, place in ((near_ref, band), (far_ref, 1 - band)):
        for piece in range(half // WIDE):
            lanes = pl.ds(pl.multiple_of(place * half + piece * WIDE, WIDE), WIDE)
            block = ref[side_begin + piece * step : side_begin + (piece + 1) * step, :].astype(F32)
            other_prior_ref[:, lanes] = block[:comp_count]
    block = near_ref[side_begin : side_begin + step, :].astype(F32)[comp_count:]
    strips = [block[:, i * LANES : i * LANES + comp_count] for i in range(channel_count // (step - comp_count))]
    other_mixing = jnp.concatenate(strips, axis=0).astype(BF16)

    span = block_count * count
    own_rows = jnp.concatenate([near_ref[:span, :], far_ref[:span, :]], axis=0).astype(F32)
    other_rows = jnp.concatenate([near_ref[span : 2 * span, :], far_ref[span : 2 * span, :]], axis=0).astype(F32)

    pieces_sum = own_rows[:, :LANES] + other_rows[:, :LANES]
    scalars = []
    for n in range(MOMENTS):
        total = jnp.zeros((1, LANES), F32)
        for i in range(block_count):
            total = total + pieces_sum[i * count + n : i * count + n + 1, :]
        lane = iota((1, LANES), 1)
        keep = (lane >= base + 2) & (lane < base + 5)
        scalars.append(jnp.sum(jnp.where(keep, total, 0.0), axis=1, keepdims=True))

    wanted = own_rows[:, base : base + 1]
    held = jnp.transpose(jnp.broadcast_to(own_rows[:, base + 1 : base + 2], (cycles, cycles)))
    pick = jnp.where(wanted == held, 1.0, 0.0).astype(BF16)
    blocks = jnp.concatenate([near_legendre_ref[...], far_legendre_ref[...]], axis=0)
    legendre_ref[...] = nn_dot(pick, blocks).astype(BF16)

    row = iota((small, cycles), 0)
    lane = iota((small, cycles), 1)
    same_m = row % m_count == lane % m_count
    summed = jnp.transpose((own_rows + other_rows)[:, 2 * LANES :])
    high, low = halves(summed)
    images = nt_dot(jnp.concatenate([high, low], axis=1), jnp.concatenate([pick, pick], axis=1))
    width = 2 * channel_count
    images = jnp.concatenate([images[n * width : (n + 1) * width] for n in range(POWERS)], axis=1)
    high, low = halves(images)
    spread_row = iota((small, width), 0)
    spread_lane = iota((small, width), 1)
    spread = (spread_row // rows == spread_lane % channel_count) & (
        spread_row % rows // m_count == spread_lane // channel_count
    )
    spread = jnp.where(spread, 1.0, 0.0).astype(BF16)
    images = nn_dot(spread, high) + nn_dot(spread, low)
    y = [jnp.where(same_m, images[:, n * cycles : (n + 1) * cycles], 0.0) for n in range(POWERS)]

    own_gram = jnp.transpose(own_rows[:, : 2 * LANES])
    other_gram = jnp.transpose(other_rows[:, : 2 * LANES])
    first_gram = jnp.where(comp == 0, own_gram, other_gram)
    second_gram = jnp.where(comp == 0, other_gram, own_gram)
    grams = []
    for k in range(2):
        gram = jnp.concatenate(
            [first_gram[k * LANES : k * LANES + base], second_gram[k * LANES : k * LANES + base]], axis=0
        )
        grams.append(gram.reshape(channel_count, rows, cycles))
    group = jnp.where(
        iota((2 * cycles, cycles), 0) % cycles // m_count == iota((2 * cycles, cycles), 1) // m_count, 1.0, 0.0
    ).astype(BF16)

    def sky(image):
        image = image.reshape(channel_count, rows, cycles)
        cosine = jnp.sum(image[:, :m_count], axis=1, keepdims=True)
        sine = jnp.sum(image[:, m_count:], axis=1, keepdims=True)
        product = (grams[0] * cosine + grams[1] * sine).reshape(small, cycles)
        high, low = halves(product)
        result = nn_dot(jnp.concatenate([high, low], axis=1), group)
        return jnp.where(same_m, result, 0.0)

    expand = jnp.where(iota((small, channel_count), 0) // rows == iota((small, channel_count), 1), 1.0, 0.0)
    expand = expand.astype(BF16)
    same_row = iota((small, small), 0) % rows == iota((small, small), 1) % rows

    def spread_matrix(matrix):
        tall = nn_dot(expand, matrix).astype(BF16)
        return jnp.where(same_row, nt_dot(tall, expand), 0.0).astype(BF16)

    def spread_transpose(matrix):
        tall = nt_dot(expand, matrix).astype(BF16)
        return jnp.where(same_row, nt_dot(tall, expand), 0.0).astype(BF16)

    own_mixing = own_mixing_ref[...].astype(BF16)
    both = (nt_dot(own_mixing, own_mixing) + nt_dot(other_mixing, other_mixing)).astype(BF16)
    square_matrix = spread_matrix(both)
    forward = [spread_matrix(own_mixing), spread_matrix(other_mixing)]
    backward = [spread_transpose(own_mixing), spread_transpose(other_mixing)]
    priors = (own_prior_ref, other_prior_ref)

    def dot(a, b):
        return jnp.sum(jnp.sum(a * b, axis=0, keepdims=True), axis=1, keepdims=True)

    chunk = l_count
    starts = range(0, l_count, chunk)

    def harmonic(z, start):
        table = legendre_ref[:, start : start + chunk]
        beam = beam_ref[:, start : start + chunk][:, None, :]
        value = nn_dot(z, table).reshape(channel_count, rows, chunk) * beam
        return table, beam, value.reshape(small, chunk).astype(BF16)

    def analyse(value, table, beam):
        value = value.reshape(channel_count, rows, chunk) * beam
        return nt_dot(value.reshape(small, chunk).astype(BF16), table)

    def first_pass(z):
        z = z.astype(BF16)
        plain = jnp.zeros((small, cycles), F32)
        primed = jnp.zeros((small, cycles), F32)
        second = jnp.zeros((rows, chunk), F32)
        third = jnp.zeros((rows, chunk), F32)
        for start in starts:
            table, beam, value = harmonic(z, start)
            plain = plain + analyse(nn_dot(square_matrix, value), table, beam)
            mixed = jnp.zeros((small, chunk), F32)
            for side in range(2):
                prior = priors[side][:, start : start + chunk][:, None, :]
                once = nn_dot(backward[side], value).reshape(comp_count, rows, chunk) * prior
                twice = once * prior
                second = second + jnp.sum(once * once, axis=0)
                third = third + jnp.sum(once * twice, axis=0)
                mixed = mixed + nn_dot(forward[side], once.reshape(small, chunk).astype(BF16))
                doubled_ref[side, :, start : start + chunk] = twice.reshape(small, chunk).astype(BF16)
            primed = primed + analyse(mixed, table, beam)
        return (
            jnp.where(same_m, plain, 0.0),
            jnp.where(same_m, primed, 0.0),
            jnp.sum(jnp.sum(second, axis=0, keepdims=True), axis=1, keepdims=True),
            jnp.sum(jnp.sum(third, axis=0, keepdims=True), axis=1, keepdims=True),
        )

    def second_pass(z):
        z = z.astype(BF16)
        plain = jnp.zeros((small, cycles), F32)
        cross = jnp.zeros((rows, chunk), F32)
        own = jnp.zeros((rows, chunk), F32)
        for start in starts:
            table, beam, value = harmonic(z, start)
            plain = plain + analyse(nn_dot(square_matrix, value), table, beam)
            for side in range(2):
                prior = priors[side][:, start : start + chunk][:, None, :]
                vector = nn_dot(backward[side], value).reshape(comp_count, rows, chunk)
                twice = doubled_ref[side, :, start : start + chunk].astype(F32).reshape(comp_count, rows, chunk)
                cross = cross + jnp.sum(vector * twice, axis=0)
                own = own + jnp.sum(vector * vector * prior, axis=0)
        return (
            jnp.where(same_m, plain, 0.0),
            jnp.sum(jnp.sum(cross, axis=0, keepdims=True), axis=1, keepdims=True),
            jnp.sum(jnp.sum(own, axis=0, keepdims=True), axis=1, keepdims=True),
        )

    s = scalars
    z0 = sky(y[0])
    y_plain0, y_prime0, pp00, ppp00 = first_pass(z0)
    norm0 = s[0]
    step0 = norm0 / (s[1] + dot(y[0], z0))
    p00, uu00 = dot(z0, y_prime0), dot(z0, y_plain0)
    by0, by1, by2, by3, by4 = [dot(y[n], z0) for n in range(5)]
    norm1 = s[0] - 2.0 * step0 * (s[1] + by0) + step0 * step0 * (s[2] + 2.0 * by1 + uu00)
    ratio0 = norm1 / norm0
    y_r1 = y[0] - step0 * (y[1] + y_plain0)
    y_d1 = y_r1 + ratio0 * y[0]
    e0, e1, e2 = 1.0 + ratio0, -step0, -step0
    z1 = sky(y_d1)
    y_plain1, p2_01, p_11 = second_pass(z1)
    quadratic1 = (
        e0 * e0 * s[1] + 2.0 * e0 * e1 * s[2] + e1 * e1 * s[3]
        + 2.0 * e0 * e2 * by1 + 2.0 * e1 * e2 * by2 + e2 * e2 * p00
    )
    step1 = norm1 / (quadratic1 + dot(y_d1, z1))
    y_pd1 = e0 * y[1] + e1 * y[2] + e2 * y_prime0
    h0, h1, h2 = 1.0 + 0.0 * step1, -step0 - step1 * e0, -step1 * e1
    h3, h4, h5 = -step0, -step1 * e2, -step1
    b1y = [dot(y[n], z1) for n in range(4)]
    uu01, p01, uu11 = dot(z1, y_plain0), dot(z1, y_prime0), dot(z1, y_plain1)
    norm2 = (
        h0 * h0 * s[0] + 2.0 * h0 * h1 * s[1] + (h1 * h1 + 2.0 * h0 * h2) * s[2]
        + 2.0 * h1 * h2 * s[3] + h2 * h2 * s[4]
        + 2.0 * h3 * (h0 * by0 + h1 * by1 + h2 * by2)
        + 2.0 * h4 * (h0 * by1 + h1 * by2 + h2 * by3)
        + 2.0 * h5 * (h0 * b1y[0] + h1 * b1y[1] + h2 * b1y[2])
        + h3 * h3 * uu00 + 2.0 * h3 * h4 * p00 + h4 * h4 * pp00
        + 2.0 * h3 * h5 * uu01 + 2.0 * h4 * h5 * p01 + h5 * h5 * uu11
    )
    ratio1 = norm2 / norm1
    y_d2 = y_r1 - step1 * (y_pd1 + y_plain1) + ratio1 * y_d1
    z2 = sky(y_d2)
    h0, h1, h3 = h0 + ratio1 * e0, h1 + ratio1 * e1, h3 + ratio1 * e2
    quadratic2 = (
        h0 * h0 * s[1] + 2.0 * h0 * h1 * s[2] + (h1 * h1 + 2.0 * h0 * h2) * s[3]
        + 2.0 * h1 * h2 * s[4] + h2 * h2 * s[5]
        + 2.0 * h3 * (h0 * by1 + h1 * by2 + h2 * by3)
        + 2.0 * h4 * (h0 * by2 + h1 * by3 + h2 * by4)
        + 2.0 * h5 * (h0 * b1y[1] + h1 * b1y[2] + h2 * b1y[3])
        + h3 * h3 * p00 + 2.0 * h3 * h4 * pp00 + h4 * h4 * ppp00
        + 2.0 * h3 * h5 * p01 + 2.0 * h4 * h5 * p2_01 + h5 * h5 * p_11
    )
    step2 = norm2 / (quadratic2 + dot(y_d2, z2))

    mine_row = iota((width, small), 0)
    mine_lane = iota((width, small), 1)
    mine = (mine_lane // rows == mine_row % channel_count) & (
        mine_lane % rows == mine_row // channel_count * m_count + owner
    )
    mine = jnp.where(mine, 1.0, 0.0).astype(BF16)
    stacked = jnp.concatenate([z.astype(BF16) for z in (z0, z1, z2)], axis=1)
    stacked = nn_dot(mine, stacked).astype(BF16)
    stacked = jnp.concatenate([stacked[:, i * cycles : (i + 1) * cycles] for i in range(ITERS)], axis=0)
    groups = l_count // LANES
    for start in starts:
        table = legendre_ref[:, start : start + chunk]
        beam = beam_ref[:, start : start + chunk]
        value = nn_dot(stacked, table)
        value = [value[i * channel_count : (i + 1) * channel_count] * beam for i in range(2 * ITERS)]
        value = jnp.concatenate(value, axis=1).astype(BF16)
        vectors = lax.dot_general(own_mixing, value, (((0,), (0,)), ((), ())), preferred_element_type=F32)
        for part in range(chunk // LANES):
            prior = own_prior_ref[:, start + part * LANES : start + (part + 1) * LANES]
            for k in range(2):
                place = pl.ds(k * groups + start // LANES + part, comp_count, stride=2 * groups)
                u = []
                for i in range(ITERS):
                    begin = (2 * i + k) * chunk + part * LANES
                    u.append(vectors[:, begin : begin + LANES])
                b = rhs_ref[place, :]
                r1 = b - step0 * (prior * b + u[0])
                d1 = r1 + ratio0 * b
                r2 = r1 - step1 * (prior * d1 + u[1])
                d2 = r2 + ratio1 * d1
                solution_ref[place, :] = step0 * b + step1 * d1 + step2 * d2
                residual_ref[place, :] = r2 - step2 * (prior * d2 + u[2])


def swap(x, axis):
    return lax.ppermute(x, axis, [(0, 1), (1, 0)])


def hop(x, distance):
    return lax.ppermute(x, "blk", [(i, i ^ distance) for i in range(lax.axis_size("blk"))])


def compact(
    rhs, legendre, beam, mixing, prior, inv_noise, mask_flags, cycle_len, cycle_slot, m_values
):
    comp_count, parts, m_own, l_count = rhs.shape
    block_count = lax.axis_size("blk")
    m_count = m_values.shape[0]
    channel_width, cycle_count = mask_flags.shape
    channel_count = beam.shape[0]
    count = cycle_count * m_count
    vmem = pl.BlockSpec(memory_space=pltpu.VMEM)
    flat = rhs.reshape(comp_count * parts * l_count // LANES, LANES)
    half = l_count // 2
    side_rows = half // WIDE * SIDE_ROWS
    hbm = pl.BlockSpec(memory_space=pltpu.HBM)
    operands = (
        flat, jnp.transpose(legendre[0]), beam, mixing, prior, inv_noise, jnp.transpose(mask_flags),
        cycle_len, cycle_slot, m_values,
    )
    spaces = [pltpu.VMEM] * 7 + [pltpu.SMEM] * 3
    message, side = pl.pallas_call(
        gather_kernel,
        out_shape=[
            jax.ShapeDtypeStruct((count, WIDE), BF16),
            jax.ShapeDtypeStruct((side_rows, WIDE), BF16),
        ],
        in_specs=[hbm] * len(operands),
        out_specs=[vmem] * 2,
        scratch_shapes=[space(x.shape, x.dtype) for space, x in zip(spaces, operands)]
        + [pltpu.VMEM((count, 2 * LANES), F32), pltpu.SemaphoreType.DMA((len(operands),))],
        compiler_params=pltpu.CompilerParams(vmem_limit_bytes=63 * 1024 * 1024),
        name="gather_kernel",
    )(*operands)
    table = operands[1]
    table_two = hop(table, 2)
    bundle = hop(jnp.concatenate([message, table, table_two], axis=1), 1)
    tables = jnp.concatenate(
        [table, bundle[:, WIDE : WIDE + l_count], table_two, bundle[:, WIDE + l_count :]], axis=0
    )
    far_tables = swap(tables, "lat")
    messages = jnp.concatenate([message, bundle[:, :WIDE], hop(message, 2), hop(message, 3)], axis=0)
    crossing = swap(jnp.concatenate([messages, side], axis=0), "comp")
    near = jnp.concatenate([messages, crossing], axis=0)
    far = swap(near, "lat")

    def kernel(*refs):
        iterate_kernel(*refs, channel_width, m_count, block_count, side_rows)

    small = channel_count * 2 * m_count
    cycles = 2 * block_count * count
    answers = pl.pallas_call(
        kernel,
        out_shape=[jax.ShapeDtypeStruct(flat.shape, F32)] * 2,
        in_specs=[vmem] * 8,
        out_specs=[vmem] * 2,
        scratch_shapes=[
            pltpu.VMEM((cycles, l_count), BF16),
            pltpu.VMEM((2, small, l_count), BF16),
            pltpu.VMEM(prior.shape, F32),
        ],
        compiler_params=pltpu.CompilerParams(vmem_limit_bytes=48 * 1024 * 1024),
        name="iterate_kernel",
    )(near, far, tables, far_tables, flat, beam, mixing, prior)
    return tuple(answer.reshape(rhs.shape) for answer in answers)


def cycle_table(m_values, length, pixel_count):
    pixels = jnp.arange(pixel_count, dtype=jnp.int32)
    phase_ids = m_values[:, None] * (2 * pixels[None, :] + 1) % (2 * length)
    angles = math.pi * phase_ids.astype(jnp.float32) / length.astype(jnp.float32)
    inside = (pixels < length)[None, :]
    cosine = jnp.where(inside, jnp.cos(angles), jnp.float32(0.0))
    sine_part = jnp.where(inside, -jnp.sin(angles), jnp.float32(0.0))
    return jnp.stack([cosine, sine_part]).astype(jnp.bfloat16)


def distributed(
    rhs, legendre, beam, mixing, prior, inv_noise, mask_flags, cycle_len, cycle_slot, m_values
):
    cycle_count = inv_noise.shape[1]
    pixel_count = inv_noise.shape[2]
    channel_width = inv_noise.shape[0]
    owner_index = lax.axis_index("blk")
    comp_index = lax.axis_index("comp")
    local_ids = lax.dynamic_slice_in_dim(cycle_slot, owner_index * cycle_count, cycle_count)
    local_lengths = cycle_len[local_ids]
    legendre_slot = legendre[:, :, cycle_slot]
    weights = mask_flags.astype(jnp.float32)
    own_beam = lax.dynamic_slice_in_dim(beam, comp_index * channel_width, channel_width, 0)
    stored = jax.vmap(cycle_table, in_axes=(None, 0, None))(m_values, local_lengths, pixel_count)
    solution = jnp.zeros_like(rhs)
    residual = rhs
    direction = rhs
    for iteration in range(ITERS):
        local_mix = jnp.einsum("fc,ckml->fkml", mixing, direction, precision=HIGHEST_PRECISION)
        summed = lax.psum(local_mix.astype(jnp.bfloat16), "comp").astype(jnp.float32)
        own_part = lax.dynamic_slice_in_dim(summed, comp_index * channel_width, channel_width, 0)
        blended = (own_part * own_beam[:, None, None, :]).astype(jnp.bfloat16)
        coeffs = jnp.einsum(
            "fkml,mlr->fkmr", blended, legendre_slot, preferred_element_type=jnp.float32
        ).astype(jnp.bfloat16)
        arrived = lax.all_to_all(coeffs, "blk", split_axis=3, concat_axis=2, tiled=True)
        sky_map = jnp.einsum("fkmq,qkmp->fqp", arrived, stored, preferred_element_type=jnp.float32)
        weighted = (weights[:, :, None] * inv_noise * sky_map).astype(jnp.bfloat16)
        projected = jnp.einsum(
            "fqp,qkmp->fkmq", weighted, stored, preferred_element_type=jnp.float32
        ).astype(jnp.bfloat16)
        returned = lax.all_to_all(projected, "blk", split_axis=2, concat_axis=3, tiled=True)
        harmonic = jnp.einsum(
            "fkms,mls->fkml", returned, legendre_slot, preferred_element_type=jnp.float32
        )
        everyone = lax.all_gather(
            harmonic.astype(jnp.bfloat16), ("comp", "lat"), axis=0, tiled=True
        ).astype(harmonic.dtype)
        stacked = everyone.reshape(
            (lax.axis_size("comp"), lax.axis_size("lat"), channel_width) + harmonic.shape[1:]
        )
        summed_bands = jnp.sum(stacked, axis=1).reshape((-1,) + harmonic.shape[1:])
        backward = jnp.einsum(
            "fc,fkml->ckml",
            mixing,
            summed_bands * beam[:, None, None, :],
            precision=HIGHEST_PRECISION,
        )
        applied = prior[:, None, None, :] * direction + backward
        totals = lax.psum(
            (
                jnp.sum(direction * applied),
                jnp.sum(residual * applied),
                jnp.sum(applied * applied),
                jnp.sum(residual * residual),
            ),
            ("blk", "comp"),
        )
        curvature, cross_term, square, norm_now = totals
        step_size = norm_now / curvature
        solution = solution + step_size * direction
        residual = residual - step_size * applied
        norm_next = norm_now - 2.0 * step_size * cross_term + step_size * step_size * square
        direction = residual + norm_next / norm_now * direction
    return (solution, residual)


def fits(mesh, rhs, legendre, beam, mixing, inv_noise, m_values):
    sizes = dict(mesh.shape)
    m_count = m_values.shape[0]
    cycles = legendre.shape[2]
    slots = cycles // (sizes["blk"] * sizes["lat"])
    channels = beam.shape[0]
    width = channels // sizes["comp"]
    comps = mixing.shape[1] // sizes["comp"]
    l_count = legendre.shape[1]
    return (
        sizes["comp"] == 2
        and sizes["lat"] == 2
        and m_count == sizes["blk"] == 4
        and 2 * m_count == SUBLANES
        and cycles * m_count == LANES
        and slots * m_count == cycles // sizes["lat"] == 16
        and comps == channels
        and SIDE_ROWS - comps >= SUBLANES
        and (SIDE_ROWS - comps) * (WIDE // LANES) >= channels
        and channels % (SIDE_ROWS - comps) == 0
        and l_count % (2 * WIDE) == 0
        and channels % SUBLANES == 0
        and width * SUBLANES + 5 <= LANES
        and 2 * POWERS * channels <= 2 * LANES
        and l_count % WIDE == 0
        and inv_noise.shape[2] % WIDE == 0
        and rhs.shape[1] == 2
        and MOMENTS <= 16
    )


def solution(mesh):
    in_specs = (
        P(("groups", "comp"), None, "blk", None),
        P("blk", None, "lat"),
        P(),
        P(None, "comp"),
        P("comp", None),
        P("comp", ("blk", "lat"), None),
        P("comp", ("blk", "lat")),
        P("lat"),
        P("lat"),
        P(),
    )
    out_specs = (P(("groups", "comp"), None, "blk", None), P(("groups", "comp"), None, "blk", None))

    def whole(rhs, legendre, beam, mixing, prior, inv_noise, mask_flags, cycle_len, cycle_slot, m_values):
        small = fits(mesh, rhs, legendre, beam, mixing, inv_noise, m_values)
        local = compact if small else distributed
        mapped = jax.shard_map(local, mesh=mesh, in_specs=in_specs, out_specs=out_specs, check_vma=False)
        return mapped(
            rhs, legendre, beam, mixing, prior, inv_noise, mask_flags, cycle_len, cycle_slot, m_values
        )

    return whole
```

```python
import math

import jax
import jax.numpy as jnp
from jax import lax
from jax.experimental import pallas as pl
from jax.experimental.pallas import tpu as pltpu
from jax.sharding import PartitionSpec as P

ITERS = 3
LANES = 128
SUBLANES = 8
WIDE = 512
SIDE_ROWS = 32
MOMENTS = 2 * ITERS
POWERS = 2 * ITERS - 1
HIGHEST_PRECISION = lax.Precision.HIGHEST
F32 = jnp.float32
BF16 = jnp.bfloat16


def nt_dot(a, b):
    return lax.dot_general(a, b, (((1,), (1,)), ((), ())), preferred_element_type=F32)


def nn_dot(a, b):
    return jnp.dot(a, b, preferred_element_type=F32)


def iota(shape, dim):
    return lax.broadcasted_iota(jnp.int32, shape, dim)


def halves(x):
    high = x.astype(BF16)
    return high, (x - high.astype(F32)).astype(BF16)


def half_turn_sine(u):
    square = u * u
    total = jnp.full_like(u, -(math.pi**11) / math.factorial(11))
    for power in (9, 7, 5, 3, 1):
        sign = 1.0 if power % 4 == 1 else -1.0
        total = total * square + sign * math.pi**power / math.factorial(power)
    return total * u


def project(rhs_ref, legendre_ref, beam_ref, mixing_ref, prior_ref):
    comp_count, l_count = prior_ref.shape
    channel_count = beam_ref.shape[0]
    band_cycles = legendre_ref.shape[0]
    mixing = mixing_ref[...].astype(BF16)
    groups = l_count // LANES
    moments = [jnp.zeros((comp_count, 2 * LANES), F32) for n in range(MOMENTS)]
    used = POWERS * 2 * channel_count
    images = jnp.zeros((band_cycles, 2 * LANES), F32)
    filler = jnp.zeros((2 * LANES - used, 2 * LANES), F32)
    for pair in range(0, groups, 2):
        parts = []
        for group in (pair, pair + 1):
            lanes = slice(group * LANES, (group + 1) * LANES)
            vector = jnp.concatenate(
                [rhs_ref[pl.ds(k * groups + group, comp_count, stride=2 * groups), :] for k in range(2)], axis=1
            )
            prior = jnp.concatenate([prior_ref[:, lanes]] * 2, axis=1)
            powers = [vector]
            for n in range(1, POWERS):
                powers.append(prior * powers[-1])
            for n in range(MOMENTS):
                moments[n] = moments[n] + powers[n // 2] * powers[n - n // 2]
            mixed = nn_dot(mixing, jnp.concatenate(powers, axis=1).astype(BF16))
            beam = beam_ref[:, lanes]
            parts.append([mixed[:, i * LANES : (i + 1) * LANES] * beam for i in range(2 * POWERS)])
        blended = jnp.concatenate(
            [jnp.concatenate([parts[0][i], parts[1][i]], axis=1) for i in range(2 * POWERS)] + [filler], axis=0
        )
        images = images + nt_dot(
            legendre_ref[:, pair * LANES : (pair + 2) * LANES], blended.astype(BF16)
        )
    return images, moments


def gather_kernel(
    rhs_in, legendre_in, beam_in, mixing_in, prior_in, noise_in, mask_in, len_in, slot_in, m_in,
    out_ref, side_ref,
    rhs_ref, legendre_ref, beam_ref, mixing_ref, prior_ref, noise_ref, mask_ref, len_ref, slot_ref, m_ref,
    gram_ref, sems,
):
    sources = (slot_in, len_in, m_in, mask_in, mixing_in, prior_in, rhs_in, beam_in, legendre_in, noise_in)
    targets = (slot_ref, len_ref, m_ref, mask_ref, mixing_ref, prior_ref, rhs_ref, beam_ref, legendre_ref, noise_ref)
    copies = [pltpu.make_async_copy(a, b, sems.at[i]) for i, (a, b) in enumerate(zip(sources, targets))]
    for copy in copies:
        copy.start()
    channel_width, cycle_count, pixel_count = noise_ref.shape
    comp_count, l_count = prior_ref.shape
    m_count = m_ref.shape[0]
    band_cycles = legendre_ref.shape[0]
    rows = 2 * m_count
    owner = lax.axis_index("blk")
    band = lax.axis_index("lat")
    bands = lax.axis_size("lat")

    for copy in copies[:-1]:
        copy.wait()
    images, moments = project(rhs_ref, legendre_ref, beam_ref, mixing_ref, prior_ref)
    copies[-1].wait()

    row_ids = iota((rows, 1), 0)
    m_column = jnp.zeros((rows, 1), F32)
    for i in range(m_count):
        m_column = jnp.where(row_ids % m_count == i, m_ref[i].astype(F32), m_column)
    quarter = jnp.where(row_ids < m_count, 0.0, 0.25).astype(F32)
    chunk = min(WIDE, pixel_count)
    lengths = [len_ref[slot_ref[owner * cycle_count + q]] for q in range(cycle_count)]
    doubles = [jnp.full((rows, 1), (2 * n).astype(F32), F32) for n in lengths]
    inverses = [1.0 / double for double in doubles]
    sums = [jnp.zeros((rows, LANES), F32) for q in range(cycle_count)]
    padding = jnp.zeros((LANES - channel_width * rows, chunk), F32)
    for start in range(0, pixel_count, chunk):
        pixels = iota((rows, chunk), 1) + start
        phases = m_column * (2 * pixels + 1).astype(F32)
        for q in range(cycle_count):
            rest = phases - jnp.floor(phases * inverses[q] + 0.5) * doubles[q]
            turns = rest * inverses[q] + quarter
            turns = turns - jnp.floor(turns + 0.5)
            sine = half_turn_sine(turns)
            table = jnp.where(pixels < lengths[q], 1.0 - 2.0 * sine * sine, 0.0).astype(BF16)
            wide = table.astype(F32)
            weighted = [noise_ref[f, q : q + 1, start : start + chunk] * wide for f in range(channel_width)]
            weighted = jnp.concatenate(weighted + [padding], axis=0).astype(BF16)
            sums[q] = sums[q] + nt_dot(table, weighted)
    spread = jnp.where(iota((channel_width, LANES), 1) // rows == iota((channel_width, LANES), 0), 1.0, 0.0)
    flags = nn_dot(mask_ref[...].astype(F32).astype(BF16), spread.astype(BF16))
    for q in range(cycle_count):
        gram = sums[q] * flags[q : q + 1]
        gram_ref[q * m_count : (q + 1) * m_count, :LANES] = gram[:m_count]
        gram_ref[q * m_count : (q + 1) * m_count, LANES:] = gram[m_count:]

    count = cycle_count * m_count
    message_rows = iota((count, LANES), 0)
    lanes = iota((count, LANES), 1)
    slots = jnp.zeros((count, LANES), jnp.int32)
    for q in range(cycle_count):
        slots = jnp.where(message_rows // m_count == q, slot_ref[owner * cycle_count + q], slots)
    wanted = (message_rows % m_count * bands + band) * band_cycles + slots
    held = (owner * bands + band) * band_cycles + message_rows
    first = gram_ref[:, :LANES]
    base = channel_width * rows
    first = jnp.where(lanes == base, wanted.astype(F32), first)
    first = jnp.where(lanes == base + 1, held.astype(F32), first)
    totals = jnp.zeros((count, LANES), F32)
    for n in range(MOMENTS):
        total = jnp.sum(jnp.sum(moments[n], axis=0, keepdims=True), axis=1, keepdims=True)
        totals = jnp.where(message_rows == n, total, totals)
    for piece in range(3):
        part = totals.astype(BF16).astype(F32)
        first = jnp.where(lanes == base + 2 + piece, part, first)
        totals = totals - part
    out_ref[:, :LANES] = first.astype(BF16)
    out_ref[:, LANES : 2 * LANES] = gram_ref[:, LANES:].astype(BF16)
    out_ref[:, 2 * LANES :] = images.astype(BF16)
    half = l_count // 2
    spare = side_ref.shape[0] // (half // WIDE) - comp_count
    for piece in range(half // WIDE):
        lanes = pl.ds(pl.multiple_of(band * half + piece * WIDE, WIDE), WIDE)
        block = [prior_ref[:, lanes]]
        strips = []
        for i in range(WIDE // LANES):
            begin = i * spare
            if piece == 0 and begin < mixing_ref.shape[0]:
                strip = jnp.concatenate(
                    [mixing_ref[begin : begin + spare, :], jnp.zeros((spare, LANES - comp_count), F32)], axis=1
                )
            else:
                strip = jnp.zeros((spare, LANES), F32)
            strips.append(strip)
        block.append(jnp.concatenate(strips, axis=1))
        side_ref[piece * (comp_count + spare) : (piece + 1) * (comp_count + spare), :] = jnp.concatenate(
            block, axis=0
        ).astype(BF16)


def iterate_kernel(
    near_ref, far_ref, near_legendre_ref, far_legendre_ref, rhs_ref, beam_ref, own_mixing_ref, own_prior_ref,
    solution_ref, residual_ref, legendre_ref, doubled_ref, other_prior_ref, channel_width, m_count, block_count,
    side_rows,
):
    comp_count, l_count = own_prior_ref.shape
    channel_count = beam_ref.shape[0]
    rows = 2 * m_count
    count = (near_ref.shape[0] - side_rows) // (block_count * 2)
    cycles = 2 * block_count * count
    small = channel_count * rows
    base = channel_width * rows
    owner = lax.axis_index("blk")
    comp = lax.axis_index("comp")
    band = lax.axis_index("lat")

    half = l_count // 2
    step = side_rows // (half // WIDE)
    side_begin = near_ref.shape[0] - side_rows
    for ref, place in ((near_ref, band), (far_ref, 1 - band)):
        for piece in range(half // WIDE):
            lanes = pl.ds(pl.multiple_of(place * half + piece * WIDE, WIDE), WIDE)
            block = ref[side_begin + piece * step : side_begin + (piece + 1) * step, :].astype(F32)
            other_prior_ref[:, lanes] = block[:comp_count]
    block = near_ref[side_begin : side_begin + step, :].astype(F32)[comp_count:]
    strips = [block[:, i * LANES : i * LANES + comp_count] for i in range(channel_count // (step - comp_count))]
    other_mixing = jnp.concatenate(strips, axis=0).astype(BF16)

    span = block_count * count
    own_rows = jnp.concatenate([near_ref[:span, :], far_ref[:span, :]], axis=0).astype(F32)
    other_rows = jnp.concatenate([near_ref[span : 2 * span, :], far_ref[span : 2 * span, :]], axis=0).astype(F32)

    pieces_sum = own_rows[:, :LANES] + other_rows[:, :LANES]
    scalars = []
    for n in range(MOMENTS):
        total = jnp.zeros((1, LANES), F32)
        for i in range(block_count):
            total = total + pieces_sum[i * count + n : i * count + n + 1, :]
        lane = iota((1, LANES), 1)
        keep = (lane >= base + 2) & (lane < base + 5)
        scalars.append(jnp.sum(jnp.where(keep, total, 0.0), axis=1, keepdims=True))

    wanted = own_rows[:, base : base + 1]
    held = jnp.transpose(jnp.broadcast_to(own_rows[:, base + 1 : base + 2], (cycles, cycles)))
    pick = jnp.where(wanted == held, 1.0, 0.0).astype(BF16)
    blocks = jnp.concatenate([near_legendre_ref[...], far_legendre_ref[...]], axis=0)
    legendre_ref[...] = nn_dot(pick, blocks).astype(BF16)

    row = iota((small, cycles), 0)
    lane = iota((small, cycles), 1)
    same_m = row % m_count == lane % m_count
    summed = jnp.transpose((own_rows + other_rows)[:, 2 * LANES :])
    high, low = halves(summed)
    images = nt_dot(jnp.concatenate([high, low], axis=1), jnp.concatenate([pick, pick], axis=1))
    width = 2 * channel_count
    images = jnp.concatenate([images[n * width : (n + 1) * width] for n in range(POWERS)], axis=1)
    high, low = halves(images)
    spread_row = iota((small, width), 0)
    spread_lane = iota((small, width), 1)
    spread = (spread_row // rows == spread_lane % channel_count) & (
        spread_row % rows // m_count == spread_lane // channel_count
    )
    spread = jnp.where(spread, 1.0, 0.0).astype(BF16)
    images = nn_dot(spread, high) + nn_dot(spread, low)
    y = [jnp.where(same_m, images[:, n * cycles : (n + 1) * cycles], 0.0) for n in range(POWERS)]

    own_gram = jnp.transpose(own_rows[:, : 2 * LANES])
    other_gram = jnp.transpose(other_rows[:, : 2 * LANES])
    first_gram = jnp.where(comp == 0, own_gram, other_gram)
    second_gram = jnp.where(comp == 0, other_gram, own_gram)
    grams = []
    for k in range(2):
        gram = jnp.concatenate(
            [first_gram[k * LANES : k * LANES + base], second_gram[k * LANES : k * LANES + base]], axis=0
        )
        grams.append(gram.reshape(channel_count, rows, cycles))
    group = jnp.where(
        iota((2 * cycles, cycles), 0) % cycles // m_count == iota((2 * cycles, cycles), 1) // m_count, 1.0, 0.0
    ).astype(BF16)

    def sky(image):
        image = image.reshape(channel_count, rows, cycles)
        cosine = jnp.sum(image[:, :m_count], axis=1, keepdims=True)
        sine = jnp.sum(image[:, m_count:], axis=1, keepdims=True)
        product = (grams[0] * cosine + grams[1] * sine).reshape(small, cycles)
        high, low = halves(product)
        result = nn_dot(jnp.concatenate([high, low], axis=1), group)
        return jnp.where(same_m, result, 0.0)

    expand = jnp.where(iota((small, channel_count), 0) // rows == iota((small, channel_count), 1), 1.0, 0.0)
    expand = expand.astype(BF16)
    same_row = iota((small, small), 0) % rows == iota((small, small), 1) % rows

    def spread_matrix(matrix):
        tall = nn_dot(expand, matrix).astype(BF16)
        return jnp.where(same_row, nt_dot(tall, expand), 0.0).astype(BF16)

    def spread_transpose(matrix):
        tall = nt_dot(expand, matrix).astype(BF16)
        return jnp.where(same_row, nt_dot(tall, expand), 0.0).astype(BF16)

    own_mixing = own_mixing_ref[...].astype(BF16)
    both = (nt_dot(own_mixing, own_mixing) + nt_dot(other_mixing, other_mixing)).astype(BF16)
    square_matrix = spread_matrix(both)
    forward = [spread_matrix(own_mixing), spread_matrix(other_mixing)]
    backward = [spread_transpose(own_mixing), spread_transpose(other_mixing)]
    priors = (own_prior_ref, other_prior_ref)

    def dot(a, b):
        return jnp.sum(jnp.sum(a * b, axis=0, keepdims=True), axis=1, keepdims=True)

    chunk = l_count
    starts = range(0, l_count, chunk)

    def harmonic(z, start):
        table = legendre_ref[:, start : start + chunk]
        beam = beam_ref[:, start : start + chunk][:, None, :]
        value = nn_dot(z, table).reshape(channel_count, rows, chunk) * beam
        return table, beam, value.reshape(small, chunk).astype(BF16)

    def analyse(value, table, beam):
        value = value.reshape(channel_count, rows, chunk) * beam
        return nt_dot(value.reshape(small, chunk).astype(BF16), table)

    def first_pass(z):
        z = z.astype(BF16)
        plain = jnp.zeros((small, cycles), F32)
        primed = jnp.zeros((small, cycles), F32)
        second = jnp.zeros((rows, chunk), F32)
        third = jnp.zeros((rows, chunk), F32)
        for start in starts:
            table, beam, value = harmonic(z, start)
            plain = plain + analyse(nn_dot(square_matrix, value), table, beam)
            mixed = jnp.zeros((small, chunk), F32)
            for side in range(2):
                prior = priors[side][:, start : start + chunk][:, None, :]
                once = nn_dot(backward[side], value).reshape(comp_count, rows, chunk) * prior
                twice = once * prior
                second = second + jnp.sum(once * once, axis=0)
                third = third + jnp.sum(once * twice, axis=0)
                mixed = mixed + nn_dot(forward[side], once.reshape(small, chunk).astype(BF16))
                doubled_ref[side, :, start : start + chunk] = twice.reshape(small, chunk).astype(BF16)
            primed = primed + analyse(mixed, table, beam)
        return (
            jnp.where(same_m, plain, 0.0),
            jnp.where(same_m, primed, 0.0),
            jnp.sum(jnp.sum(second, axis=0, keepdims=True), axis=1, keepdims=True),
            jnp.sum(jnp.sum(third, axis=0, keepdims=True), axis=1, keepdims=True),
        )

    def second_pass(z):
        z = z.astype(BF16)
        plain = jnp.zeros((small, cycles), F32)
        cross = jnp.zeros((rows, chunk), F32)
        own = jnp.zeros((rows, chunk), F32)
        for start in starts:
            table, beam, value = harmonic(z, start)
            plain = plain + analyse(nn_dot(square_matrix, value), table, beam)
            for side in range(2):
                prior = priors[side][:, start : start + chunk][:, None, :]
                vector = nn_dot(backward[side], value).reshape(comp_count, rows, chunk)
                twice = doubled_ref[side, :, start : start + chunk].astype(F32).reshape(comp_count, rows, chunk)
                cross = cross + jnp.sum(vector * twice, axis=0)
                own = own + jnp.sum(vector * vector * prior, axis=0)
        return (
            jnp.where(same_m, plain, 0.0),
            jnp.sum(jnp.sum(cross, axis=0, keepdims=True), axis=1, keepdims=True),
            jnp.sum(jnp.sum(own, axis=0, keepdims=True), axis=1, keepdims=True),
        )

    s = scalars
    z0 = sky(y[0])
    y_plain0, y_prime0, pp00, ppp00 = first_pass(z0)
    norm0 = s[0]
    step0 = norm0 / (s[1] + dot(y[0], z0))
    p00, uu00 = dot(z0, y_prime0), dot(z0, y_plain0)
    by0, by1, by2, by3, by4 = [dot(y[n], z0) for n in range(5)]
    norm1 = s[0] - 2.0 * step0 * (s[1] + by0) + step0 * step0 * (s[2] + 2.0 * by1 + uu00)
    ratio0 = norm1 / norm0
    y_r1 = y[0] - step0 * (y[1] + y_plain0)
    y_d1 = y_r1 + ratio0 * y[0]
    e0, e1, e2 = 1.0 + ratio0, -step0, -step0
    z1 = sky(y_d1)
    y_plain1, p2_01, p_11 = second_pass(z1)
    quadratic1 = (
        e0 * e0 * s[1] + 2.0 * e0 * e1 * s[2] + e1 * e1 * s[3]
        + 2.0 * e0 * e2 * by1 + 2.0 * e1 * e2 * by2 + e2 * e2 * p00
    )
    step1 = norm1 / (quadratic1 + dot(y_d1, z1))
    y_pd1 = e0 * y[1] + e1 * y[2] + e2 * y_prime0
    h0, h1, h2 = 1.0 + 0.0 * step1, -step0 - step1 * e0, -step1 * e1
    h3, h4, h5 = -step0, -step1 * e2, -step1
    b1y = [dot(y[n], z1) for n in range(4)]
    uu01, p01, uu11 = dot(z1, y_plain0), dot(z1, y_prime0), dot(z1, y_plain1)
    norm2 = (
        h0 * h0 * s[0] + 2.0 * h0 * h1 * s[1] + (h1 * h1 + 2.0 * h0 * h2) * s[2]
        + 2.0 * h1 * h2 * s[3] + h2 * h2 * s[4]
        + 2.0 * h3 * (h0 * by0 + h1 * by1 + h2 * by2)
        + 2.0 * h4 * (h0 * by1 + h1 * by2 + h2 * by3)
        + 2.0 * h5 * (h0 * b1y[0] + h1 * b1y[1] + h2 * b1y[2])
        + h3 * h3 * uu00 + 2.0 * h3 * h4 * p00 + h4 * h4 * pp00
        + 2.0 * h3 * h5 * uu01 + 2.0 * h4 * h5 * p01 + h5 * h5 * uu11
    )
    ratio1 = norm2 / norm1
    y_d2 = y_r1 - step1 * (y_pd1 + y_plain1) + ratio1 * y_d1
    z2 = sky(y_d2)
    h0, h1, h3 = h0 + ratio1 * e0, h1 + ratio1 * e1, h3 + ratio1 * e2
    quadratic2 = (
        h0 * h0 * s[1] + 2.0 * h0 * h1 * s[2] + (h1 * h1 + 2.0 * h0 * h2) * s[3]
        + 2.0 * h1 * h2 * s[4] + h2 * h2 * s[5]
        + 2.0 * h3 * (h0 * by1 + h1 * by2 + h2 * by3)
        + 2.0 * h4 * (h0 * by2 + h1 * by3 + h2 * by4)
        + 2.0 * h5 * (h0 * b1y[1] + h1 * b1y[2] + h2 * b1y[3])
        + h3 * h3 * p00 + 2.0 * h3 * h4 * pp00 + h4 * h4 * ppp00
        + 2.0 * h3 * h5 * p01 + 2.0 * h4 * h5 * p2_01 + h5 * h5 * p_11
    )
    step2 = norm2 / (quadratic2 + dot(y_d2, z2))

    mine_row = iota((width, small), 0)
    mine_lane = iota((width, small), 1)
    mine = (mine_lane // rows == mine_row % channel_count) & (
        mine_lane % rows == mine_row // channel_count * m_count + owner
    )
    mine = jnp.where(mine, 1.0, 0.0).astype(BF16)
    stacked = jnp.concatenate([z.astype(BF16) for z in (z0, z1, z2)], axis=1)
    stacked = nn_dot(mine, stacked).astype(BF16)
    stacked = jnp.concatenate([stacked[:, i * cycles : (i + 1) * cycles] for i in range(ITERS)], axis=0)
    groups = l_count // LANES
    for start in starts:
        table = legendre_ref[:, start : start + chunk]
        beam = beam_ref[:, start : start + chunk]
        value = nn_dot(stacked, table)
        value = [value[i * channel_count : (i + 1) * channel_count] * beam for i in range(2 * ITERS)]
        value = jnp.concatenate(value, axis=1).astype(BF16)
        vectors = lax.dot_general(own_mixing, value, (((0,), (0,)), ((), ())), preferred_element_type=F32)
        for part in range(chunk // LANES):
            prior = own_prior_ref[:, start + part * LANES : start + (part + 1) * LANES]
            for k in range(2):
                place = pl.ds(k * groups + start // LANES + part, comp_count, stride=2 * groups)
                u = []
                for i in range(ITERS):
                    begin = (2 * i + k) * chunk + part * LANES
                    u.append(vectors[:, begin : begin + LANES])
                b = rhs_ref[place, :]
                r1 = b - step0 * (prior * b + u[0])
                d1 = r1 + ratio0 * b
                r2 = r1 - step1 * (prior * d1 + u[1])
                d2 = r2 + ratio1 * d1
                solution_ref[place, :] = step0 * b + step1 * d1 + step2 * d2
                residual_ref[place, :] = r2 - step2 * (prior * d2 + u[2])


def swap(x, axis):
    return lax.ppermute(x, axis, [(0, 1), (1, 0)])


def hop(x, distance):
    return lax.ppermute(x, "blk", [(i, i ^ distance) for i in range(lax.axis_size("blk"))])


def compact(
    rhs, legendre, beam, mixing, prior, inv_noise, mask_flags, cycle_len, cycle_slot, m_values
):
    comp_count, parts, m_own, l_count = rhs.shape
    block_count = lax.axis_size("blk")
    m_count = m_values.shape[0]
    channel_width, cycle_count = mask_flags.shape
    channel_count = beam.shape[0]
    count = cycle_count * m_count
    vmem = pl.BlockSpec(memory_space=pltpu.VMEM)
    flat = rhs.reshape(comp_count * parts * l_count // LANES, LANES)
    half = l_count // 2
    side_rows = half // WIDE * SIDE_ROWS
    hbm = pl.BlockSpec(memory_space=pltpu.HBM)
    operands = (
        flat, jnp.transpose(legendre[0]), beam, mixing, prior, inv_noise, jnp.transpose(mask_flags),
        cycle_len, cycle_slot, m_values,
    )
    spaces = [pltpu.VMEM] * 7 + [pltpu.SMEM] * 3
    message, side = pl.pallas_call(
        gather_kernel,
        out_shape=[
            pltpu.VMEM((count, WIDE), BF16),
            pltpu.VMEM((side_rows, WIDE), BF16),
        ],
        in_specs=[hbm] * len(operands),
        out_specs=[vmem] * 2,
        scratch_shapes=[space(x.shape, x.dtype) for space, x in zip(spaces, operands)]
        + [pltpu.VMEM((count, 2 * LANES), F32), pltpu.SemaphoreType.DMA((len(operands),))],
        compiler_params=pltpu.CompilerParams(vmem_limit_bytes=40 * 1024 * 1024),
        name="gather_kernel",
    )(*[pltpu.with_memory_space_constraint(x, pltpu.HBM) for x in operands])
    table = operands[1]
    hops = [hop(message, 1), hop(message, 2), hop(message, 3)]
    table_two = hop(table, 2)
    bundle = hop(jnp.concatenate([table, table_two], axis=1), 1)
    tables = jnp.concatenate([table, bundle[:, :l_count], table_two, bundle[:, l_count:]], axis=0)
    far_tables = swap(tables, "lat")
    messages = jnp.concatenate([message] + hops, axis=0)
    crossing = swap(jnp.concatenate([messages, side], axis=0), "comp")
    near = jnp.concatenate([messages, crossing], axis=0)
    far = swap(near, "lat")

    def kernel(*refs):
        iterate_kernel(*refs, channel_width, m_count, block_count, side_rows)

    small = channel_count * 2 * m_count
    cycles = 2 * block_count * count
    answers = pl.pallas_call(
        kernel,
        out_shape=[jax.ShapeDtypeStruct(flat.shape, F32)] * 2,
        in_specs=[vmem] * 8,
        out_specs=[vmem] * 2,
        scratch_shapes=[
            pltpu.VMEM((cycles, l_count), BF16),
            pltpu.VMEM((2, small, l_count), BF16),
            pltpu.VMEM(prior.shape, F32),
        ],
        compiler_params=pltpu.CompilerParams(vmem_limit_bytes=48 * 1024 * 1024),
        name="iterate_kernel",
    )(near, far, tables, far_tables, flat, beam, mixing, prior)
    return tuple(answer.reshape(rhs.shape) for answer in answers)


def cycle_table(m_values, length, pixel_count):
    pixels = jnp.arange(pixel_count, dtype=jnp.int32)
    phase_ids = m_values[:, None] * (2 * pixels[None, :] + 1) % (2 * length)
    angles = math.pi * phase_ids.astype(jnp.float32) / length.astype(jnp.float32)
    inside = (pixels < length)[None, :]
    cosine = jnp.where(inside, jnp.cos(angles), jnp.float32(0.0))
    sine_part = jnp.where(inside, -jnp.sin(angles), jnp.float32(0.0))
    return jnp.stack([cosine, sine_part]).astype(jnp.bfloat16)


def distributed(
    rhs, legendre, beam, mixing, prior, inv_noise, mask_flags, cycle_len, cycle_slot, m_values
):
    cycle_count = inv_noise.shape[1]
    pixel_count = inv_noise.shape[2]
    channel_width = inv_noise.shape[0]
    owner_index = lax.axis_index("blk")
    comp_index = lax.axis_index("comp")
    local_ids = lax.dynamic_slice_in_dim(cycle_slot, owner_index * cycle_count, cycle_count)
    local_lengths = cycle_len[local_ids]
    legendre_slot = legendre[:, :, cycle_slot]
    weights = mask_flags.astype(jnp.float32)
    own_beam = lax.dynamic_slice_in_dim(beam, comp_index * channel_width, channel_width, 0)
    stored = jax.vmap(cycle_table, in_axes=(None, 0, None))(m_values, local_lengths, pixel_count)
    solution = jnp.zeros_like(rhs)
    residual = rhs
    direction = rhs
    for iteration in range(ITERS):
        local_mix = jnp.einsum("fc,ckml->fkml", mixing, direction, precision=HIGHEST_PRECISION)
        summed = lax.psum(local_mix.astype(jnp.bfloat16), "comp").astype(jnp.float32)
        own_part = lax.dynamic_slice_in_dim(summed, comp_index * channel_width, channel_width, 0)
        blended = (own_part * own_beam[:, None, None, :]).astype(jnp.bfloat16)
        coeffs = jnp.einsum(
            "fkml,mlr->fkmr", blended, legendre_slot, preferred_element_type=jnp.float32
        ).astype(jnp.bfloat16)
        arrived = lax.all_to_all(coeffs, "blk", split_axis=3, concat_axis=2, tiled=True)
        sky_map = jnp.einsum("fkmq,qkmp->fqp", arrived, stored, preferred_element_type=jnp.float32)
        weighted = (weights[:, :, None] * inv_noise * sky_map).astype(jnp.bfloat16)
        projected = jnp.einsum(
            "fqp,qkmp->fkmq", weighted, stored, preferred_element_type=jnp.float32
        ).astype(jnp.bfloat16)
        returned = lax.all_to_all(projected, "blk", split_axis=2, concat_axis=3, tiled=True)
        harmonic = jnp.einsum(
            "fkms,mls->fkml", returned, legendre_slot, preferred_element_type=jnp.float32
        )
        everyone = lax.all_gather(
            harmonic.astype(jnp.bfloat16), ("comp", "lat"), axis=0, tiled=True
        ).astype(harmonic.dtype)
        stacked = everyone.reshape(
            (lax.axis_size("comp"), lax.axis_size("lat"), channel_width) + harmonic.shape[1:]
        )
        summed_bands = jnp.sum(stacked, axis=1).reshape((-1,) + harmonic.shape[1:])
        backward = jnp.einsum(
            "fc,fkml->ckml",
            mixing,
            summed_bands * beam[:, None, None, :],
            precision=HIGHEST_PRECISION,
        )
        applied = prior[:, None, None, :] * direction + backward
        totals = lax.psum(
            (
                jnp.sum(direction * applied),
                jnp.sum(residual * applied),
                jnp.sum(applied * applied),
                jnp.sum(residual * residual),
            ),
            ("blk", "comp"),
        )
        curvature, cross_term, square, norm_now = totals
        step_size = norm_now / curvature
        solution = solution + step_size * direction
        residual = residual - step_size * applied
        norm_next = norm_now - 2.0 * step_size * cross_term + step_size * step_size * square
        direction = residual + norm_next / norm_now * direction
    return (solution, residual)


def fits(mesh, rhs, legendre, beam, mixing, inv_noise, m_values):
    sizes = dict(mesh.shape)
    m_count = m_values.shape[0]
    cycles = legendre.shape[2]
    slots = cycles // (sizes["blk"] * sizes["lat"])
    channels = beam.shape[0]
    width = channels // sizes["comp"]
    comps = mixing.shape[1] // sizes["comp"]
    l_count = legendre.shape[1]
    return (
        sizes["comp"] == 2
        and sizes["lat"] == 2
        and m_count == sizes["blk"] == 4
        and 2 * m_count == SUBLANES
        and cycles * m_count == LANES
        and slots * m_count == cycles // sizes["lat"] == 16
        and comps == channels
        and SIDE_ROWS - comps >= SUBLANES
        and (SIDE_ROWS - comps) * (WIDE // LANES) >= channels
        and channels % (SIDE_ROWS - comps) == 0
        and l_count % (2 * WIDE) == 0
        and channels % SUBLANES == 0
        and width * SUBLANES + 5 <= LANES
        and 2 * POWERS * channels <= 2 * LANES
        and l_count % WIDE == 0
        and inv_noise.shape[2] % WIDE == 0
        and rhs.shape[1] == 2
        and MOMENTS <= 16
    )


def solution(mesh):
    in_specs = (
        P(("groups", "comp"), None, "blk", None),
        P("blk", None, "lat"),
        P(),
        P(None, "comp"),
        P("comp", None),
        P("comp", ("blk", "lat"), None),
        P("comp", ("blk", "lat")),
        P("lat"),
        P("lat"),
        P(),
    )
    out_specs = (P(("groups", "comp"), None, "blk", None), P(("groups", "comp"), None, "blk", None))

    def whole(rhs, legendre, beam, mixing, prior, inv_noise, mask_flags, cycle_len, cycle_slot, m_values):
        small = fits(mesh, rhs, legendre, beam, mixing, inv_noise, m_values)
        local = compact if small else distributed
        mapped = jax.shard_map(local, mesh=mesh, in_specs=in_specs, out_specs=out_specs, check_vma=False)
        return mapped(
            rhs, legendre, beam, mixing, prior, inv_noise, mask_flags, cycle_len, cycle_slot, m_values
        )

    return whole
```

```python
import functools
import math

import jax
import jax.numpy as jnp
from jax import lax
from jax.experimental import pallas as pl
from jax.experimental.pallas import tpu as pltpu
from jax.sharding import PartitionSpec as P

ITERS = 3
LANES = 128
SUBLANES = 8
WIDE = 512
SIDE_ROWS = 32
PIECES = 4
MOMENTS = 2 * ITERS
POWERS = 2 * ITERS - 1
HIGHEST_PRECISION = lax.Precision.HIGHEST
F32 = jnp.float32
BF16 = jnp.bfloat16


def nt_dot(a, b):
    return lax.dot_general(a, b, (((1,), (1,)), ((), ())), preferred_element_type=F32)


def nn_dot(a, b):
    return jnp.dot(a, b, preferred_element_type=F32)


def iota(shape, dim):
    return lax.broadcasted_iota(jnp.int32, shape, dim)


def halves(x):
    high = x.astype(BF16)
    return high, (x - high.astype(F32)).astype(BF16)


def plane_copies(outside, inside, sems, inward):
    copies = []
    width = inside.shape[2] // sems.shape[0]
    for piece in range(sems.shape[0]):
        for k in range(inside.shape[0]):
            lanes = pl.ds(piece * width, width)
            pair = (outside.at[:, k, 0, lanes], inside.at[k, :, lanes])
            source, target = pair if inward else pair[::-1]
            copies.append(pltpu.make_async_copy(source, target, sems.at[piece, k]))
    return copies


def half_turn_sine(u):
    square = u * u
    total = jnp.full_like(u, -(math.pi**11) / math.factorial(11))
    for power in (9, 7, 5, 3, 1):
        sign = 1.0 if power % 4 == 1 else -1.0
        total = total * square + sign * math.pi**power / math.factorial(power)
    return total * u


def project(rhs_ref, legendre_ref, beam_ref, mixing_ref, prior_ref):
    comp_count, l_count = prior_ref.shape
    channel_count = beam_ref.shape[0]
    band_cycles = legendre_ref.shape[0]
    mixing = mixing_ref[...].astype(BF16)
    groups = l_count // LANES
    moments = [jnp.zeros((comp_count, 2 * LANES), F32) for n in range(MOMENTS)]
    used = POWERS * 2 * channel_count
    images = jnp.zeros((band_cycles, 2 * LANES), F32)
    filler = jnp.zeros((2 * LANES - used, 2 * LANES), F32)
    for pair in range(0, groups, 2):
        parts = []
        for group in (pair, pair + 1):
            lanes = slice(group * LANES, (group + 1) * LANES)
            vector = jnp.concatenate(
                [rhs_ref[k, :, lanes] for k in range(2)], axis=1
            )
            prior = jnp.concatenate([prior_ref[:, lanes]] * 2, axis=1)
            powers = [vector]
            for n in range(1, POWERS):
                powers.append(prior * powers[-1])
            for n in range(MOMENTS):
                moments[n] = moments[n] + powers[n // 2] * powers[n - n // 2]
            mixed = nn_dot(mixing, jnp.concatenate(powers, axis=1).astype(BF16))
            beam = beam_ref[:, lanes]
            parts.append([mixed[:, i * LANES : (i + 1) * LANES] * beam for i in range(2 * POWERS)])
        blended = jnp.concatenate(
            [jnp.concatenate([parts[0][i], parts[1][i]], axis=1) for i in range(2 * POWERS)] + [filler], axis=0
        )
        images = images + nt_dot(
            legendre_ref[:, pair * LANES : (pair + 2) * LANES], blended.astype(BF16)
        )
    return images, moments


def gather_kernel(
    rhs_in, legendre_in, beam_in, mixing_in, prior_in, noise_in, mask_in, len_in, slot_in, m_in,
    out_ref, side_ref,
    rhs_ref, legendre_ref, beam_ref, mixing_ref, prior_ref, noise_ref, mask_ref, len_ref, slot_ref, m_ref,
    gram_ref, sems, rhs_sems,
):
    sources = (slot_in, len_in, m_in, mask_in, mixing_in, prior_in, beam_in, legendre_in, noise_in)
    targets = (slot_ref, len_ref, m_ref, mask_ref, mixing_ref, prior_ref, beam_ref, legendre_ref, noise_ref)
    copies = [pltpu.make_async_copy(a, b, sems.at[i]) for i, (a, b) in enumerate(zip(sources, targets))]
    copies = plane_copies(rhs_in, rhs_ref, rhs_sems, True) + copies
    for copy in copies:
        copy.start()
    channel_width, cycle_count, pixel_count = noise_ref.shape
    comp_count, l_count = prior_ref.shape
    m_count = m_ref.shape[0]
    band_cycles = legendre_ref.shape[0]
    rows = 2 * m_count
    owner = lax.axis_index("blk")
    band = lax.axis_index("lat")
    bands = lax.axis_size("lat")

    for copy in copies[:-1]:
        copy.wait()
    images, moments = project(rhs_ref, legendre_ref, beam_ref, mixing_ref, prior_ref)
    copies[-1].wait()

    row_ids = iota((rows, 1), 0)
    m_column = jnp.zeros((rows, 1), F32)
    for i in range(m_count):
        m_column = jnp.where(row_ids % m_count == i, m_ref[i].astype(F32), m_column)
    quarter = jnp.where(row_ids < m_count, 0.0, 0.25).astype(F32)
    chunk = min(WIDE, pixel_count)
    lengths = [len_ref[slot_ref[owner * cycle_count + q]] for q in range(cycle_count)]
    doubles = [jnp.full((rows, 1), (2 * n).astype(F32), F32) for n in lengths]
    inverses = [1.0 / double for double in doubles]
    sums = [jnp.zeros((rows, LANES), F32) for q in range(cycle_count)]
    padding = jnp.zeros((LANES - channel_width * rows, chunk), F32)
    for start in range(0, pixel_count, chunk):
        pixels = iota((rows, chunk), 1) + start
        phases = m_column * (2 * pixels + 1).astype(F32)
        for q in range(cycle_count):
            rest = phases - jnp.floor(phases * inverses[q] + 0.5) * doubles[q]
            turns = rest * inverses[q] + quarter
            turns = turns - jnp.floor(turns + 0.5)
            sine = half_turn_sine(turns)
            table = jnp.where(pixels < lengths[q], 1.0 - 2.0 * sine * sine, 0.0).astype(BF16)
            wide = table.astype(F32)
            weighted = [noise_ref[f, q : q + 1, start : start + chunk] * wide for f in range(channel_width)]
            weighted = jnp.concatenate(weighted + [padding], axis=0).astype(BF16)
            sums[q] = sums[q] + nt_dot(table, weighted)
    spread = jnp.where(iota((channel_width, LANES), 1) // rows == iota((channel_width, LANES), 0), 1.0, 0.0)
    flags = nn_dot(mask_ref[...].astype(F32).astype(BF16), spread.astype(BF16))
    for q in range(cycle_count):
        gram = sums[q] * flags[q : q + 1]
        gram_ref[q * m_count : (q + 1) * m_count, :LANES] = gram[:m_count]
        gram_ref[q * m_count : (q + 1) * m_count, LANES:] = gram[m_count:]

    count = cycle_count * m_count
    message_rows = iota((count, LANES), 0)
    lanes = iota((count, LANES), 1)
    slots = jnp.zeros((count, LANES), jnp.int32)
    for q in range(cycle_count):
        slots = jnp.where(message_rows // m_count == q, slot_ref[owner * cycle_count + q], slots)
    wanted = (message_rows % m_count * bands + band) * band_cycles + slots
    held = (owner * bands + band) * band_cycles + message_rows
    first = gram_ref[:, :LANES]
    base = channel_width * rows
    first = jnp.where(lanes == base, wanted.astype(F32), first)
    first = jnp.where(lanes == base + 1, held.astype(F32), first)
    totals = jnp.zeros((count, LANES), F32)
    for n in range(MOMENTS):
        total = jnp.sum(jnp.sum(moments[n], axis=0, keepdims=True), axis=1, keepdims=True)
        totals = jnp.where(message_rows == n, total, totals)
    for piece in range(3):
        part = totals.astype(BF16).astype(F32)
        first = jnp.where(lanes == base + 2 + piece, part, first)
        totals = totals - part
    out_ref[:, :LANES] = first.astype(BF16)
    out_ref[:, LANES : 2 * LANES] = gram_ref[:, LANES:].astype(BF16)
    out_ref[:, 2 * LANES :] = images.astype(BF16)
    half = l_count // 2
    spare = side_ref.shape[0] // (half // WIDE) - comp_count
    for piece in range(half // WIDE):
        lanes = pl.ds(pl.multiple_of(band * half + piece * WIDE, WIDE), WIDE)
        block = [prior_ref[:, lanes]]
        strips = []
        for i in range(WIDE // LANES):
            begin = i * spare
            if piece == 0 and begin < mixing_ref.shape[0]:
                strip = jnp.concatenate(
                    [mixing_ref[begin : begin + spare, :], jnp.zeros((spare, LANES - comp_count), F32)], axis=1
                )
            else:
                strip = jnp.zeros((spare, LANES), F32)
            strips.append(strip)
        block.append(jnp.concatenate(strips, axis=1))
        side_ref[piece * (comp_count + spare) : (piece + 1) * (comp_count + spare), :] = jnp.concatenate(
            block, axis=0
        ).astype(BF16)


def widen(talls, expand):
    small = expand.shape[0]
    rows = small // expand.shape[1]
    wide = nt_dot(jnp.concatenate([tall.astype(BF16) for tall in talls], axis=0), expand)
    same_row = iota((small, small), 0) % rows == iota((small, small), 1) % rows
    return [jnp.where(same_row, wide[i * small : (i + 1) * small], 0.0).astype(BF16) for i in range(len(talls))]


def expander(small, count):
    rows = small // count
    return jnp.where(iota((small, count), 0) // rows == iota((small, count), 1), 1.0, 0.0).astype(BF16)


def iterate_kernel(
    near_ref, far_ref, near_legendre_ref, far_legendre_ref, beam_ref, own_mixing_ref,
    own_prior_ref, rhs_in,
    solution_out, residual_out, legendre_ref, once_ref, other_prior_ref, rhs_ref, solution_ref, residual_ref,
    rhs_sems, solution_sems, residual_sems, channel_width, m_count, block_count, side_rows,
):
    arrivals = plane_copies(rhs_in, rhs_ref, rhs_sems, True)
    for copy in arrivals:
        copy.start()
    departures = plane_copies(solution_out, solution_ref, solution_sems, False)
    departures = list(zip(departures, plane_copies(residual_out, residual_ref, residual_sems, False)))
    comp_count, l_count = own_prior_ref.shape
    channel_count = beam_ref.shape[0]
    rows = 2 * m_count
    count = (near_ref.shape[0] - side_rows) // (block_count * 2)
    cycles = 2 * block_count * count
    small = channel_count * rows
    base = channel_width * rows
    owner = lax.axis_index("blk")
    comp = lax.axis_index("comp")
    band = lax.axis_index("lat")

    half = l_count // 2
    step = side_rows // (half // WIDE)
    side_begin = near_ref.shape[0] - side_rows
    for ref, place in ((near_ref, band), (far_ref, 1 - band)):
        for piece in range(half // WIDE):
            lanes = pl.ds(pl.multiple_of(place * half + piece * WIDE, WIDE), WIDE)
            block = ref[side_begin + piece * step : side_begin + (piece + 1) * step, :].astype(F32)
            other_prior_ref[:, lanes] = block[:comp_count]
    span = block_count * count
    own_rows = jnp.concatenate([near_ref[:span, :], far_ref[:span, :]], axis=0).astype(F32)
    other_rows = jnp.concatenate([near_ref[span : 2 * span, :], far_ref[span : 2 * span, :]], axis=0).astype(F32)

    pieces_sum = own_rows[:, :LANES] + other_rows[:, :LANES]
    scalars = []
    for n in range(MOMENTS):
        total = jnp.zeros((1, LANES), F32)
        for i in range(block_count):
            total = total + pieces_sum[i * count + n : i * count + n + 1, :]
        lane = iota((1, LANES), 1)
        keep = (lane >= base + 2) & (lane < base + 5)
        scalars.append(jnp.sum(jnp.where(keep, total, 0.0), axis=1, keepdims=True))

    wanted = own_rows[:, base : base + 1]
    held = jnp.transpose(jnp.broadcast_to(own_rows[:, base + 1 : base + 2], (cycles, cycles)))
    pick = jnp.where(wanted == held, 1.0, 0.0).astype(BF16)
    blocks = jnp.concatenate([near_legendre_ref[...], far_legendre_ref[...]], axis=0)
    legendre_ref[...] = nn_dot(pick, blocks).astype(BF16)

    row = iota((small, cycles), 0)
    lane = iota((small, cycles), 1)
    same_m = row % m_count == lane % m_count
    summed = jnp.transpose((own_rows + other_rows)[:, 2 * LANES :])
    high, low = halves(summed)
    images = nt_dot(jnp.concatenate([high, low], axis=1), jnp.concatenate([pick, pick], axis=1))
    width = 2 * channel_count
    images = jnp.concatenate([images[n * width : (n + 1) * width] for n in range(POWERS)], axis=1)
    high, low = halves(images)
    spread_row = iota((small, width), 0)
    spread_lane = iota((small, width), 1)
    spread = (spread_row // rows == spread_lane % channel_count) & (
        spread_row % rows // m_count == spread_lane // channel_count
    )
    spread = jnp.where(spread, 1.0, 0.0).astype(BF16)
    images = nn_dot(spread, high) + nn_dot(spread, low)
    y = [jnp.where(same_m, images[:, n * cycles : (n + 1) * cycles], 0.0) for n in range(POWERS)]

    own_gram = jnp.transpose(own_rows[:, : 2 * LANES])
    other_gram = jnp.transpose(other_rows[:, : 2 * LANES])
    first_gram = jnp.where(comp == 0, own_gram, other_gram)
    second_gram = jnp.where(comp == 0, other_gram, own_gram)
    grams = []
    for k in range(2):
        gram = jnp.concatenate(
            [first_gram[k * LANES : k * LANES + base], second_gram[k * LANES : k * LANES + base]], axis=0
        )
        grams.append(gram.reshape(channel_count, rows, cycles))
    group = jnp.where(
        iota((2 * cycles, cycles), 0) % cycles // m_count == iota((2 * cycles, cycles), 1) // m_count, 1.0, 0.0
    ).astype(BF16)

    def sky(image):
        image = image.reshape(channel_count, rows, cycles)
        cosine = jnp.sum(image[:, :m_count], axis=1, keepdims=True)
        sine = jnp.sum(image[:, m_count:], axis=1, keepdims=True)
        product = (grams[0] * cosine + grams[1] * sine).reshape(small, cycles)
        high, low = halves(product)
        result = nn_dot(jnp.concatenate([high, low], axis=1), group)
        return jnp.where(same_m, result, 0.0)

    block = near_ref[side_begin : side_begin + step, :].astype(F32)[comp_count:]
    strips = [block[:, i * LANES : i * LANES + comp_count] for i in range(channel_count // (step - comp_count))]
    other = jnp.concatenate(strips, axis=0).astype(BF16)
    own_mixing = own_mixing_ref[...].astype(BF16)
    both = (nt_dot(own_mixing, own_mixing) + nt_dot(other, other)).astype(BF16)
    expand = expander(small, channel_count)
    talls = [nn_dot(expand, both)]
    talls += [nt_dot(expand, own_mixing), nt_dot(expand, other), nn_dot(expand, own_mixing), nn_dot(expand, other)]
    square_matrix, *widened = widen(talls, expand)
    spreads, gathers = widened[:2], widened[2:]
    priors = (own_prior_ref, other_prior_ref)

    def dot(a, b):
        return jnp.sum(jnp.sum(a * b, axis=0, keepdims=True), axis=1, keepdims=True)

    def total(x):
        return jnp.sum(jnp.sum(x, axis=0, keepdims=True), axis=1, keepdims=True)

    def harmonic(z):
        table = legendre_ref[...]
        beam = beam_ref[...][:, None, :]
        value = nn_dot(z.astype(BF16), table).reshape(channel_count, rows, l_count) * beam
        value = value.reshape(small, l_count).astype(BF16)
        return value

    def analyse(values):
        table = legendre_ref[...]
        beam = beam_ref[...][:, None, :]
        shaped = [value.reshape(channel_count, rows, l_count) * beam for value in values]
        images = [nt_dot(value.reshape(small, l_count).astype(BF16), table) for value in shaped]
        return [jnp.where(same_m, image, 0.0) for image in images]

    def first_pass(z):
        value = harmonic(z)
        (plain,) = analyse([nn_dot(square_matrix, value)])
        mixed = jnp.zeros((small, l_count), F32)
        second = jnp.zeros((rows, l_count), F32)
        third = jnp.zeros((rows, l_count), F32)
        for side in range(2):
            prior = priors[side][...][:, None, :]
            once = nn_dot(spreads[side], value).reshape(comp_count, rows, l_count) * prior
            square = once * once
            second = second + jnp.sum(square, axis=0)
            third = third + jnp.sum(square * prior, axis=0)
            once = once.reshape(small, l_count).astype(BF16)
            once_ref[side * small : (side + 1) * small, :] = once
            mixed = mixed + nn_dot(gathers[side], once)
        (primed,) = analyse([mixed])
        return plain, primed, total(second), total(third)

    def second_pass(z):
        value = harmonic(z)
        (plain,) = analyse([nn_dot(square_matrix, value)])
        cross = jnp.zeros((rows, l_count), F32)
        own = jnp.zeros((rows, l_count), F32)
        for side in range(2):
            prior = priors[side][...][:, None, :]
            vector = nn_dot(spreads[side], value).reshape(comp_count, rows, l_count)
            once = once_ref[side * small : (side + 1) * small, :].astype(F32).reshape(comp_count, rows, l_count)
            primed = vector * prior
            cross = cross + jnp.sum(primed * once, axis=0)
            own = own + jnp.sum(vector * primed, axis=0)
        return plain, total(cross), total(own)

    s = scalars
    z0 = sky(y[0])
    y_plain0, y_prime0, pp00, ppp00 = first_pass(z0)
    norm0 = s[0]
    step0 = norm0 / (s[1] + dot(y[0], z0))
    p00, uu00 = dot(z0, y_prime0), dot(z0, y_plain0)
    by0, by1, by2, by3, by4 = [dot(y[n], z0) for n in range(5)]
    norm1 = s[0] - 2.0 * step0 * (s[1] + by0) + step0 * step0 * (s[2] + 2.0 * by1 + uu00)
    ratio0 = norm1 / norm0
    y_r1 = y[0] - step0 * (y[1] + y_plain0)
    y_d1 = y_r1 + ratio0 * y[0]
    e0, e1, e2 = 1.0 + ratio0, -step0, -step0
    z1 = sky(y_d1)
    y_plain1, p2_01, p_11 = second_pass(z1)
    quadratic1 = (
        e0 * e0 * s[1] + 2.0 * e0 * e1 * s[2] + e1 * e1 * s[3]
        + 2.0 * e0 * e2 * by1 + 2.0 * e1 * e2 * by2 + e2 * e2 * p00
    )
    step1 = norm1 / (quadratic1 + dot(y_d1, z1))
    y_pd1 = e0 * y[1] + e1 * y[2] + e2 * y_prime0
    h0, h1, h2 = 1.0 + 0.0 * step1, -step0 - step1 * e0, -step1 * e1
    h3, h4, h5 = -step0, -step1 * e2, -step1
    b1y = [dot(y[n], z1) for n in range(4)]
    uu01, p01, uu11 = dot(z1, y_plain0), dot(z1, y_prime0), dot(z1, y_plain1)
    norm2 = (
        h0 * h0 * s[0] + 2.0 * h0 * h1 * s[1] + (h1 * h1 + 2.0 * h0 * h2) * s[2]
        + 2.0 * h1 * h2 * s[3] + h2 * h2 * s[4]
        + 2.0 * h3 * (h0 * by0 + h1 * by1 + h2 * by2)
        + 2.0 * h4 * (h0 * by1 + h1 * by2 + h2 * by3)
        + 2.0 * h5 * (h0 * b1y[0] + h1 * b1y[1] + h2 * b1y[2])
        + h3 * h3 * uu00 + 2.0 * h3 * h4 * p00 + h4 * h4 * pp00
        + 2.0 * h3 * h5 * uu01 + 2.0 * h4 * h5 * p01 + h5 * h5 * uu11
    )
    ratio1 = norm2 / norm1
    y_d2 = y_r1 - step1 * (y_pd1 + y_plain1) + ratio1 * y_d1
    z2 = sky(y_d2)
    h0, h1, h3 = h0 + ratio1 * e0, h1 + ratio1 * e1, h3 + ratio1 * e2
    quadratic2 = (
        h0 * h0 * s[1] + 2.0 * h0 * h1 * s[2] + (h1 * h1 + 2.0 * h0 * h2) * s[3]
        + 2.0 * h1 * h2 * s[4] + h2 * h2 * s[5]
        + 2.0 * h3 * (h0 * by1 + h1 * by2 + h2 * by3)
        + 2.0 * h4 * (h0 * by2 + h1 * by3 + h2 * by4)
        + 2.0 * h5 * (h0 * b1y[1] + h1 * b1y[2] + h2 * b1y[3])
        + h3 * h3 * p00 + 2.0 * h3 * h4 * pp00 + h4 * h4 * ppp00
        + 2.0 * h3 * h5 * p01 + 2.0 * h4 * h5 * p2_01 + h5 * h5 * p_11
    )
    step2 = norm2 / (quadratic2 + dot(y_d2, z2))

    mine_row = iota((width, small), 0)
    mine_lane = iota((width, small), 1)
    mine = (mine_lane // rows == mine_row % channel_count) & (
        mine_lane % rows == mine_row // channel_count * m_count + owner
    )
    mine = jnp.where(mine, 1.0, 0.0).astype(BF16)
    stacked = jnp.concatenate([z.astype(BF16) for z in (z0, z1, z2)], axis=1)
    stacked = nn_dot(mine, stacked).astype(BF16)
    stacked = jnp.concatenate([stacked[:, i * cycles : (i + 1) * cycles] for i in range(ITERS)], axis=0)
    for copy in arrivals:
        copy.wait()
    value = nn_dot(stacked, legendre_ref[...])
    value = [value[i * channel_count : (i + 1) * channel_count] * beam_ref[...] for i in range(2 * ITERS)]
    value = jnp.concatenate(value, axis=1).astype(BF16)
    vectors = lax.dot_general(own_mixing, value, (((0,), (0,)), ((), ())), preferred_element_type=F32)
    start, chunk = 0, l_count
    if True:
        for part in range(chunk // LANES):
            prior = own_prior_ref[:, start + part * LANES : start + (part + 1) * LANES]
            for k in range(2):
                lanes = slice(start + part * LANES, start + (part + 1) * LANES)
                u = []
                for i in range(ITERS):
                    begin = (2 * i + k) * chunk + part * LANES
                    u.append(vectors[:, begin : begin + LANES])
                b = rhs_ref[k, :, lanes]
                r1 = b - step0 * (prior * b + u[0])
                d1 = r1 + ratio0 * b
                r2 = r1 - step1 * (prior * d1 + u[1])
                d2 = r2 + ratio1 * d1
                solution_ref[k, :, lanes] = step0 * b + step1 * d1 + step2 * d2
                residual_ref[k, :, lanes] = r2 - step2 * (prior * d2 + u[2])
            place, rest = divmod(start + (part + 1) * LANES, l_count // PIECES)
            if rest == 0:
                for pair in departures[2 * (place - 1) : 2 * place]:
                    for copy in pair:
                        copy.start()
    for pair in departures:
        for copy in pair:
            copy.wait()


def swap(x, axis):
    return lax.ppermute(x, axis, [(0, 1), (1, 0)])


def hop(x, distance):
    return lax.ppermute(x, "blk", [(i, i ^ distance) for i in range(lax.axis_size("blk"))])


def compact(
    rhs, legendre, beam, mixing, prior, inv_noise, mask_flags, cycle_len, cycle_slot, m_values
):
    comp_count, parts, m_own, l_count = rhs.shape
    block_count = lax.axis_size("blk")
    m_count = m_values.shape[0]
    channel_width, cycle_count = mask_flags.shape
    channel_count = beam.shape[0]
    count = cycle_count * m_count
    vmem = pl.BlockSpec(memory_space=pltpu.VMEM)
    flat = rhs
    inside = (parts, comp_count, l_count)
    in_sems = pltpu.SemaphoreType.DMA((1, parts))
    out_sems = pltpu.SemaphoreType.DMA((PIECES, parts))
    half = l_count // 2
    side_rows = half // WIDE * SIDE_ROWS
    hbm = pl.BlockSpec(memory_space=pltpu.HBM)
    operands = (
        flat, jnp.transpose(legendre[0]), beam, mixing, prior, inv_noise, jnp.transpose(mask_flags),
        cycle_len, cycle_slot, m_values,
    )
    spaces = [pltpu.VMEM] * 7 + [pltpu.SMEM] * 3
    rows = 2 * m_count
    small = channel_count * rows
    message, side = pl.pallas_call(
        gather_kernel,
        out_shape=[
            pltpu.VMEM((count, WIDE), BF16),
            pltpu.VMEM((side_rows, WIDE), BF16),
        ],
        in_specs=[hbm] * len(operands),
        out_specs=[vmem] * 2,
        scratch_shapes=[pltpu.VMEM(inside, F32)]
        + [space(x.shape, x.dtype) for space, x in zip(spaces[1:], operands[1:])]
        + [
            pltpu.VMEM((count, 2 * LANES), F32),
            pltpu.SemaphoreType.DMA((len(operands),)),
            in_sems,
        ],
        compiler_params=pltpu.CompilerParams(vmem_limit_bytes=40 * 1024 * 1024),
        name="gather_kernel",
    )(*[pltpu.with_memory_space_constraint(x, pltpu.HBM) for x in operands])
    table = operands[1]
    both = jnp.concatenate([message, table], axis=1)

    def turn(x, distance):
        return lax.ppermute(x, "blk", [(i, (i + distance) % block_count) for i in range(block_count)])

    first, second = hop(both, 1), hop(both, 2)
    hops = [first[:, :WIDE], second[:, :WIDE], hop(message, 3)]
    legs = [first[:, WIDE:], second[:, WIDE:], hop(second[:, WIDE:], 1)]
    tables = jnp.concatenate([table] + legs, axis=0)
    far_tables = swap(tables, "lat")
    messages = jnp.concatenate([message] + hops, axis=0)
    other_side = swap(side, "comp")
    crossing = swap(messages, "comp")
    near = jnp.concatenate([messages, crossing, other_side], axis=0)
    far = swap(near, "lat")

    def kernel(*refs):
        iterate_kernel(*refs, channel_width, m_count, block_count, side_rows)

    cycles = 2 * block_count * count
    answers = pl.pallas_call(
        kernel,
        out_shape=[jax.ShapeDtypeStruct(rhs.shape, F32)] * 2,
        in_specs=[vmem] * 7 + [hbm],
        out_specs=[hbm] * 2,
        scratch_shapes=[
            pltpu.VMEM((cycles, l_count), BF16),
            pltpu.VMEM((2 * small, l_count), BF16),
            pltpu.VMEM(prior.shape, F32),
        ]
        + [pltpu.VMEM(inside, F32)] * 3
        + [in_sems, out_sems, out_sems],
        compiler_params=pltpu.CompilerParams(vmem_limit_bytes=48 * 1024 * 1024),
        name="iterate_kernel",
    )(near, far, tables, far_tables, beam, mixing, prior, pltpu.with_memory_space_constraint(flat, pltpu.HBM))
    return tuple(answers)


def cycle_table(m_values, length, pixel_count):
    pixels = jnp.arange(pixel_count, dtype=jnp.int32)
    phase_ids = m_values[:, None] * (2 * pixels[None, :] + 1) % (2 * length)
    angles = math.pi * phase_ids.astype(jnp.float32) / length.astype(jnp.float32)
    inside = (pixels < length)[None, :]
    cosine = jnp.where(inside, jnp.cos(angles), jnp.float32(0.0))
    sine_part = jnp.where(inside, -jnp.sin(angles), jnp.float32(0.0))
    return jnp.stack([cosine, sine_part]).astype(jnp.bfloat16)


def distributed(
    rhs, legendre, beam, mixing, prior, inv_noise, mask_flags, cycle_len, cycle_slot, m_values
):
    cycle_count = inv_noise.shape[1]
    pixel_count = inv_noise.shape[2]
    channel_width = inv_noise.shape[0]
    owner_index = lax.axis_index("blk")
    comp_index = lax.axis_index("comp")
    local_ids = lax.dynamic_slice_in_dim(cycle_slot, owner_index * cycle_count, cycle_count)
    local_lengths = cycle_len[local_ids]
    legendre_slot = legendre[:, :, cycle_slot]
    weights = mask_flags.astype(jnp.float32)
    own_beam = lax.dynamic_slice_in_dim(beam, comp_index * channel_width, channel_width, 0)
    stored = jax.vmap(cycle_table, in_axes=(None, 0, None))(m_values, local_lengths, pixel_count)
    solution = jnp.zeros_like(rhs)
    residual = rhs
    direction = rhs
    for iteration in range(ITERS):
        local_mix = jnp.einsum("fc,ckml->fkml", mixing, direction, precision=HIGHEST_PRECISION)
        summed = lax.psum(local_mix.astype(jnp.bfloat16), "comp").astype(jnp.float32)
        own_part = lax.dynamic_slice_in_dim(summed, comp_index * channel_width, channel_width, 0)
        blended = (own_part * own_beam[:, None, None, :]).astype(jnp.bfloat16)
        coeffs = jnp.einsum(
            "fkml,mlr->fkmr", blended, legendre_slot, preferred_element_type=jnp.float32
        ).astype(jnp.bfloat16)
        arrived = lax.all_to_all(coeffs, "blk", split_axis=3, concat_axis=2, tiled=True)
        sky_map = jnp.einsum("fkmq,qkmp->fqp", arrived, stored, preferred_element_type=jnp.float32)
        weighted = (weights[:, :, None] * inv_noise * sky_map).astype(jnp.bfloat16)
        projected = jnp.einsum(
            "fqp,qkmp->fkmq", weighted, stored, preferred_element_type=jnp.float32
        ).astype(jnp.bfloat16)
        returned = lax.all_to_all(projected, "blk", split_axis=2, concat_axis=3, tiled=True)
        harmonic = jnp.einsum(
            "fkms,mls->fkml", returned, legendre_slot, preferred_element_type=jnp.float32
        )
        everyone = lax.all_gather(
            harmonic.astype(jnp.bfloat16), ("comp", "lat"), axis=0, tiled=True
        ).astype(harmonic.dtype)
        stacked = everyone.reshape(
            (lax.axis_size("comp"), lax.axis_size("lat"), channel_width) + harmonic.shape[1:]
        )
        summed_bands = jnp.sum(stacked, axis=1).reshape((-1,) + harmonic.shape[1:])
        backward = jnp.einsum(
            "fc,fkml->ckml",
            mixing,
            summed_bands * beam[:, None, None, :],
            precision=HIGHEST_PRECISION,
        )
        applied = prior[:, None, None, :] * direction + backward
        totals = lax.psum(
            (
                jnp.sum(direction * applied),
                jnp.sum(residual * applied),
                jnp.sum(applied * applied),
                jnp.sum(residual * residual),
            ),
            ("blk", "comp"),
        )
        curvature, cross_term, square, norm_now = totals
        step_size = norm_now / curvature
        solution = solution + step_size * direction
        residual = residual - step_size * applied
        norm_next = norm_now - 2.0 * step_size * cross_term + step_size * step_size * square
        direction = residual + norm_next / norm_now * direction
    return (solution, residual)


def fits(mesh, rhs, legendre, beam, mixing, inv_noise, m_values):
    sizes = dict(mesh.shape)
    m_count = m_values.shape[0]
    cycles = legendre.shape[2]
    slots = cycles // (sizes["blk"] * sizes["lat"])
    channels = beam.shape[0]
    width = channels // sizes["comp"]
    comps = mixing.shape[1] // sizes["comp"]
    l_count = legendre.shape[1]
    return (
        sizes["comp"] == 2
        and sizes["lat"] == 2
        and m_count == sizes["blk"] == 4
        and 2 * m_count == SUBLANES
        and cycles * m_count == LANES
        and slots * m_count == cycles // sizes["lat"] == 16
        and comps == channels
        and SIDE_ROWS - comps >= SUBLANES
        and (SIDE_ROWS - comps) * (WIDE // LANES) >= channels
        and channels % (SIDE_ROWS - comps) == 0
        and l_count % (2 * WIDE) == 0
        and channels % SUBLANES == 0
        and width * SUBLANES + 5 <= LANES
        and 2 * POWERS * channels <= 2 * LANES
        and l_count % WIDE == 0
        and inv_noise.shape[2] % WIDE == 0
        and rhs.shape[1] == 2
        and MOMENTS <= 16
    )


def solution(mesh):
    in_specs = (
        P(("groups", "comp"), None, "blk", None),
        P("blk", None, "lat"),
        P(),
        P(None, "comp"),
        P("comp", None),
        P("comp", ("blk", "lat"), None),
        P("comp", ("blk", "lat")),
        P("lat"),
        P("lat"),
        P(),
    )
    out_specs = (P(("groups", "comp"), None, "blk", None), P(("groups", "comp"), None, "blk", None))

    def whole(rhs, legendre, beam, mixing, prior, inv_noise, mask_flags, cycle_len, cycle_slot, m_values):
        small = fits(mesh, rhs, legendre, beam, mixing, inv_noise, m_values)
        local = compact if small else distributed
        mapped = jax.shard_map(local, mesh=mesh, in_specs=in_specs, out_specs=out_specs, check_vma=False)
        return mapped(
            rhs, legendre, beam, mixing, prior, inv_noise, mask_flags, cycle_len, cycle_slot, m_values
        )

    return whole
```

```python
import functools
import math

import jax
import jax.numpy as jnp
from jax import lax
from jax.experimental import pallas as pl
from jax.experimental.pallas import tpu as pltpu
from jax.sharding import PartitionSpec as P

ITERS = 3
LANES = 128
SUBLANES = 8
WIDE = 512
SIDE_ROWS = 32
PIECES = 4
MOMENTS = 2 * ITERS
POWERS = 2 * ITERS - 1
HIGHEST_PRECISION = lax.Precision.HIGHEST
F32 = jnp.float32
BF16 = jnp.bfloat16


def nt_dot(a, b):
    return lax.dot_general(a, b, (((1,), (1,)), ((), ())), preferred_element_type=F32)


def nn_dot(a, b):
    return jnp.dot(a, b, preferred_element_type=F32)


def iota(shape, dim):
    return lax.broadcasted_iota(jnp.int32, shape, dim)


def halves(x):
    high = x.astype(BF16)
    return high, (x - high.astype(F32)).astype(BF16)


def plane_copies(outside, inside, sems, inward):
    copies = []
    width = inside.shape[2] // sems.shape[0]
    for piece in range(sems.shape[0]):
        for k in range(inside.shape[0]):
            lanes = pl.ds(piece * width, width)
            pair = (outside.at[:, k, 0, lanes], inside.at[k, :, lanes])
            source, target = pair if inward else pair[::-1]
            copies.append(pltpu.make_async_copy(source, target, sems.at[piece, k]))
    return copies


def half_turn_sine(u):
    square = u * u
    total = jnp.full_like(u, -(math.pi**11) / math.factorial(11))
    for power in (9, 7, 5, 3, 1):
        sign = 1.0 if power % 4 == 1 else -1.0
        total = total * square + sign * math.pi**power / math.factorial(power)
    return total * u


def project(rhs_ref, legendre_ref, beam_ref, mixing_ref, prior_ref):
    comp_count, l_count = prior_ref.shape
    channel_count = beam_ref.shape[0]
    band_cycles = legendre_ref.shape[0]
    mixing = mixing_ref[...].astype(BF16)
    width = 256
    moments = [jnp.zeros((comp_count, 2 * width), F32) for n in range(MOMENTS)]
    used = POWERS * 2 * channel_count
    images = jnp.zeros((band_cycles, 2 * LANES), F32)
    filler = jnp.zeros((2 * LANES - used, width), F32)
    for start in range(0, l_count, width):
        lanes = slice(start, start + width)
        vector = jnp.concatenate([rhs_ref[k, :, lanes] for k in range(2)], axis=1)
        prior = jnp.concatenate([prior_ref[:, lanes]] * 2, axis=1)
        powers = [vector]
        for n in range(1, POWERS):
            powers.append(prior * powers[-1])
        for n in range(MOMENTS):
            moments[n] = moments[n] + powers[n // 2] * powers[n - n // 2]
        beam = beam_ref[:, lanes]
        blended = []
        for power in powers:
            mixed = nn_dot(mixing, power.astype(BF16))
            blended += [mixed[:, :width] * beam, mixed[:, width:] * beam]
        blended = jnp.concatenate(blended + [filler], axis=0).astype(BF16)
        images = images + nt_dot(legendre_ref[:, lanes], blended)
    return images, moments


def gather_kernel(
    rhs_in, legendre_in, beam_in, mixing_in, prior_in, noise_in, mask_in, len_in, slot_in, m_in,
    out_ref, side_ref, slotted_ref,
    rhs_ref, legendre_ref, beam_ref, mixing_ref, prior_ref, noise_ref, mask_ref, len_ref, slot_ref, m_ref,
    gram_ref, sems, rhs_sems,
):
    sources = (slot_in, len_in, m_in, mask_in, mixing_in, prior_in, beam_in, legendre_in, noise_in)
    targets = (slot_ref, len_ref, m_ref, mask_ref, mixing_ref, prior_ref, beam_ref, legendre_ref, noise_ref)
    copies = [pltpu.make_async_copy(a, b, sems.at[i]) for i, (a, b) in enumerate(zip(sources, targets))]
    copies = plane_copies(rhs_in, rhs_ref, rhs_sems, True) + copies
    for copy in copies:
        copy.start()
    channel_width, cycle_count, pixel_count = noise_ref.shape
    comp_count, l_count = prior_ref.shape
    m_count = m_ref.shape[0]
    band_cycles = legendre_ref.shape[0]
    rows = 2 * m_count
    owner = lax.axis_index("blk")
    band = lax.axis_index("lat")
    bands = lax.axis_size("lat")

    for copy in copies[:-1]:
        copy.wait()
    slot_rows = iota((band_cycles, 1), 0)
    slot_column = jnp.zeros((band_cycles, 1), jnp.int32)
    for n in range(band_cycles):
        slot_column = jnp.where(slot_rows == n, slot_ref[n], slot_column)
    order = jnp.where(slot_column == iota((band_cycles, band_cycles), 1), 1.0, 0.0).astype(BF16)
    slotted_ref[...] = nn_dot(order, legendre_ref[...]).astype(BF16)
    images, moments = project(rhs_ref, slotted_ref, beam_ref, mixing_ref, prior_ref)
    count = cycle_count * m_count
    message_rows = iota((count, LANES), 0)
    totals = jnp.zeros((count, LANES), F32)
    for n in range(MOMENTS):
        total = jnp.sum(jnp.sum(moments[n], axis=0, keepdims=True), axis=1, keepdims=True)
        totals = jnp.where(message_rows == n, total, totals)
    copies[-1].wait()

    row_ids = iota((rows, 1), 0)
    m_column = jnp.zeros((rows, 1), F32)
    for i in range(m_count):
        m_column = jnp.where(row_ids % m_count == i, m_ref[i].astype(F32), m_column)
    quarter = jnp.where(row_ids < m_count, 0.0, 0.25).astype(F32)
    chunk = min(WIDE, pixel_count)
    lengths = [len_ref[slot_ref[owner * cycle_count + q]] for q in range(cycle_count)]
    doubles = [jnp.full((rows, 1), (2 * n).astype(F32), F32) for n in lengths]
    inverses = [1.0 / double for double in doubles]
    sums = [jnp.zeros((rows, LANES), F32) for q in range(cycle_count)]
    padding = jnp.zeros((LANES - channel_width * rows, chunk), F32)
    for start in range(0, pixel_count, chunk):
        pixels = iota((rows, chunk), 1) + start
        phases = m_column * (2 * pixels + 1).astype(F32)
        for q in range(cycle_count):
            rest = phases - jnp.floor(phases * inverses[q] + 0.5) * doubles[q]
            turns = rest * inverses[q] + quarter
            turns = turns - jnp.floor(turns + 0.5)
            sine = half_turn_sine(turns)
            table = jnp.where(pixels < lengths[q], 1.0 - 2.0 * sine * sine, 0.0).astype(BF16)
            wide = table.astype(F32)
            weighted = [noise_ref[f, q : q + 1, start : start + chunk] * wide for f in range(channel_width)]
            weighted = jnp.concatenate(weighted + [padding], axis=0).astype(BF16)
            sums[q] = sums[q] + nt_dot(table, weighted)
    spread = jnp.where(iota((channel_width, LANES), 1) // rows == iota((channel_width, LANES), 0), 1.0, 0.0)
    flags = nn_dot(mask_ref[...].astype(F32).astype(BF16), spread.astype(BF16))
    for q in range(cycle_count):
        gram = sums[q] * flags[q : q + 1]
        gram_ref[q * m_count : (q + 1) * m_count, :LANES] = gram[:m_count]
        gram_ref[q * m_count : (q + 1) * m_count, LANES:] = gram[m_count:]

    lanes = iota((count, LANES), 1)
    first = gram_ref[:, :LANES]
    base = channel_width * rows
    for piece in range(3):
        part = totals.astype(BF16).astype(F32)
        first = jnp.where(lanes == base + piece, part, first)
        totals = totals - part
    out_ref[:, :LANES] = first.astype(BF16)
    out_ref[:, LANES : 2 * LANES] = gram_ref[:, LANES:].astype(BF16)
    out_ref[:, 2 * LANES :] = images.astype(BF16)
    half = l_count // 2
    spare = side_ref.shape[0] // (half // WIDE) - comp_count
    for piece in range(half // WIDE):
        lanes = pl.ds(pl.multiple_of(band * half + piece * WIDE, WIDE), WIDE)
        block = [prior_ref[:, lanes]]
        strips = []
        for i in range(WIDE // LANES):
            begin = i * spare
            if piece == 0 and begin < mixing_ref.shape[0]:
                strip = jnp.concatenate(
                    [mixing_ref[begin : begin + spare, :], jnp.zeros((spare, LANES - comp_count), F32)], axis=1
                )
            else:
                strip = jnp.zeros((spare, LANES), F32)
            strips.append(strip)
        block.append(jnp.concatenate(strips, axis=1))
        side_ref[piece * (comp_count + spare) : (piece + 1) * (comp_count + spare), :] = jnp.concatenate(
            block, axis=0
        ).astype(BF16)


def widen(talls, expand):
    small = expand.shape[0]
    rows = small // expand.shape[1]
    wide = nt_dot(jnp.concatenate([tall.astype(BF16) for tall in talls], axis=0), expand)
    same_row = iota((small, small), 0) % rows == iota((small, small), 1) % rows
    return [jnp.where(same_row, wide[i * small : (i + 1) * small], 0.0).astype(BF16) for i in range(len(talls))]


def expander(small, count):
    rows = small // count
    return jnp.where(iota((small, count), 0) // rows == iota((small, count), 1), 1.0, 0.0).astype(BF16)


def iterate_kernel(
    near_ref, far_ref, near_legendre_ref, far_legendre_ref, beam_ref, own_mixing_ref,
    own_prior_ref, rhs_in,
    solution_out, residual_out, legendre_ref, once_ref, other_prior_ref, rhs_ref, solution_ref, residual_ref,
    rhs_sems, solution_sems, residual_sems, channel_width, m_count, block_count, side_rows,
):
    arrivals = plane_copies(rhs_in, rhs_ref, rhs_sems, True)
    for copy in arrivals:
        copy.start()
    departures = plane_copies(solution_out, solution_ref, solution_sems, False)
    departures = list(zip(departures, plane_copies(residual_out, residual_ref, residual_sems, False)))
    comp_count, l_count = own_prior_ref.shape
    channel_count = beam_ref.shape[0]
    rows = 2 * m_count
    count = (near_ref.shape[0] - side_rows) // (block_count * 2)
    cycles = 2 * block_count * count
    small = channel_count * rows
    base = channel_width * rows
    owner = lax.axis_index("blk")
    comp = lax.axis_index("comp")
    band = lax.axis_index("lat")

    half = l_count // 2
    step = side_rows // (half // WIDE)
    side_begin = near_ref.shape[0] - side_rows
    for ref, place in ((near_ref, band), (far_ref, 1 - band)):
        for piece in range(half // WIDE):
            lanes = pl.ds(pl.multiple_of(place * half + piece * WIDE, WIDE), WIDE)
            block = ref[side_begin + piece * step : side_begin + (piece + 1) * step, :].astype(F32)
            other_prior_ref[:, lanes] = block[:comp_count]
    span = block_count * count
    own_rows = jnp.concatenate([near_ref[:span, :], far_ref[:span, :]], axis=0).astype(F32)
    other_rows = jnp.concatenate([near_ref[span : 2 * span, :], far_ref[span : 2 * span, :]], axis=0).astype(F32)

    pieces_sum = own_rows[:, :LANES] + other_rows[:, :LANES]
    scalars = []
    for n in range(MOMENTS):
        total = jnp.zeros((1, LANES), F32)
        for i in range(block_count):
            total = total + pieces_sum[i * count + n : i * count + n + 1, :]
        lane = iota((1, LANES), 1)
        keep = (lane >= base) & (lane < base + 3)
        scalars.append(jnp.sum(jnp.where(keep, total, 0.0), axis=1, keepdims=True))

    legendre_ref[:span, :] = near_legendre_ref[...]
    legendre_ref[span:, :] = far_legendre_ref[...]
    slots = count // m_count
    lane_m = iota((small, cycles), 1) // count % block_count ^ owner
    same_m = iota((small, cycles), 0) % m_count == lane_m
    given = iota((cycles, cycles), 0)
    wanted = iota((cycles, cycles), 1)
    pick = (
        (given // span == wanted // span)
        & (given // m_count % slots == wanted % slots)
        & (given % m_count == (wanted // count % block_count ^ owner))
        & ((given // count % block_count ^ owner) == wanted // slots % block_count)
    )
    pick = jnp.where(pick, 1.0, 0.0).astype(BF16)
    images = jnp.transpose((own_rows + other_rows)[:, 2 * LANES :])
    width = 2 * channel_count
    images = jnp.concatenate([images[n * width : (n + 1) * width] for n in range(POWERS)], axis=1)
    high, low = halves(images)
    spread_row = iota((small, width), 0)
    spread_lane = iota((small, width), 1)
    spread = (spread_row // rows == spread_lane % channel_count) & (
        spread_row % rows // m_count == spread_lane // channel_count
    )
    spread = jnp.where(spread, 1.0, 0.0).astype(BF16)
    images = nn_dot(spread, high) + nn_dot(spread, low)
    y = [jnp.where(same_m, images[:, n * cycles : (n + 1) * cycles], 0.0) for n in range(POWERS)]

    own_gram = nn_dot(jnp.transpose(own_rows[:, : 2 * LANES]).astype(BF16), pick)
    other_gram = nn_dot(jnp.transpose(other_rows[:, : 2 * LANES]).astype(BF16), pick)
    first_gram = jnp.where(comp == 0, own_gram, other_gram)
    second_gram = jnp.where(comp == 0, other_gram, own_gram)
    grams = []
    for k in range(2):
        gram = jnp.concatenate(
            [first_gram[k * LANES : k * LANES + base], second_gram[k * LANES : k * LANES + base]], axis=0
        )
        grams.append(gram.reshape(channel_count, rows, cycles))
    first_lane = iota((2 * cycles, cycles), 0) % cycles
    second_lane = iota((2 * cycles, cycles), 1)
    group = (first_lane // span == second_lane // span) & (first_lane % count == second_lane % count)
    group = jnp.where(group, 1.0, 0.0).astype(BF16)

    def sky(image):
        image = image.reshape(channel_count, rows, cycles)
        cosine = jnp.sum(image[:, :m_count], axis=1, keepdims=True)
        sine = jnp.sum(image[:, m_count:], axis=1, keepdims=True)
        product = (grams[0] * cosine + grams[1] * sine).reshape(small, cycles)
        high, low = halves(product)
        result = nn_dot(jnp.concatenate([high, low], axis=1), group)
        return jnp.where(same_m, result, 0.0)

    block = near_ref[side_begin : side_begin + step, :].astype(F32)[comp_count:]
    strips = [block[:, i * LANES : i * LANES + comp_count] for i in range(channel_count // (step - comp_count))]
    other = jnp.concatenate(strips, axis=0).astype(BF16)
    own_mixing = own_mixing_ref[...].astype(BF16)
    both = (nt_dot(own_mixing, own_mixing) + nt_dot(other, other)).astype(BF16)
    expand = expander(small, channel_count)
    talls = [nn_dot(expand, both)]
    talls += [nt_dot(expand, own_mixing), nt_dot(expand, other), nn_dot(expand, own_mixing), nn_dot(expand, other)]
    square_matrix, *widened = widen(talls, expand)
    spreads, gathers = widened[:2], widened[2:]
    priors = (own_prior_ref, other_prior_ref)

    def dot(a, b):
        return jnp.sum(jnp.sum(a * b, axis=0, keepdims=True), axis=1, keepdims=True)

    def total(x):
        return jnp.sum(jnp.sum(x, axis=0, keepdims=True), axis=1, keepdims=True)

    def harmonic(z):
        table = legendre_ref[...]
        beam = beam_ref[...][:, None, :]
        value = nn_dot(z.astype(BF16), table).reshape(channel_count, rows, l_count) * beam
        value = value.reshape(small, l_count).astype(BF16)
        return value

    def analyse(values):
        table = legendre_ref[...]
        beam = beam_ref[...][:, None, :]
        shaped = [value.reshape(channel_count, rows, l_count) * beam for value in values]
        images = [nt_dot(value.reshape(small, l_count).astype(BF16), table) for value in shaped]
        return [jnp.where(same_m, image, 0.0) for image in images]

    def first_pass(z):
        value = harmonic(z)
        (plain,) = analyse([nn_dot(square_matrix, value)])
        second = jnp.zeros((rows, l_count), F32)
        third = jnp.zeros((rows, l_count), F32)
        for side in range(2):
            prior = priors[side][...][:, None, :]
            once = nn_dot(spreads[side], value).reshape(comp_count, rows, l_count) * prior
            square = once * once
            second = second + jnp.sum(square, axis=0)
            third = third + jnp.sum(square * prior, axis=0)
            once = once.reshape(small, l_count).astype(BF16)
            once_ref[side * small : (side + 1) * small, :] = once
        (primed,) = analyse([nn_dot(jnp.concatenate(gathers, axis=1), once_ref[...])])
        return plain, primed, total(second), total(third)

    def second_pass(z):
        value = harmonic(z)
        (plain,) = analyse([nn_dot(square_matrix, value)])
        cross = jnp.zeros((rows, l_count), F32)
        own = jnp.zeros((rows, l_count), F32)
        for side in range(2):
            prior = priors[side][...][:, None, :]
            vector = nn_dot(spreads[side], value).reshape(comp_count, rows, l_count)
            once = once_ref[side * small : (side + 1) * small, :].astype(F32).reshape(comp_count, rows, l_count)
            primed = vector * prior
            cross = cross + jnp.sum(primed * once, axis=0)
            own = own + jnp.sum(vector * primed, axis=0)
        return plain, total(cross), total(own)

    s = scalars
    z0 = sky(y[0])
    y_plain0, y_prime0, pp00, ppp00 = first_pass(z0)
    norm0 = s[0]
    step0 = norm0 / (s[1] + dot(y[0], z0))
    p00, uu00 = dot(z0, y_prime0), dot(z0, y_plain0)
    by0, by1, by2, by3, by4 = [dot(y[n], z0) for n in range(5)]
    norm1 = s[0] - 2.0 * step0 * (s[1] + by0) + step0 * step0 * (s[2] + 2.0 * by1 + uu00)
    ratio0 = norm1 / norm0
    y_r1 = y[0] - step0 * (y[1] + y_plain0)
    y_d1 = y_r1 + ratio0 * y[0]
    e0, e1, e2 = 1.0 + ratio0, -step0, -step0
    z1 = sky(y_d1)
    y_plain1, p2_01, p_11 = second_pass(z1)
    quadratic1 = (
        e0 * e0 * s[1] + 2.0 * e0 * e1 * s[2] + e1 * e1 * s[3]
        + 2.0 * e0 * e2 * by1 + 2.0 * e1 * e2 * by2 + e2 * e2 * p00
    )
    step1 = norm1 / (quadratic1 + dot(y_d1, z1))
    y_pd1 = e0 * y[1] + e1 * y[2] + e2 * y_prime0
    h0, h1, h2 = 1.0 + 0.0 * step1, -step0 - step1 * e0, -step1 * e1
    h3, h4, h5 = -step0, -step1 * e2, -step1
    b1y = [dot(y[n], z1) for n in range(4)]
    uu01, p01, uu11 = dot(z1, y_plain0), dot(z1, y_prime0), dot(z1, y_plain1)
    norm2 = (
        h0 * h0 * s[0] + 2.0 * h0 * h1 * s[1] + (h1 * h1 + 2.0 * h0 * h2) * s[2]
        + 2.0 * h1 * h2 * s[3] + h2 * h2 * s[4]
        + 2.0 * h3 * (h0 * by0 + h1 * by1 + h2 * by2)
        + 2.0 * h4 * (h0 * by1 + h1 * by2 + h2 * by3)
        + 2.0 * h5 * (h0 * b1y[0] + h1 * b1y[1] + h2 * b1y[2])
        + h3 * h3 * uu00 + 2.0 * h3 * h4 * p00 + h4 * h4 * pp00
        + 2.0 * h3 * h5 * uu01 + 2.0 * h4 * h5 * p01 + h5 * h5 * uu11
    )
    ratio1 = norm2 / norm1
    y_d2 = y_r1 - step1 * (y_pd1 + y_plain1) + ratio1 * y_d1
    z2 = sky(y_d2)
    h0, h1, h3 = h0 + ratio1 * e0, h1 + ratio1 * e1, h3 + ratio1 * e2
    quadratic2 = (
        h0 * h0 * s[1] + 2.0 * h0 * h1 * s[2] + (h1 * h1 + 2.0 * h0 * h2) * s[3]
        + 2.0 * h1 * h2 * s[4] + h2 * h2 * s[5]
        + 2.0 * h3 * (h0 * by1 + h1 * by2 + h2 * by3)
        + 2.0 * h4 * (h0 * by2 + h1 * by3 + h2 * by4)
        + 2.0 * h5 * (h0 * b1y[1] + h1 * b1y[2] + h2 * b1y[3])
        + h3 * h3 * p00 + 2.0 * h3 * h4 * pp00 + h4 * h4 * ppp00
        + 2.0 * h3 * h5 * p01 + 2.0 * h4 * h5 * p2_01 + h5 * h5 * p_11
    )
    step2 = norm2 / (quadratic2 + dot(y_d2, z2))

    mine_row = iota((width, small), 0)
    mine_lane = iota((width, small), 1)
    mine = (mine_lane // rows == mine_row % channel_count) & (
        mine_lane % rows == mine_row // channel_count * m_count + owner
    )
    mine = jnp.where(mine, 1.0, 0.0).astype(BF16)
    stacked = jnp.concatenate([z.astype(BF16) for z in (z0, z1, z2)], axis=1)
    stacked = nn_dot(mine, stacked).astype(BF16)
    stacked = jnp.concatenate([stacked[:, i * cycles : (i + 1) * cycles] for i in range(ITERS)], axis=0)
    for copy in arrivals:
        copy.wait()
    value = nn_dot(stacked, legendre_ref[...])
    value = [value[i * channel_count : (i + 1) * channel_count] * beam_ref[...] for i in range(2 * ITERS)]
    value = jnp.concatenate(value, axis=1).astype(BF16)
    vectors = lax.dot_general(own_mixing, value, (((0,), (0,)), ((), ())), preferred_element_type=F32)
    start, chunk = 0, l_count
    if True:
        for part in range(chunk // LANES):
            prior = own_prior_ref[:, start + part * LANES : start + (part + 1) * LANES]
            for k in range(2):
                lanes = slice(start + part * LANES, start + (part + 1) * LANES)
                u = []
                for i in range(ITERS):
                    begin = (2 * i + k) * chunk + part * LANES
                    u.append(vectors[:, begin : begin + LANES])
                b = rhs_ref[k, :, lanes]
                r1 = b - step0 * (prior * b + u[0])
                d1 = r1 + ratio0 * b
                r2 = r1 - step1 * (prior * d1 + u[1])
                d2 = r2 + ratio1 * d1
                solution_ref[k, :, lanes] = step0 * b + step1 * d1 + step2 * d2
                residual_ref[k, :, lanes] = r2 - step2 * (prior * d2 + u[2])
            place, rest = divmod(start + (part + 1) * LANES, l_count // PIECES)
            if rest == 0:
                for pair in departures[2 * (place - 1) : 2 * place]:
                    for copy in pair:
                        copy.start()
    for pair in departures:
        for copy in pair:
            copy.wait()


def swap(x, axis):
    return lax.ppermute(x, axis, [(0, 1), (1, 0)])


def hop(x, distance):
    return lax.ppermute(x, "blk", [(i, i ^ distance) for i in range(lax.axis_size("blk"))])


def compact(
    rhs, legendre, beam, mixing, prior, inv_noise, mask_flags, cycle_len, cycle_slot, m_values
):
    comp_count, parts, m_own, l_count = rhs.shape
    block_count = lax.axis_size("blk")
    m_count = m_values.shape[0]
    channel_width, cycle_count = mask_flags.shape
    channel_count = beam.shape[0]
    count = cycle_count * m_count
    vmem = pl.BlockSpec(memory_space=pltpu.VMEM)
    flat = rhs
    inside = (parts, comp_count, l_count)
    in_sems = pltpu.SemaphoreType.DMA((1, parts))
    out_sems = pltpu.SemaphoreType.DMA((PIECES, parts))
    half = l_count // 2
    side_rows = half // WIDE * SIDE_ROWS
    hbm = pl.BlockSpec(memory_space=pltpu.HBM)
    operands = (
        flat, jnp.transpose(legendre[0]), beam, mixing, prior, inv_noise, jnp.transpose(mask_flags),
        cycle_len, cycle_slot, m_values,
    )
    spaces = [pltpu.VMEM] * 7 + [pltpu.SMEM] * 3
    rows = 2 * m_count
    small = channel_count * rows
    message, side, table = pl.pallas_call(
        gather_kernel,
        out_shape=[
            pltpu.VMEM((count, WIDE), BF16),
            pltpu.VMEM((side_rows, WIDE), BF16),
            pltpu.VMEM(operands[1].shape, BF16),
        ],
        in_specs=[hbm] * len(operands),
        out_specs=[vmem] * 3,
        scratch_shapes=[pltpu.VMEM(inside, F32)]
        + [space(x.shape, x.dtype) for space, x in zip(spaces[1:], operands[1:])]
        + [
            pltpu.VMEM((count, 2 * LANES), F32),
            pltpu.SemaphoreType.DMA((len(operands),)),
            in_sems,
        ],
        compiler_params=pltpu.CompilerParams(vmem_limit_bytes=40 * 1024 * 1024),
        name="gather_kernel",
    )(*[pltpu.with_memory_space_constraint(x, pltpu.HBM) for x in operands])
    both = jnp.concatenate([message, table], axis=1)

    def turn(x, distance):
        return lax.ppermute(x, "blk", [(i, (i + distance) % block_count) for i in range(block_count)])

    first, second = hop(both, 1), hop(both, 2)
    hops = [first[:, :WIDE], second[:, :WIDE], hop(message, 3)]
    legs = [first[:, WIDE:], second[:, WIDE:], hop(second[:, WIDE:], 1)]
    tables = jnp.concatenate([table] + legs, axis=0)
    middle = tables.shape[0] // 2
    far_tables = jnp.concatenate([swap(tables[:middle], "lat"), swap(tables[middle:], "lat")], axis=0)
    messages = jnp.concatenate([message] + hops, axis=0)
    other_side = swap(side, "comp")
    crossing = swap(messages, "comp")
    near = jnp.concatenate([messages, crossing, other_side], axis=0)
    far = swap(near, "lat")

    def kernel(*refs):
        iterate_kernel(*refs, channel_width, m_count, block_count, side_rows)

    cycles = 2 * block_count * count
    answers = pl.pallas_call(
        kernel,
        out_shape=[jax.ShapeDtypeStruct(rhs.shape, F32)] * 2,
        in_specs=[vmem] * 7 + [hbm],
        out_specs=[hbm] * 2,
        scratch_shapes=[
            pltpu.VMEM((cycles, l_count), BF16),
            pltpu.VMEM((2 * small, l_count), BF16),
            pltpu.VMEM(prior.shape, F32),
        ]
        + [pltpu.VMEM(inside, F32)] * 3
        + [in_sems, out_sems, out_sems],
        compiler_params=pltpu.CompilerParams(vmem_limit_bytes=48 * 1024 * 1024),
        name="iterate_kernel",
    )(near, far, tables, far_tables, beam, mixing, prior, pltpu.with_memory_space_constraint(flat, pltpu.HBM))
    return tuple(answers)


def cycle_table(m_values, length, pixel_count):
    pixels = jnp.arange(pixel_count, dtype=jnp.int32)
    phase_ids = m_values[:, None] * (2 * pixels[None, :] + 1) % (2 * length)
    angles = math.pi * phase_ids.astype(jnp.float32) / length.astype(jnp.float32)
    inside = (pixels < length)[None, :]
    cosine = jnp.where(inside, jnp.cos(angles), jnp.float32(0.0))
    sine_part = jnp.where(inside, -jnp.sin(angles), jnp.float32(0.0))
    return jnp.stack([cosine, sine_part]).astype(jnp.bfloat16)


def distributed(
    rhs, legendre, beam, mixing, prior, inv_noise, mask_flags, cycle_len, cycle_slot, m_values
):
    cycle_count = inv_noise.shape[1]
    pixel_count = inv_noise.shape[2]
    channel_width = inv_noise.shape[0]
    owner_index = lax.axis_index("blk")
    comp_index = lax.axis_index("comp")
    local_ids = lax.dynamic_slice_in_dim(cycle_slot, owner_index * cycle_count, cycle_count)
    local_lengths = cycle_len[local_ids]
    legendre_slot = legendre[:, :, cycle_slot]
    weights = mask_flags.astype(jnp.float32)
    own_beam = lax.dynamic_slice_in_dim(beam, comp_index * channel_width, channel_width, 0)
    stored = jax.vmap(cycle_table, in_axes=(None, 0, None))(m_values, local_lengths, pixel_count)
    solution = jnp.zeros_like(rhs)
    residual = rhs
    direction = rhs
    for iteration in range(ITERS):
        local_mix = jnp.einsum("fc,ckml->fkml", mixing, direction, precision=HIGHEST_PRECISION)
        summed = lax.psum(local_mix.astype(jnp.bfloat16), "comp").astype(jnp.float32)
        own_part = lax.dynamic_slice_in_dim(summed, comp_index * channel_width, channel_width, 0)
        blended = (own_part * own_beam[:, None, None, :]).astype(jnp.bfloat16)
        coeffs = jnp.einsum(
            "fkml,mlr->fkmr", blended, legendre_slot, preferred_element_type=jnp.float32
        ).astype(jnp.bfloat16)
        arrived = lax.all_to_all(coeffs, "blk", split_axis=3, concat_axis=2, tiled=True)
        sky_map = jnp.einsum("fkmq,qkmp->fqp", arrived, stored, preferred_element_type=jnp.float32)
        weighted = (weights[:, :, None] * inv_noise * sky_map).astype(jnp.bfloat16)
        projected = jnp.einsum(
            "fqp,qkmp->fkmq", weighted, stored, preferred_element_type=jnp.float32
        ).astype(jnp.bfloat16)
        returned = lax.all_to_all(projected, "blk", split_axis=2, concat_axis=3, tiled=True)
        harmonic = jnp.einsum(
            "fkms,mls->fkml", returned, legendre_slot, preferred_element_type=jnp.float32
        )
        everyone = lax.all_gather(
            harmonic.astype(jnp.bfloat16), ("comp", "lat"), axis=0, tiled=True
        ).astype(harmonic.dtype)
        stacked = everyone.reshape(
            (lax.axis_size("comp"), lax.axis_size("lat"), channel_width) + harmonic.shape[1:]
        )
        summed_bands = jnp.sum(stacked, axis=1).reshape((-1,) + harmonic.shape[1:])
        backward = jnp.einsum(
            "fc,fkml->ckml",
            mixing,
            summed_bands * beam[:, None, None, :],
            precision=HIGHEST_PRECISION,
        )
        applied = prior[:, None, None, :] * direction + backward
        totals = lax.psum(
            (
                jnp.sum(direction * applied),
                jnp.sum(residual * applied),
                jnp.sum(applied * applied),
                jnp.sum(residual * residual),
            ),
            ("blk", "comp"),
        )
        curvature, cross_term, square, norm_now = totals
        step_size = norm_now / curvature
        solution = solution + step_size * direction
        residual = residual - step_size * applied
        norm_next = norm_now - 2.0 * step_size * cross_term + step_size * step_size * square
        direction = residual + norm_next / norm_now * direction
    return (solution, residual)


def fits(mesh, rhs, legendre, beam, mixing, inv_noise, m_values):
    sizes = dict(mesh.shape)
    m_count = m_values.shape[0]
    cycles = legendre.shape[2]
    slots = cycles // (sizes["blk"] * sizes["lat"])
    channels = beam.shape[0]
    width = channels // sizes["comp"]
    comps = mixing.shape[1] // sizes["comp"]
    l_count = legendre.shape[1]
    return (
        sizes["comp"] == 2
        and sizes["lat"] == 2
        and m_count == sizes["blk"] == 4
        and 2 * m_count == SUBLANES
        and cycles * m_count == LANES
        and slots * m_count == cycles // sizes["lat"] == 16
        and comps == channels
        and SIDE_ROWS - comps >= SUBLANES
        and (SIDE_ROWS - comps) * (WIDE // LANES) >= channels
        and channels % (SIDE_ROWS - comps) == 0
        and l_count % (2 * WIDE) == 0
        and channels % SUBLANES == 0
        and width * SUBLANES + 3 <= LANES
        and 2 * POWERS * channels <= 2 * LANES
        and l_count % WIDE == 0
        and inv_noise.shape[2] % WIDE == 0
        and rhs.shape[1] == 2
        and MOMENTS <= 16
    )


def solution(mesh):
    in_specs = (
        P(("groups", "comp"), None, "blk", None),
        P("blk", None, "lat"),
        P(),
        P(None, "comp"),
        P("comp", None),
        P("comp", ("blk", "lat"), None),
        P("comp", ("blk", "lat")),
        P("lat"),
        P("lat"),
        P(),
    )
    out_specs = (P(("groups", "comp"), None, "blk", None), P(("groups", "comp"), None, "blk", None))

    def whole(rhs, legendre, beam, mixing, prior, inv_noise, mask_flags, cycle_len, cycle_slot, m_values):
        small = fits(mesh, rhs, legendre, beam, mixing, inv_noise, m_values)
        local = compact if small else distributed
        mapped = jax.shard_map(local, mesh=mesh, in_specs=in_specs, out_specs=out_specs, check_vma=False)
        return mapped(
            rhs, legendre, beam, mixing, prior, inv_noise, mask_flags, cycle_len, cycle_slot, m_values
        )

    return whole
```

```python
import functools
import math

import jax
import jax.numpy as jnp
from jax import lax
from jax.experimental import pallas as pl
from jax.experimental.pallas import tpu as pltpu
from jax.sharding import PartitionSpec as P

ITERS = 3
LANES = 128
SUBLANES = 8
WIDE = 512
SIDE_ROWS = 32
PIECES = 4
MOMENTS = 2 * ITERS
POWERS = 2 * ITERS - 1
HIGHEST_PRECISION = lax.Precision.HIGHEST
F32 = jnp.float32
BF16 = jnp.bfloat16


def nt_dot(a, b):
    return lax.dot_general(a, b, (((1,), (1,)), ((), ())), preferred_element_type=F32)


def nn_dot(a, b):
    return jnp.dot(a, b, preferred_element_type=F32)


def iota(shape, dim):
    return lax.broadcasted_iota(jnp.int32, shape, dim)


def halves(x):
    high = x.astype(BF16)
    return high, (x - high.astype(F32)).astype(BF16)


def plane_copies(outside, inside, sems, inward):
    copies = []
    width = inside.shape[2] // sems.shape[0]
    for piece in range(sems.shape[0]):
        for k in range(inside.shape[0]):
            lanes = pl.ds(piece * width, width)
            pair = (outside.at[:, k, 0, lanes], inside.at[k, :, lanes])
            source, target = pair if inward else pair[::-1]
            copies.append(pltpu.make_async_copy(source, target, sems.at[piece, k]))
    return copies


def half_turn_sine(u):
    square = u * u
    total = jnp.full_like(u, -(math.pi**11) / math.factorial(11))
    for power in (9, 7, 5, 3, 1):
        sign = 1.0 if power % 4 == 1 else -1.0
        total = total * square + sign * math.pi**power / math.factorial(power)
    return total * u


def project(rhs_ref, legendre_ref, beam_ref, mixing_ref, prior_ref):
    comp_count, l_count = prior_ref.shape
    channel_count = beam_ref.shape[0]
    band_cycles = legendre_ref.shape[0]
    mixing = mixing_ref[...].astype(BF16)
    width = 256
    moments = [jnp.zeros((comp_count, 2 * width), F32) for n in range(MOMENTS)]
    used = POWERS * 2 * channel_count
    images = jnp.zeros((band_cycles, 2 * LANES), F32)
    filler = jnp.zeros((2 * LANES - used, width), F32)
    for start in range(0, l_count, width):
        lanes = slice(start, start + width)
        vector = jnp.concatenate([rhs_ref[k, :, lanes] for k in range(2)], axis=1)
        prior = jnp.concatenate([prior_ref[:, lanes]] * 2, axis=1)
        powers = [vector]
        for n in range(1, POWERS):
            powers.append(prior * powers[-1])
        for n in range(MOMENTS):
            moments[n] = moments[n] + powers[n // 2] * powers[n - n // 2]
        beam = beam_ref[:, lanes]
        blended = []
        for power in powers:
            mixed = nn_dot(mixing, power.astype(BF16))
            blended += [mixed[:, :width] * beam, mixed[:, width:] * beam]
        blended = jnp.concatenate(blended + [filler], axis=0).astype(BF16)
        images = images + nt_dot(legendre_ref[:, lanes], blended)
    return images, moments


def gather_kernel(
    rhs_in, legendre_in, beam_in, mixing_in, prior_in, noise_in, mask_in, len_in, slot_in, m_in,
    out_ref, side_ref, slotted_ref,
    rhs_ref, legendre_ref, beam_ref, mixing_ref, prior_ref, noise_ref, mask_ref, len_ref, slot_ref, m_ref,
    gram_ref, sems, rhs_sems,
):
    sources = (slot_in, len_in, m_in, mask_in, mixing_in, prior_in, beam_in, legendre_in, noise_in)
    targets = (slot_ref, len_ref, m_ref, mask_ref, mixing_ref, prior_ref, beam_ref, legendre_ref, noise_ref)
    copies = [pltpu.make_async_copy(a, b, sems.at[i]) for i, (a, b) in enumerate(zip(sources, targets))]
    copies = plane_copies(rhs_in, rhs_ref, rhs_sems, True) + copies
    for copy in copies:
        copy.start()
    channel_width, cycle_count, pixel_count = noise_ref.shape
    comp_count, l_count = prior_ref.shape
    m_count = m_ref.shape[0]
    band_cycles = legendre_ref.shape[0]
    rows = 2 * m_count
    owner = lax.axis_index("blk")
    band = lax.axis_index("lat")
    bands = lax.axis_size("lat")

    for copy in copies[:-1]:
        copy.wait()
    slot_rows = iota((band_cycles, 1), 0)
    slot_column = jnp.zeros((band_cycles, 1), jnp.int32)
    for n in range(band_cycles):
        slot_column = jnp.where(slot_rows == n, slot_ref[n], slot_column)
    order = jnp.where(slot_column == iota((band_cycles, band_cycles), 1), 1.0, 0.0).astype(BF16)
    slotted_ref[...] = nn_dot(order, legendre_ref[...]).astype(BF16)
    images, moments = project(rhs_ref, slotted_ref, beam_ref, mixing_ref, prior_ref)
    count = cycle_count * m_count
    message_rows = iota((count, LANES), 0)
    totals = jnp.zeros((count, LANES), F32)
    for n in range(MOMENTS):
        total = jnp.sum(jnp.sum(moments[n], axis=0, keepdims=True), axis=1, keepdims=True)
        totals = jnp.where(message_rows == n, total, totals)
    copies[-1].wait()

    row_ids = iota((rows, 1), 0)
    m_column = jnp.zeros((rows, 1), F32)
    for i in range(m_count):
        m_column = jnp.where(row_ids % m_count == i, m_ref[i].astype(F32), m_column)
    quarter = jnp.where(row_ids < m_count, 0.0, 0.25).astype(F32)
    chunk = min(WIDE, pixel_count)
    lengths = [len_ref[slot_ref[owner * cycle_count + q]] for q in range(cycle_count)]
    doubles = [jnp.full((rows, 1), (2 * n).astype(F32), F32) for n in lengths]
    inverses = [1.0 / double for double in doubles]
    sums = [jnp.zeros((rows, LANES), F32) for q in range(cycle_count)]
    padding = jnp.zeros((LANES - channel_width * rows, chunk), F32)
    for start in range(0, pixel_count, chunk):
        pixels = iota((rows, chunk), 1) + start
        phases = m_column * (2 * pixels + 1).astype(F32)
        for q in range(cycle_count):
            rest = phases - jnp.floor(phases * inverses[q] + 0.5) * doubles[q]
            turns = rest * inverses[q] + quarter
            turns = turns - jnp.floor(turns + 0.5)
            sine = half_turn_sine(turns)
            table = jnp.where(pixels < lengths[q], 1.0 - 2.0 * sine * sine, 0.0).astype(BF16)
            wide = table.astype(F32)
            weighted = [noise_ref[f, q : q + 1, start : start + chunk] * wide for f in range(channel_width)]
            weighted = jnp.concatenate(weighted + [padding], axis=0).astype(BF16)
            sums[q] = sums[q] + nt_dot(table, weighted)
    spread = jnp.where(iota((channel_width, LANES), 1) // rows == iota((channel_width, LANES), 0), 1.0, 0.0)
    flags = nn_dot(mask_ref[...].astype(F32).astype(BF16), spread.astype(BF16))
    for q in range(cycle_count):
        gram = sums[q] * flags[q : q + 1]
        gram_ref[q * m_count : (q + 1) * m_count, :LANES] = gram[:m_count]
        gram_ref[q * m_count : (q + 1) * m_count, LANES:] = gram[m_count:]

    lanes = iota((count, LANES), 1)
    first = gram_ref[:, :LANES]
    base = channel_width * rows
    for piece in range(3):
        part = totals.astype(BF16).astype(F32)
        first = jnp.where(lanes == base + piece, part, first)
        totals = totals - part
    out_ref[:, :LANES] = first.astype(BF16)
    out_ref[:, LANES : 2 * LANES] = gram_ref[:, LANES:].astype(BF16)
    out_ref[:, 2 * LANES :] = images.astype(BF16)
    half = l_count // 2
    spare = side_ref.shape[0] // (half // WIDE) - comp_count
    for piece in range(half // WIDE):
        lanes = pl.ds(pl.multiple_of(band * half + piece * WIDE, WIDE), WIDE)
        block = [prior_ref[:, lanes]]
        strips = []
        for i in range(WIDE // LANES):
            begin = i * spare
            if piece == 0 and begin < mixing_ref.shape[0]:
                strip = jnp.concatenate(
                    [mixing_ref[begin : begin + spare, :], jnp.zeros((spare, LANES - comp_count), F32)], axis=1
                )
            else:
                strip = jnp.zeros((spare, LANES), F32)
            strips.append(strip)
        block.append(jnp.concatenate(strips, axis=1))
        side_ref[piece * (comp_count + spare) : (piece + 1) * (comp_count + spare), :] = jnp.concatenate(
            block, axis=0
        ).astype(BF16)


def widen(talls, expand):
    small = expand.shape[0]
    rows = small // expand.shape[1]
    wide = nt_dot(jnp.concatenate([tall.astype(BF16) for tall in talls], axis=0), expand)
    same_row = iota((small, small), 0) % rows == iota((small, small), 1) % rows
    return [jnp.where(same_row, wide[i * small : (i + 1) * small], 0.0).astype(BF16) for i in range(len(talls))]


def expander(small, count):
    rows = small // count
    return jnp.where(iota((small, count), 0) // rows == iota((small, count), 1), 1.0, 0.0).astype(BF16)


def iterate_kernel(
    near_ref, far_ref, near_side_ref, far_side_ref, near_legendre_ref, far_legendre_ref, beam_ref, own_mixing_ref,
    own_prior_ref, rhs_in,
    solution_out, residual_out, legendre_ref, once_ref, other_prior_ref, rhs_ref, solution_ref, residual_ref,
    rhs_sems, solution_sems, residual_sems, channel_width, m_count, block_count, side_rows,
):
    arrivals = plane_copies(rhs_in, rhs_ref, rhs_sems, True)
    for copy in arrivals:
        copy.start()
    departures = plane_copies(solution_out, solution_ref, solution_sems, False)
    departures = list(zip(departures, plane_copies(residual_out, residual_ref, residual_sems, False)))
    comp_count, l_count = own_prior_ref.shape
    channel_count = beam_ref.shape[0]
    rows = 2 * m_count
    count = near_ref.shape[0] // (block_count * 2)
    cycles = 2 * block_count * count
    small = channel_count * rows
    base = channel_width * rows
    owner = lax.axis_index("blk")
    comp = lax.axis_index("comp")
    band = lax.axis_index("lat")

    half = l_count // 2
    step = side_rows // (half // WIDE)
    for ref, place in ((near_side_ref, band), (far_side_ref, 1 - band)):
        for piece in range(half // WIDE):
            lanes = pl.ds(pl.multiple_of(place * half + piece * WIDE, WIDE), WIDE)
            block = ref[piece * step : (piece + 1) * step, :].astype(F32)
            other_prior_ref[:, lanes] = block[:comp_count]
    span = block_count * count
    own_rows = jnp.concatenate([near_ref[:span, :], far_ref[:span, :]], axis=0).astype(F32)
    other_rows = jnp.concatenate([near_ref[span : 2 * span, :], far_ref[span : 2 * span, :]], axis=0).astype(F32)

    pieces_sum = own_rows[:, :LANES] + other_rows[:, :LANES]
    scalars = []
    for n in range(MOMENTS):
        total = jnp.zeros((1, LANES), F32)
        for i in range(block_count):
            total = total + pieces_sum[i * count + n : i * count + n + 1, :]
        lane = iota((1, LANES), 1)
        keep = (lane >= base) & (lane < base + 3)
        scalars.append(jnp.sum(jnp.where(keep, total, 0.0), axis=1, keepdims=True))

    legendre_ref[:span, :] = near_legendre_ref[...]
    legendre_ref[span:, :] = far_legendre_ref[...]
    slots = count // m_count
    lane_m = iota((small, cycles), 1) // count % block_count ^ owner
    same_m = iota((small, cycles), 0) % m_count == lane_m
    given = iota((cycles, cycles), 0)
    wanted = iota((cycles, cycles), 1)
    pick = (
        (given // span == wanted // span)
        & (given // m_count % slots == wanted % slots)
        & (given % m_count == (wanted // count % block_count ^ owner))
        & ((given // count % block_count ^ owner) == wanted // slots % block_count)
    )
    pick = jnp.where(pick, 1.0, 0.0).astype(BF16)
    images = jnp.transpose((own_rows + other_rows)[:, 2 * LANES :])
    width = 2 * channel_count
    images = jnp.concatenate([images[n * width : (n + 1) * width] for n in range(POWERS)], axis=1)
    high, low = halves(images)
    spread_row = iota((small, width), 0)
    spread_lane = iota((small, width), 1)
    spread = (spread_row // rows == spread_lane % channel_count) & (
        spread_row % rows // m_count == spread_lane // channel_count
    )
    spread = jnp.where(spread, 1.0, 0.0).astype(BF16)
    images = nn_dot(spread, high) + nn_dot(spread, low)
    y = [jnp.where(same_m, images[:, n * cycles : (n + 1) * cycles], 0.0) for n in range(POWERS)]

    own_gram = nn_dot(jnp.transpose(own_rows[:, : 2 * LANES]).astype(BF16), pick)
    other_gram = nn_dot(jnp.transpose(other_rows[:, : 2 * LANES]).astype(BF16), pick)
    first_gram = jnp.where(comp == 0, own_gram, other_gram)
    second_gram = jnp.where(comp == 0, other_gram, own_gram)
    grams = []
    for k in range(2):
        gram = jnp.concatenate(
            [first_gram[k * LANES : k * LANES + base], second_gram[k * LANES : k * LANES + base]], axis=0
        )
        grams.append(gram.reshape(channel_count, rows, cycles))
    first_lane = iota((2 * cycles, cycles), 0) % cycles
    second_lane = iota((2 * cycles, cycles), 1)
    group = (first_lane // span == second_lane // span) & (first_lane % count == second_lane % count)
    group = jnp.where(group, 1.0, 0.0).astype(BF16)

    def sky(image):
        image = image.reshape(channel_count, rows, cycles)
        cosine = jnp.sum(image[:, :m_count], axis=1, keepdims=True)
        sine = jnp.sum(image[:, m_count:], axis=1, keepdims=True)
        product = (grams[0] * cosine + grams[1] * sine).reshape(small, cycles)
        high, low = halves(product)
        result = nn_dot(jnp.concatenate([high, low], axis=1), group)
        return jnp.where(same_m, result, 0.0)

    block = near_side_ref[:step, :].astype(F32)[comp_count:]
    strips = [block[:, i * LANES : i * LANES + comp_count] for i in range(channel_count // (step - comp_count))]
    other = jnp.concatenate(strips, axis=0).astype(BF16)
    own_mixing = own_mixing_ref[...].astype(BF16)
    both = (nt_dot(own_mixing, own_mixing) + nt_dot(other, other)).astype(BF16)
    expand = expander(small, channel_count)
    talls = [nn_dot(expand, both)]
    talls += [nt_dot(expand, own_mixing), nt_dot(expand, other), nn_dot(expand, own_mixing), nn_dot(expand, other)]
    square_matrix, *widened = widen(talls, expand)
    spreads, gathers = widened[:2], widened[2:]
    priors = (own_prior_ref, other_prior_ref)

    def dot(a, b):
        return jnp.sum(jnp.sum(a * b, axis=0, keepdims=True), axis=1, keepdims=True)

    def total(x):
        return jnp.sum(jnp.sum(x, axis=0, keepdims=True), axis=1, keepdims=True)

    def harmonic(z):
        table = legendre_ref[...]
        beam = beam_ref[...][:, None, :]
        value = nn_dot(z.astype(BF16), table).reshape(channel_count, rows, l_count) * beam
        value = value.reshape(small, l_count).astype(BF16)
        return value

    def analyse(values):
        table = legendre_ref[...]
        beam = beam_ref[...][:, None, :]
        shaped = [value.reshape(channel_count, rows, l_count) * beam for value in values]
        images = [nt_dot(value.reshape(small, l_count).astype(BF16), table) for value in shaped]
        return [jnp.where(same_m, image, 0.0) for image in images]

    def first_pass(z):
        value = harmonic(z)
        (plain,) = analyse([nn_dot(square_matrix, value)])
        second = jnp.zeros((rows, l_count), F32)
        third = jnp.zeros((rows, l_count), F32)
        for side in range(2):
            prior = priors[side][...][:, None, :]
            once = nn_dot(spreads[side], value).reshape(comp_count, rows, l_count) * prior
            square = once * once
            second = second + jnp.sum(square, axis=0)
            third = third + jnp.sum(square * prior, axis=0)
            once = once.reshape(small, l_count).astype(BF16)
            once_ref[side * small : (side + 1) * small, :] = once
        (primed,) = analyse([nn_dot(jnp.concatenate(gathers, axis=1), once_ref[...])])
        return plain, primed, total(second), total(third)

    def second_pass(z):
        value = harmonic(z)
        (plain,) = analyse([nn_dot(square_matrix, value)])
        cross = jnp.zeros((rows, l_count), F32)
        own = jnp.zeros((rows, l_count), F32)
        for side in range(2):
            prior = priors[side][...][:, None, :]
            vector = nn_dot(spreads[side], value).reshape(comp_count, rows, l_count)
            once = once_ref[side * small : (side + 1) * small, :].astype(F32).reshape(comp_count, rows, l_count)
            primed = vector * prior
            cross = cross + jnp.sum(primed * once, axis=0)
            own = own + jnp.sum(vector * primed, axis=0)
        return plain, total(cross), total(own)

    s = scalars
    z0 = sky(y[0])
    y_plain0, y_prime0, pp00, ppp00 = first_pass(z0)
    norm0 = s[0]
    step0 = norm0 / (s[1] + dot(y[0], z0))
    p00, uu00 = dot(z0, y_prime0), dot(z0, y_plain0)
    by0, by1, by2, by3, by4 = [dot(y[n], z0) for n in range(5)]
    norm1 = s[0] - 2.0 * step0 * (s[1] + by0) + step0 * step0 * (s[2] + 2.0 * by1 + uu00)
    ratio0 = norm1 / norm0
    y_r1 = y[0] - step0 * (y[1] + y_plain0)
    y_d1 = y_r1 + ratio0 * y[0]
    e0, e1, e2 = 1.0 + ratio0, -step0, -step0
    z1 = sky(y_d1)
    y_plain1, p2_01, p_11 = second_pass(z1)
    quadratic1 = (
        e0 * e0 * s[1] + 2.0 * e0 * e1 * s[2] + e1 * e1 * s[3]
        + 2.0 * e0 * e2 * by1 + 2.0 * e1 * e2 * by2 + e2 * e2 * p00
    )
    step1 = norm1 / (quadratic1 + dot(y_d1, z1))
    y_pd1 = e0 * y[1] + e1 * y[2] + e2 * y_prime0
    h0, h1, h2 = 1.0 + 0.0 * step1, -step0 - step1 * e0, -step1 * e1
    h3, h4, h5 = -step0, -step1 * e2, -step1
    b1y = [dot(y[n], z1) for n in range(4)]
    uu01, p01, uu11 = dot(z1, y_plain0), dot(z1, y_prime0), dot(z1, y_plain1)
    norm2 = (
        h0 * h0 * s[0] + 2.0 * h0 * h1 * s[1] + (h1 * h1 + 2.0 * h0 * h2) * s[2]
        + 2.0 * h1 * h2 * s[3] + h2 * h2 * s[4]
        + 2.0 * h3 * (h0 * by0 + h1 * by1 + h2 * by2)
        + 2.0 * h4 * (h0 * by1 + h1 * by2 + h2 * by3)
        + 2.0 * h5 * (h0 * b1y[0] + h1 * b1y[1] + h2 * b1y[2])
        + h3 * h3 * uu00 + 2.0 * h3 * h4 * p00 + h4 * h4 * pp00
        + 2.0 * h3 * h5 * uu01 + 2.0 * h4 * h5 * p01 + h5 * h5 * uu11
    )
    ratio1 = norm2 / norm1
    y_d2 = y_r1 - step1 * (y_pd1 + y_plain1) + ratio1 * y_d1
    z2 = sky(y_d2)
    h0, h1, h3 = h0 + ratio1 * e0, h1 + ratio1 * e1, h3 + ratio1 * e2
    quadratic2 = (
        h0 * h0 * s[1] + 2.0 * h0 * h1 * s[2] + (h1 * h1 + 2.0 * h0 * h2) * s[3]
        + 2.0 * h1 * h2 * s[4] + h2 * h2 * s[5]
        + 2.0 * h3 * (h0 * by1 + h1 * by2 + h2 * by3)
        + 2.0 * h4 * (h0 * by2 + h1 * by3 + h2 * by4)
        + 2.0 * h5 * (h0 * b1y[1] + h1 * b1y[2] + h2 * b1y[3])
        + h3 * h3 * p00 + 2.0 * h3 * h4 * pp00 + h4 * h4 * ppp00
        + 2.0 * h3 * h5 * p01 + 2.0 * h4 * h5 * p2_01 + h5 * h5 * p_11
    )
    step2 = norm2 / (quadratic2 + dot(y_d2, z2))

    mine_row = iota((width, small), 0)
    mine_lane = iota((width, small), 1)
    mine = (mine_lane // rows == mine_row % channel_count) & (
        mine_lane % rows == mine_row // channel_count * m_count + owner
    )
    mine = jnp.where(mine, 1.0, 0.0).astype(BF16)
    stacked = jnp.concatenate([z.astype(BF16) for z in (z0, z1, z2)], axis=1)
    stacked = nn_dot(mine, stacked).astype(BF16)
    stacked = jnp.concatenate([stacked[:, i * cycles : (i + 1) * cycles] for i in range(ITERS)], axis=0)
    for copy in arrivals:
        copy.wait()
    value = nn_dot(stacked, legendre_ref[...])
    value = [value[i * channel_count : (i + 1) * channel_count] * beam_ref[...] for i in range(2 * ITERS)]
    value = jnp.concatenate(value, axis=1).astype(BF16)
    vectors = lax.dot_general(own_mixing, value, (((0,), (0,)), ((), ())), preferred_element_type=F32)
    start, chunk = 0, l_count
    if True:
        for part in range(chunk // LANES):
            prior = own_prior_ref[:, start + part * LANES : start + (part + 1) * LANES]
            for k in range(2):
                lanes = slice(start + part * LANES, start + (part + 1) * LANES)
                u = []
                for i in range(ITERS):
                    begin = (2 * i + k) * chunk + part * LANES
                    u.append(vectors[:, begin : begin + LANES])
                b = rhs_ref[k, :, lanes]
                r1 = b - step0 * (prior * b + u[0])
                d1 = r1 + ratio0 * b
                r2 = r1 - step1 * (prior * d1 + u[1])
                d2 = r2 + ratio1 * d1
                solution_ref[k, :, lanes] = step0 * b + step1 * d1 + step2 * d2
                residual_ref[k, :, lanes] = r2 - step2 * (prior * d2 + u[2])
            place, rest = divmod(start + (part + 1) * LANES, l_count // PIECES)
            if rest == 0:
                for pair in departures[2 * (place - 1) : 2 * place]:
                    for copy in pair:
                        copy.start()
    for pair in departures:
        for copy in pair:
            copy.wait()


def swap(x, axis):
    return lax.ppermute(x, axis, [(0, 1), (1, 0)])


def hop(x, distance):
    return lax.ppermute(x, "blk", [(i, i ^ distance) for i in range(lax.axis_size("blk"))])


def compact(
    rhs, legendre, beam, mixing, prior, inv_noise, mask_flags, cycle_len, cycle_slot, m_values
):
    comp_count, parts, m_own, l_count = rhs.shape
    block_count = lax.axis_size("blk")
    m_count = m_values.shape[0]
    channel_width, cycle_count = mask_flags.shape
    channel_count = beam.shape[0]
    count = cycle_count * m_count
    vmem = pl.BlockSpec(memory_space=pltpu.VMEM)
    flat = rhs
    inside = (parts, comp_count, l_count)
    in_sems = pltpu.SemaphoreType.DMA((1, parts))
    out_sems = pltpu.SemaphoreType.DMA((PIECES, parts))
    half = l_count // 2
    side_rows = half // WIDE * SIDE_ROWS
    hbm = pl.BlockSpec(memory_space=pltpu.HBM)
    operands = (
        flat, jnp.transpose(legendre[0]), beam, mixing, prior, inv_noise, jnp.transpose(mask_flags),
        cycle_len, cycle_slot, m_values,
    )
    spaces = [pltpu.VMEM] * 7 + [pltpu.SMEM] * 3
    rows = 2 * m_count
    small = channel_count * rows
    message, side, table = pl.pallas_call(
        gather_kernel,
        out_shape=[
            pltpu.VMEM((count, WIDE), BF16),
            pltpu.VMEM((side_rows, WIDE), BF16),
            pltpu.VMEM(operands[1].shape, BF16),
        ],
        in_specs=[hbm] * len(operands),
        out_specs=[vmem] * 3,
        scratch_shapes=[pltpu.VMEM(inside, F32)]
        + [space(x.shape, x.dtype) for space, x in zip(spaces[1:], operands[1:])]
        + [
            pltpu.VMEM((count, 2 * LANES), F32),
            pltpu.SemaphoreType.DMA((len(operands),)),
            in_sems,
        ],
        compiler_params=pltpu.CompilerParams(vmem_limit_bytes=40 * 1024 * 1024),
        name="gather_kernel",
    )(*[pltpu.with_memory_space_constraint(x, pltpu.HBM) for x in operands])
    both = jnp.concatenate([message, table], axis=1)

    def turn(x, distance):
        return lax.ppermute(x, "blk", [(i, (i + distance) % block_count) for i in range(block_count)])

    other_side = swap(side, "comp")
    first, second = hop(both, 1), hop(both, 2)
    hops = [first[:, :WIDE], second[:, :WIDE], hop(message, 3)]
    legs = [first[:, WIDE:], second[:, WIDE:], hop(second[:, WIDE:], 1)]
    tables = jnp.concatenate([table] + legs, axis=0)
    far_tables = swap(tables, "lat")
    messages = jnp.concatenate([message] + hops, axis=0)
    crossing = swap(messages, "comp")
    near = jnp.concatenate([messages, crossing], axis=0)
    far = swap(near, "lat")
    far_side = swap(other_side, "lat")

    def kernel(*refs):
        iterate_kernel(*refs, channel_width, m_count, block_count, side_rows)

    cycles = 2 * block_count * count
    answers = pl.pallas_call(
        kernel,
        out_shape=[jax.ShapeDtypeStruct(rhs.shape, F32)] * 2,
        in_specs=[vmem] * 9 + [hbm],
        out_specs=[hbm] * 2,
        scratch_shapes=[
            pltpu.VMEM((cycles, l_count), BF16),
            pltpu.VMEM((2 * small, l_count), BF16),
            pltpu.VMEM(prior.shape, F32),
        ]
        + [pltpu.VMEM(inside, F32)] * 3
        + [in_sems, out_sems, out_sems],
        compiler_params=pltpu.CompilerParams(vmem_limit_bytes=48 * 1024 * 1024),
        name="iterate_kernel",
    )(near, far, other_side, far_side, tables, far_tables, beam, mixing, prior, pltpu.with_memory_space_constraint(flat, pltpu.HBM))
    return tuple(answers)


def cycle_table(m_values, length, pixel_count):
    pixels = jnp.arange(pixel_count, dtype=jnp.int32)
    phase_ids = m_values[:, None] * (2 * pixels[None, :] + 1) % (2 * length)
    angles = math.pi * phase_ids.astype(jnp.float32) / length.astype(jnp.float32)
    inside = (pixels < length)[None, :]
    cosine = jnp.where(inside, jnp.cos(angles), jnp.float32(0.0))
    sine_part = jnp.where(inside, -jnp.sin(angles), jnp.float32(0.0))
    return jnp.stack([cosine, sine_part]).astype(jnp.bfloat16)


def distributed(
    rhs, legendre, beam, mixing, prior, inv_noise, mask_flags, cycle_len, cycle_slot, m_values
):
    cycle_count = inv_noise.shape[1]
    pixel_count = inv_noise.shape[2]
    channel_width = inv_noise.shape[0]
    owner_index = lax.axis_index("blk")
    comp_index = lax.axis_index("comp")
    local_ids = lax.dynamic_slice_in_dim(cycle_slot, owner_index * cycle_count, cycle_count)
    local_lengths = cycle_len[local_ids]
    legendre_slot = legendre[:, :, cycle_slot]
    weights = mask_flags.astype(jnp.float32)
    own_beam = lax.dynamic_slice_in_dim(beam, comp_index * channel_width, channel_width, 0)
    stored = jax.vmap(cycle_table, in_axes=(None, 0, None))(m_values, local_lengths, pixel_count)
    solution = jnp.zeros_like(rhs)
    residual = rhs
    direction = rhs
    for iteration in range(ITERS):
        local_mix = jnp.einsum("fc,ckml->fkml", mixing, direction, precision=HIGHEST_PRECISION)
        summed = lax.psum(local_mix.astype(jnp.bfloat16), "comp").astype(jnp.float32)
        own_part = lax.dynamic_slice_in_dim(summed, comp_index * channel_width, channel_width, 0)
        blended = (own_part * own_beam[:, None, None, :]).astype(jnp.bfloat16)
        coeffs = jnp.einsum(
            "fkml,mlr->fkmr", blended, legendre_slot, preferred_element_type=jnp.float32
        ).astype(jnp.bfloat16)
        arrived = lax.all_to_all(coeffs, "blk", split_axis=3, concat_axis=2, tiled=True)
        sky_map = jnp.einsum("fkmq,qkmp->fqp", arrived, stored, preferred_element_type=jnp.float32)
        weighted = (weights[:, :, None] * inv_noise * sky_map).astype(jnp.bfloat16)
        projected = jnp.einsum(
            "fqp,qkmp->fkmq", weighted, stored, preferred_element_type=jnp.float32
        ).astype(jnp.bfloat16)
        returned = lax.all_to_all(projected, "blk", split_axis=2, concat_axis=3, tiled=True)
        harmonic = jnp.einsum(
            "fkms,mls->fkml", returned, legendre_slot, preferred_element_type=jnp.float32
        )
        everyone = lax.all_gather(
            harmonic.astype(jnp.bfloat16), ("comp", "lat"), axis=0, tiled=True
        ).astype(harmonic.dtype)
        stacked = everyone.reshape(
            (lax.axis_size("comp"), lax.axis_size("lat"), channel_width) + harmonic.shape[1:]
        )
        summed_bands = jnp.sum(stacked, axis=1).reshape((-1,) + harmonic.shape[1:])
        backward = jnp.einsum(
            "fc,fkml->ckml",
            mixing,
            summed_bands * beam[:, None, None, :],
            precision=HIGHEST_PRECISION,
        )
        applied = prior[:, None, None, :] * direction + backward
        totals = lax.psum(
            (
                jnp.sum(direction * applied),
                jnp.sum(residual * applied),
                jnp.sum(applied * applied),
                jnp.sum(residual * residual),
            ),
            ("blk", "comp"),
        )
        curvature, cross_term, square, norm_now = totals
        step_size = norm_now / curvature
        solution = solution + step_size * direction
        residual = residual - step_size * applied
        norm_next = norm_now - 2.0 * step_size * cross_term + step_size * step_size * square
        direction = residual + norm_next / norm_now * direction
    return (solution, residual)


def fits(mesh, rhs, legendre, beam, mixing, inv_noise, m_values):
    sizes = dict(mesh.shape)
    m_count = m_values.shape[0]
    cycles = legendre.shape[2]
    slots = cycles // (sizes["blk"] * sizes["lat"])
    channels = beam.shape[0]
    width = channels // sizes["comp"]
    comps = mixing.shape[1] // sizes["comp"]
    l_count = legendre.shape[1]
    return (
        sizes["comp"] == 2
        and sizes["lat"] == 2
        and m_count == sizes["blk"] == 4
        and 2 * m_count == SUBLANES
        and cycles * m_count == LANES
        and slots * m_count == cycles // sizes["lat"] == 16
        and comps == channels
        and SIDE_ROWS - comps >= SUBLANES
        and (SIDE_ROWS - comps) * (WIDE // LANES) >= channels
        and channels % (SIDE_ROWS - comps) == 0
        and l_count % (2 * WIDE) == 0
        and channels % SUBLANES == 0
        and width * SUBLANES + 3 <= LANES
        and 2 * POWERS * channels <= 2 * LANES
        and l_count % WIDE == 0
        and inv_noise.shape[2] % WIDE == 0
        and rhs.shape[1] == 2
        and MOMENTS <= 16
    )


def solution(mesh):
    in_specs = (
        P(("groups", "comp"), None, "blk", None),
        P("blk", None, "lat"),
        P(),
        P(None, "comp"),
        P("comp", None),
        P("comp", ("blk", "lat"), None),
        P("comp", ("blk", "lat")),
        P("lat"),
        P("lat"),
        P(),
    )
    out_specs = (P(("groups", "comp"), None, "blk", None), P(("groups", "comp"), None, "blk", None))

    def whole(rhs, legendre, beam, mixing, prior, inv_noise, mask_flags, cycle_len, cycle_slot, m_values):
        small = fits(mesh, rhs, legendre, beam, mixing, inv_noise, m_values)
        local = compact if small else distributed
        mapped = jax.shard_map(local, mesh=mesh, in_specs=in_specs, out_specs=out_specs, check_vma=False)
        return mapped(
            rhs, legendre, beam, mixing, prior, inv_noise, mask_flags, cycle_len, cycle_slot, m_values
        )

    return whole
```

```python
import functools
import math

import jax
import jax.numpy as jnp
from jax import lax
from jax.experimental import pallas as pl
from jax.experimental.pallas import tpu as pltpu
from jax.sharding import PartitionSpec as P

ITERS = 3
LANES = 128
SUBLANES = 8
WIDE = 512
SIDE_ROWS = 32
PIECES = 4
MOMENTS = 2 * ITERS
POWERS = 2 * ITERS - 1
HIGHEST_PRECISION = lax.Precision.HIGHEST
F32 = jnp.float32
BF16 = jnp.bfloat16


def nt_dot(a, b):
    return lax.dot_general(a, b, (((1,), (1,)), ((), ())), preferred_element_type=F32)


def nn_dot(a, b):
    return jnp.dot(a, b, preferred_element_type=F32)


def iota(shape, dim):
    return lax.broadcasted_iota(jnp.int32, shape, dim)


def halves(x):
    high = x.astype(BF16)
    return high, (x - high.astype(F32)).astype(BF16)


def plane_copies(outside, inside, sems, inward):
    copies = []
    width = inside.shape[2] // sems.shape[0]
    for piece in range(sems.shape[0]):
        for k in range(inside.shape[0]):
            lanes = pl.ds(piece * width, width)
            pair = (outside.at[:, k, 0, lanes], inside.at[k, :, lanes])
            source, target = pair if inward else pair[::-1]
            copies.append(pltpu.make_async_copy(source, target, sems.at[piece, k]))
    return copies


def half_turn_sine(u):
    square = u * u
    total = jnp.full_like(u, -(math.pi**11) / math.factorial(11))
    for power in (9, 7, 5, 3, 1):
        sign = 1.0 if power % 4 == 1 else -1.0
        total = total * square + sign * math.pi**power / math.factorial(power)
    return total * u


def project(rhs_ref, legendre_ref, beam_ref, mixing_ref, prior_ref):
    comp_count, l_count = prior_ref.shape
    channel_count = beam_ref.shape[0]
    band_cycles = legendre_ref.shape[0]
    mixing = mixing_ref[...].astype(BF16)
    width = 256
    moments = [jnp.zeros((comp_count, 2 * width), F32) for n in range(MOMENTS)]
    used = POWERS * 2 * channel_count
    images = jnp.zeros((band_cycles, 2 * LANES), F32)
    filler = jnp.zeros((2 * LANES - used, width), F32)
    for start in range(0, l_count, width):
        lanes = slice(start, start + width)
        vector = jnp.concatenate([rhs_ref[k, :, lanes] for k in range(2)], axis=1)
        prior = jnp.concatenate([prior_ref[:, lanes]] * 2, axis=1)
        powers = [vector]
        for n in range(1, POWERS):
            powers.append(prior * powers[-1])
        for n in range(MOMENTS):
            moments[n] = moments[n] + powers[n // 2] * powers[n - n // 2]
        beam = beam_ref[:, lanes]
        blended = []
        for power in powers:
            mixed = nn_dot(mixing, power.astype(BF16))
            blended += [mixed[:, :width] * beam, mixed[:, width:] * beam]
        blended = jnp.concatenate(blended + [filler], axis=0).astype(BF16)
        images = images + nt_dot(legendre_ref[:, lanes], blended)
    return images, moments


def gather_kernel(
    rhs_in, legendre_in, beam_in, mixing_in, prior_in, noise_in, mask_in, len_in, slot_in, m_in,
    out_ref, side_ref, slotted_ref,
    rhs_ref, legendre_ref, beam_ref, mixing_ref, prior_ref, noise_ref, mask_ref, len_ref, slot_ref, m_ref,
    gram_ref, sems, rhs_sems,
):
    sources = (slot_in, len_in, m_in, mask_in, mixing_in, prior_in, beam_in, legendre_in, noise_in)
    targets = (slot_ref, len_ref, m_ref, mask_ref, mixing_ref, prior_ref, beam_ref, legendre_ref, noise_ref)
    copies = [pltpu.make_async_copy(a, b, sems.at[i]) for i, (a, b) in enumerate(zip(sources, targets))]
    copies = plane_copies(rhs_in, rhs_ref, rhs_sems, True) + copies
    for copy in copies:
        copy.start()
    channel_width, cycle_count, pixel_count = noise_ref.shape
    comp_count, l_count = prior_ref.shape
    m_count = m_ref.shape[0]
    band_cycles = legendre_ref.shape[0]
    rows = 2 * m_count
    owner = lax.axis_index("blk")
    band = lax.axis_index("lat")
    bands = lax.axis_size("lat")

    for copy in copies[:-1]:
        copy.wait()
    slot_rows = iota((band_cycles, 1), 0)
    slot_column = jnp.zeros((band_cycles, 1), jnp.int32)
    for n in range(band_cycles):
        slot_column = jnp.where(slot_rows == n, slot_ref[n], slot_column)
    order = jnp.where(slot_column == iota((band_cycles, band_cycles), 1), 1.0, 0.0).astype(BF16)
    slotted_ref[...] = nn_dot(order, legendre_ref[...]).astype(BF16)
    images, moments = project(rhs_ref, slotted_ref, beam_ref, mixing_ref, prior_ref)
    count = cycle_count * m_count
    message_rows = iota((count, LANES), 0)
    totals = jnp.zeros((count, LANES), F32)
    for n in range(MOMENTS):
        total = jnp.sum(jnp.sum(moments[n], axis=0, keepdims=True), axis=1, keepdims=True)
        totals = jnp.where(message_rows == n, total, totals)
    copies[-1].wait()

    row_ids = iota((rows, 1), 0)
    m_column = jnp.zeros((rows, 1), F32)
    for i in range(m_count):
        m_column = jnp.where(row_ids % m_count == i, m_ref[i].astype(F32), m_column)
    quarter = jnp.where(row_ids < m_count, 0.0, 0.25).astype(F32)
    chunk = min(WIDE, pixel_count)
    lengths = [len_ref[slot_ref[owner * cycle_count + q]] for q in range(cycle_count)]
    doubles = [jnp.full((rows, 1), (2 * n).astype(F32), F32) for n in lengths]
    inverses = [1.0 / double for double in doubles]
    sums = [jnp.zeros((rows, LANES), F32) for q in range(cycle_count)]
    padding = jnp.zeros((LANES - channel_width * rows, chunk), F32)
    for start in range(0, pixel_count, chunk):
        pixels = iota((rows, chunk), 1) + start
        phases = m_column * (2 * pixels + 1).astype(F32)
        for q in range(cycle_count):
            rest = phases - jnp.floor(phases * inverses[q] + 0.5) * doubles[q]
            turns = rest * inverses[q] + quarter
            turns = turns - jnp.floor(turns + 0.5)
            sine = half_turn_sine(turns)
            table = jnp.where(pixels < lengths[q], 1.0 - 2.0 * sine * sine, 0.0).astype(BF16)
            wide = table.astype(F32)
            weighted = [noise_ref[f, q : q + 1, start : start + chunk] * wide for f in range(channel_width)]
            weighted = jnp.concatenate(weighted + [padding], axis=0).astype(BF16)
            sums[q] = sums[q] + nt_dot(table, weighted)
    spread = jnp.where(iota((channel_width, LANES), 1) // rows == iota((channel_width, LANES), 0), 1.0, 0.0)
    flags = nn_dot(mask_ref[...].astype(F32).astype(BF16), spread.astype(BF16))
    for q in range(cycle_count):
        gram = sums[q] * flags[q : q + 1]
        gram_ref[q * m_count : (q + 1) * m_count, :LANES] = gram[:m_count]
        gram_ref[q * m_count : (q + 1) * m_count, LANES:] = gram[m_count:]

    lanes = iota((count, LANES), 1)
    first = gram_ref[:, :LANES]
    base = channel_width * rows
    for piece in range(3):
        part = totals.astype(BF16).astype(F32)
        first = jnp.where(lanes == base + piece, part, first)
        totals = totals - part
    out_ref[:, :LANES] = first.astype(BF16)
    out_ref[:, LANES : 2 * LANES] = gram_ref[:, LANES:].astype(BF16)
    out_ref[:, 2 * LANES :] = images.astype(BF16)
    half = l_count // 2
    spare = side_ref.shape[0] // (half // WIDE) - comp_count
    for piece in range(half // WIDE):
        lanes = pl.ds(pl.multiple_of(band * half + piece * WIDE, WIDE), WIDE)
        block = [prior_ref[:, lanes]]
        strips = []
        for i in range(WIDE // LANES):
            begin = i * spare
            if piece == 0 and begin < mixing_ref.shape[0]:
                strip = jnp.concatenate(
                    [mixing_ref[begin : begin + spare, :], jnp.zeros((spare, LANES - comp_count), F32)], axis=1
                )
            else:
                strip = jnp.zeros((spare, LANES), F32)
            strips.append(strip)
        block.append(jnp.concatenate(strips, axis=1))
        side_ref[piece * (comp_count + spare) : (piece + 1) * (comp_count + spare), :] = jnp.concatenate(
            block, axis=0
        ).astype(BF16)


def widen(talls, expand):
    small = expand.shape[0]
    rows = small // expand.shape[1]
    wide = nt_dot(jnp.concatenate([tall.astype(BF16) for tall in talls], axis=0), expand)
    same_row = iota((small, small), 0) % rows == iota((small, small), 1) % rows
    return [jnp.where(same_row, wide[i * small : (i + 1) * small], 0.0).astype(BF16) for i in range(len(talls))]


def expander(small, count):
    rows = small // count
    return jnp.where(iota((small, count), 0) // rows == iota((small, count), 1), 1.0, 0.0).astype(BF16)


def iterate_kernel(
    near_ref, far_ref, near_side_ref, far_side_ref, near_legendre_ref, far_legendre_ref, beam_ref, own_mixing_ref,
    own_prior_ref, rhs_in,
    solution_out, residual_out, legendre_ref, once_ref, other_prior_ref, rhs_ref, solution_ref, residual_ref,
    rhs_sems, solution_sems, residual_sems, channel_width, m_count, block_count, side_rows,
):
    arrivals = plane_copies(rhs_in, rhs_ref, rhs_sems, True)
    for copy in arrivals:
        copy.start()
    departures = plane_copies(solution_out, solution_ref, solution_sems, False)
    departures = list(zip(departures, plane_copies(residual_out, residual_ref, residual_sems, False)))
    comp_count, l_count = own_prior_ref.shape
    channel_count = beam_ref.shape[0]
    rows = 2 * m_count
    count = near_ref.shape[0] // (block_count * 2)
    cycles = 2 * block_count * count
    small = channel_count * rows
    base = channel_width * rows
    owner = lax.axis_index("blk")
    comp = lax.axis_index("comp")
    band = lax.axis_index("lat")

    half = l_count // 2
    step = side_rows // (half // WIDE)
    for ref, place in ((near_side_ref, band), (far_side_ref, 1 - band)):
        for piece in range(half // WIDE):
            lanes = pl.ds(pl.multiple_of(place * half + piece * WIDE, WIDE), WIDE)
            block = ref[piece * step : (piece + 1) * step, :].astype(F32)
            other_prior_ref[:, lanes] = block[:comp_count]
    span = block_count * count
    own_rows = jnp.concatenate([near_ref[:span, :], far_ref[:span, :]], axis=0).astype(F32)
    other_rows = jnp.concatenate([near_ref[span : 2 * span, :], far_ref[span : 2 * span, :]], axis=0).astype(F32)

    pieces_sum = own_rows[:, :LANES] + other_rows[:, :LANES]
    scalars = []
    for n in range(MOMENTS):
        total = jnp.zeros((1, LANES), F32)
        for i in range(block_count):
            total = total + pieces_sum[i * count + n : i * count + n + 1, :]
        lane = iota((1, LANES), 1)
        keep = (lane >= base) & (lane < base + 3)
        scalars.append(jnp.sum(jnp.where(keep, total, 0.0), axis=1, keepdims=True))

    legendre_ref[:span, :] = near_legendre_ref[...]
    legendre_ref[span:, :] = far_legendre_ref[...]
    part = lax.axis_index("groups")

    def block_of(lanes):
        place = lanes // count % block_count
        return jnp.where(place >= 2, place ^ 1 ^ part, place) ^ owner

    slots = count // m_count
    lane_m = block_of(iota((small, cycles), 1))
    same_m = iota((small, cycles), 0) % m_count == lane_m
    given = iota((cycles, cycles), 0)
    wanted = iota((cycles, cycles), 1)
    pick = (
        (given // span == wanted // span)
        & (given // m_count % slots == wanted % slots)
        & (given % m_count == block_of(wanted))
        & (block_of(given) == wanted // slots % block_count)
    )
    pick = jnp.where(pick, 1.0, 0.0).astype(BF16)
    images = jnp.transpose((own_rows + other_rows)[:, 2 * LANES :])
    width = 2 * channel_count
    images = jnp.concatenate([images[n * width : (n + 1) * width] for n in range(POWERS)], axis=1)
    high, low = halves(images)
    spread_row = iota((small, width), 0)
    spread_lane = iota((small, width), 1)
    spread = (spread_row // rows == spread_lane % channel_count) & (
        spread_row % rows // m_count == spread_lane // channel_count
    )
    spread = jnp.where(spread, 1.0, 0.0).astype(BF16)
    images = nn_dot(jnp.concatenate([spread, spread], axis=1), jnp.concatenate([high, low], axis=0))
    y = [jnp.where(same_m, images[:, n * cycles : (n + 1) * cycles], 0.0) for n in range(POWERS)]

    own_gram = nn_dot(jnp.transpose(own_rows[:, : 2 * LANES]).astype(BF16), pick)
    other_gram = nn_dot(jnp.transpose(other_rows[:, : 2 * LANES]).astype(BF16), pick)
    first_gram = jnp.where(comp == 0, own_gram, other_gram)
    second_gram = jnp.where(comp == 0, other_gram, own_gram)
    grams = []
    for k in range(2):
        gram = jnp.concatenate(
            [first_gram[k * LANES : k * LANES + base], second_gram[k * LANES : k * LANES + base]], axis=0
        )
        grams.append(gram.reshape(channel_count, rows, cycles))
    first_lane = iota((2 * cycles, cycles), 0) % cycles
    second_lane = iota((2 * cycles, cycles), 1)
    group = (first_lane // span == second_lane // span) & (first_lane % count == second_lane % count)
    group = jnp.where(group, 1.0, 0.0).astype(BF16)

    def sky(image):
        image = image.reshape(channel_count, rows, cycles)
        cosine = jnp.sum(image[:, :m_count], axis=1, keepdims=True)
        sine = jnp.sum(image[:, m_count:], axis=1, keepdims=True)
        product = (grams[0] * cosine + grams[1] * sine).reshape(small, cycles)
        high, low = halves(product)
        result = nn_dot(jnp.concatenate([high, low], axis=1), group)
        return jnp.where(same_m, result, 0.0)

    block = near_side_ref[:step, :].astype(F32)[comp_count:]
    strips = [block[:, i * LANES : i * LANES + comp_count] for i in range(channel_count // (step - comp_count))]
    other = jnp.concatenate(strips, axis=0).astype(BF16)
    own_mixing = own_mixing_ref[...].astype(BF16)
    both = (nt_dot(own_mixing, own_mixing) + nt_dot(other, other)).astype(BF16)
    expand = expander(small, channel_count)
    def repeat(x):
        x = x.astype(F32)
        return jnp.broadcast_to(x[:, None, :], (channel_count, rows, x.shape[1])).reshape(small, x.shape[1])

    talls = [repeat(both), nt_dot(expand, own_mixing), nt_dot(expand, other), repeat(own_mixing), repeat(other)]
    square_matrix, *widened = widen(talls, expand)
    spreads, gathers = widened[:2], widened[2:]
    priors = (own_prior_ref, other_prior_ref)

    def dot(a, b):
        return jnp.sum(jnp.sum(a * b, axis=0, keepdims=True), axis=1, keepdims=True)

    def total(x):
        return jnp.sum(jnp.sum(x, axis=0, keepdims=True), axis=1, keepdims=True)

    def harmonic(z):
        table = legendre_ref[...]
        beam = beam_ref[...][:, None, :]
        value = nn_dot(z.astype(BF16), table).reshape(channel_count, rows, l_count) * beam
        value = value.reshape(small, l_count).astype(BF16)
        return value

    def analyse(values):
        table = legendre_ref[...]
        beam = beam_ref[...][:, None, :]
        shaped = [value.reshape(channel_count, rows, l_count) * beam for value in values]
        images = [nt_dot(value.reshape(small, l_count).astype(BF16), table) for value in shaped]
        return [jnp.where(same_m, image, 0.0) for image in images]

    def first_pass(z):
        value = harmonic(z)
        (plain,) = analyse([nn_dot(square_matrix, value)])
        second = jnp.zeros((rows, l_count), F32)
        third = jnp.zeros((rows, l_count), F32)
        for side in range(2):
            prior = priors[side][...][:, None, :]
            once = nn_dot(spreads[side], value).reshape(comp_count, rows, l_count) * prior
            square = once * once
            second = second + jnp.sum(square, axis=0)
            third = third + jnp.sum(square * prior, axis=0)
            once = once.reshape(small, l_count).astype(BF16)
            once_ref[side * small : (side + 1) * small, :] = once
        (primed,) = analyse([nn_dot(jnp.concatenate(gathers, axis=1), once_ref[...])])
        return plain, primed, total(second), total(third)

    def second_pass(z):
        value = harmonic(z)
        (plain,) = analyse([nn_dot(square_matrix, value)])
        cross = jnp.zeros((rows, l_count), F32)
        own = jnp.zeros((rows, l_count), F32)
        for side in range(2):
            prior = priors[side][...][:, None, :]
            vector = nn_dot(spreads[side], value).reshape(comp_count, rows, l_count)
            once = once_ref[side * small : (side + 1) * small, :].astype(F32).reshape(comp_count, rows, l_count)
            primed = vector * prior
            cross = cross + jnp.sum(primed * once, axis=0)
            own = own + jnp.sum(vector * primed, axis=0)
        return plain, total(cross), total(own)

    s = scalars
    z0 = sky(y[0])
    y_plain0, y_prime0, pp00, ppp00 = first_pass(z0)
    norm0 = s[0]
    step0 = norm0 / (s[1] + dot(y[0], z0))
    p00, uu00 = dot(z0, y_prime0), dot(z0, y_plain0)
    by0, by1, by2, by3, by4 = [dot(y[n], z0) for n in range(5)]
    norm1 = s[0] - 2.0 * step0 * (s[1] + by0) + step0 * step0 * (s[2] + 2.0 * by1 + uu00)
    ratio0 = norm1 / norm0
    y_r1 = y[0] - step0 * (y[1] + y_plain0)
    y_d1 = y_r1 + ratio0 * y[0]
    e0, e1, e2 = 1.0 + ratio0, -step0, -step0
    z1 = sky(y_d1)
    y_plain1, p2_01, p_11 = second_pass(z1)
    quadratic1 = (
        e0 * e0 * s[1] + 2.0 * e0 * e1 * s[2] + e1 * e1 * s[3]
        + 2.0 * e0 * e2 * by1 + 2.0 * e1 * e2 * by2 + e2 * e2 * p00
    )
    step1 = norm1 / (quadratic1 + dot(y_d1, z1))
    y_pd1 = e0 * y[1] + e1 * y[2] + e2 * y_prime0
    h0, h1, h2 = 1.0 + 0.0 * step1, -step0 - step1 * e0, -step1 * e1
    h3, h4, h5 = -step0, -step1 * e2, -step1
    b1y = [dot(y[n], z1) for n in range(4)]
    uu01, p01, uu11 = dot(z1, y_plain0), dot(z1, y_prime0), dot(z1, y_plain1)
    norm2 = (
        h0 * h0 * s[0] + 2.0 * h0 * h1 * s[1] + (h1 * h1 + 2.0 * h0 * h2) * s[2]
        + 2.0 * h1 * h2 * s[3] + h2 * h2 * s[4]
        + 2.0 * h3 * (h0 * by0 + h1 * by1 + h2 * by2)
        + 2.0 * h4 * (h0 * by1 + h1 * by2 + h2 * by3)
        + 2.0 * h5 * (h0 * b1y[0] + h1 * b1y[1] + h2 * b1y[2])
        + h3 * h3 * uu00 + 2.0 * h3 * h4 * p00 + h4 * h4 * pp00
        + 2.0 * h3 * h5 * uu01 + 2.0 * h4 * h5 * p01 + h5 * h5 * uu11
    )
    ratio1 = norm2 / norm1
    y_d2 = y_r1 - step1 * (y_pd1 + y_plain1) + ratio1 * y_d1
    z2 = sky(y_d2)
    h0, h1, h3 = h0 + ratio1 * e0, h1 + ratio1 * e1, h3 + ratio1 * e2
    quadratic2 = (
        h0 * h0 * s[1] + 2.0 * h0 * h1 * s[2] + (h1 * h1 + 2.0 * h0 * h2) * s[3]
        + 2.0 * h1 * h2 * s[4] + h2 * h2 * s[5]
        + 2.0 * h3 * (h0 * by1 + h1 * by2 + h2 * by3)
        + 2.0 * h4 * (h0 * by2 + h1 * by3 + h2 * by4)
        + 2.0 * h5 * (h0 * b1y[1] + h1 * b1y[2] + h2 * b1y[3])
        + h3 * h3 * p00 + 2.0 * h3 * h4 * pp00 + h4 * h4 * ppp00
        + 2.0 * h3 * h5 * p01 + 2.0 * h4 * h5 * p2_01 + h5 * h5 * p_11
    )
    step2 = norm2 / (quadratic2 + dot(y_d2, z2))

    mine_row = iota((width, small), 0)
    mine_lane = iota((width, small), 1)
    mine = (mine_lane // rows == mine_row % channel_count) & (
        mine_lane % rows == mine_row // channel_count * m_count + owner
    )
    mine = jnp.where(mine, 1.0, 0.0).astype(BF16)
    stacked = jnp.concatenate([z.astype(BF16) for z in (z0, z1, z2)], axis=1)
    stacked = nn_dot(mine, stacked).astype(BF16)
    stacked = jnp.concatenate([stacked[:, i * cycles : (i + 1) * cycles] for i in range(ITERS)], axis=0)
    for copy in arrivals:
        copy.wait()
    value = nn_dot(stacked, legendre_ref[...])
    value = [value[i * channel_count : (i + 1) * channel_count] * beam_ref[...] for i in range(2 * ITERS)]
    value = jnp.concatenate(value, axis=1).astype(BF16)
    vectors = lax.dot_general(own_mixing, value, (((0,), (0,)), ((), ())), preferred_element_type=F32)
    start, chunk = 0, l_count
    if True:
        for part in range(chunk // LANES):
            prior = own_prior_ref[:, start + part * LANES : start + (part + 1) * LANES]
            for k in range(2):
                lanes = slice(start + part * LANES, start + (part + 1) * LANES)
                u = []
                for i in range(ITERS):
                    begin = (2 * i + k) * chunk + part * LANES
                    u.append(vectors[:, begin : begin + LANES])
                b = rhs_ref[k, :, lanes]
                r1 = b - step0 * (prior * b + u[0])
                d1 = r1 + ratio0 * b
                r2 = r1 - step1 * (prior * d1 + u[1])
                d2 = r2 + ratio1 * d1
                solution_ref[k, :, lanes] = step0 * b + step1 * d1 + step2 * d2
                residual_ref[k, :, lanes] = r2 - step2 * (prior * d2 + u[2])
            place, rest = divmod(start + (part + 1) * LANES, l_count // PIECES)
            if rest == 0:
                for pair in departures[2 * (place - 1) : 2 * place]:
                    for copy in pair:
                        copy.start()
    for pair in departures:
        for copy in pair:
            copy.wait()


def swap(x, axis):
    return lax.ppermute(x, axis, [(0, 1), (1, 0)])


def hop(x, distance):
    return lax.ppermute(x, "blk", [(i, i ^ distance) for i in range(lax.axis_size("blk"))])


def compact(
    rhs, legendre, beam, mixing, prior, inv_noise, mask_flags, cycle_len, cycle_slot, m_values
):
    comp_count, parts, m_own, l_count = rhs.shape
    block_count = lax.axis_size("blk")
    m_count = m_values.shape[0]
    channel_width, cycle_count = mask_flags.shape
    channel_count = beam.shape[0]
    count = cycle_count * m_count
    vmem = pl.BlockSpec(memory_space=pltpu.VMEM)
    flat = rhs
    inside = (parts, comp_count, l_count)
    in_sems = pltpu.SemaphoreType.DMA((1, parts))
    out_sems = pltpu.SemaphoreType.DMA((PIECES, parts))
    half = l_count // 2
    side_rows = half // WIDE * SIDE_ROWS
    hbm = pl.BlockSpec(memory_space=pltpu.HBM)
    operands = (
        flat, jnp.transpose(legendre[0]), beam, mixing, prior, inv_noise, jnp.transpose(mask_flags),
        cycle_len, cycle_slot, m_values,
    )
    spaces = [pltpu.VMEM] * 7 + [pltpu.SMEM] * 3
    rows = 2 * m_count
    small = channel_count * rows
    message, side, table = pl.pallas_call(
        gather_kernel,
        out_shape=[
            pltpu.VMEM((count, WIDE), BF16),
            pltpu.VMEM((side_rows, WIDE), BF16),
            pltpu.VMEM(operands[1].shape, BF16),
        ],
        in_specs=[hbm] * len(operands),
        out_specs=[vmem] * 3,
        scratch_shapes=[pltpu.VMEM(inside, F32)]
        + [space(x.shape, x.dtype) for space, x in zip(spaces[1:], operands[1:])]
        + [
            pltpu.VMEM((count, 2 * LANES), F32),
            pltpu.SemaphoreType.DMA((len(operands),)),
            in_sems,
        ],
        compiler_params=pltpu.CompilerParams(vmem_limit_bytes=40 * 1024 * 1024),
        name="gather_kernel",
    )(*[pltpu.with_memory_space_constraint(x, pltpu.HBM) for x in operands])
    both = jnp.concatenate([message, table], axis=1)

    def split(x, distances):
        pairs = [
            (g * block_count + i, g * block_count + (i ^ distances[g])) for g in range(2) for i in range(block_count)
        ]
        return lax.ppermute(x, ("groups", "blk"), pairs)

    other_side = swap(side, "comp")
    first, second = hop(both, 1), split(both, (3, 2))
    hops = [first[:, :WIDE], second[:, :WIDE], split(message, (2, 3))]
    legs = [first[:, WIDE:], second[:, WIDE:], swap(second[:, WIDE:], "groups")]
    tables = jnp.concatenate([table] + legs, axis=0)
    far_tables = swap(tables, "lat")
    messages = jnp.concatenate([message] + hops, axis=0)
    crossing = swap(messages, "comp")
    near = jnp.concatenate([messages, crossing], axis=0)
    far = swap(near, "lat")
    far_side = swap(other_side, "lat")

    def kernel(*refs):
        iterate_kernel(*refs, channel_width, m_count, block_count, side_rows)

    cycles = 2 * block_count * count
    answers = pl.pallas_call(
        kernel,
        out_shape=[jax.ShapeDtypeStruct(rhs.shape, F32)] * 2,
        in_specs=[vmem] * 9 + [hbm],
        out_specs=[hbm] * 2,
        scratch_shapes=[
            pltpu.VMEM((cycles, l_count), BF16),
            pltpu.VMEM((2 * small, l_count), BF16),
            pltpu.VMEM(prior.shape, F32),
        ]
        + [pltpu.VMEM(inside, F32)] * 3
        + [in_sems, out_sems, out_sems],
        compiler_params=pltpu.CompilerParams(vmem_limit_bytes=48 * 1024 * 1024),
        name="iterate_kernel",
    )(near, far, other_side, far_side, tables, far_tables, beam, mixing, prior, pltpu.with_memory_space_constraint(flat, pltpu.HBM))
    return tuple(answers)


def cycle_table(m_values, length, pixel_count):
    pixels = jnp.arange(pixel_count, dtype=jnp.int32)
    phase_ids = m_values[:, None] * (2 * pixels[None, :] + 1) % (2 * length)
    angles = math.pi * phase_ids.astype(jnp.float32) / length.astype(jnp.float32)
    inside = (pixels < length)[None, :]
    cosine = jnp.where(inside, jnp.cos(angles), jnp.float32(0.0))
    sine_part = jnp.where(inside, -jnp.sin(angles), jnp.float32(0.0))
    return jnp.stack([cosine, sine_part]).astype(jnp.bfloat16)


def distributed(
    rhs, legendre, beam, mixing, prior, inv_noise, mask_flags, cycle_len, cycle_slot, m_values
):
    cycle_count = inv_noise.shape[1]
    pixel_count = inv_noise.shape[2]
    channel_width = inv_noise.shape[0]
    owner_index = lax.axis_index("blk")
    comp_index = lax.axis_index("comp")
    local_ids = lax.dynamic_slice_in_dim(cycle_slot, owner_index * cycle_count, cycle_count)
    local_lengths = cycle_len[local_ids]
    legendre_slot = legendre[:, :, cycle_slot]
    weights = mask_flags.astype(jnp.float32)
    own_beam = lax.dynamic_slice_in_dim(beam, comp_index * channel_width, channel_width, 0)
    stored = jax.vmap(cycle_table, in_axes=(None, 0, None))(m_values, local_lengths, pixel_count)
    solution = jnp.zeros_like(rhs)
    residual = rhs
    direction = rhs
    for iteration in range(ITERS):
        local_mix = jnp.einsum("fc,ckml->fkml", mixing, direction, precision=HIGHEST_PRECISION)
        summed = lax.psum(local_mix.astype(jnp.bfloat16), "comp").astype(jnp.float32)
        own_part = lax.dynamic_slice_in_dim(summed, comp_index * channel_width, channel_width, 0)
        blended = (own_part * own_beam[:, None, None, :]).astype(jnp.bfloat16)
        coeffs = jnp.einsum(
            "fkml,mlr->fkmr", blended, legendre_slot, preferred_element_type=jnp.float32
        ).astype(jnp.bfloat16)
        arrived = lax.all_to_all(coeffs, "blk", split_axis=3, concat_axis=2, tiled=True)
        sky_map = jnp.einsum("fkmq,qkmp->fqp", arrived, stored, preferred_element_type=jnp.float32)
        weighted = (weights[:, :, None] * inv_noise * sky_map).astype(jnp.bfloat16)
        projected = jnp.einsum(
            "fqp,qkmp->fkmq", weighted, stored, preferred_element_type=jnp.float32
        ).astype(jnp.bfloat16)
        returned = lax.all_to_all(projected, "blk", split_axis=2, concat_axis=3, tiled=True)
        harmonic = jnp.einsum(
            "fkms,mls->fkml", returned, legendre_slot, preferred_element_type=jnp.float32
        )
        everyone = lax.all_gather(
            harmonic.astype(jnp.bfloat16), ("comp", "lat"), axis=0, tiled=True
        ).astype(harmonic.dtype)
        stacked = everyone.reshape(
            (lax.axis_size("comp"), lax.axis_size("lat"), channel_width) + harmonic.shape[1:]
        )
        summed_bands = jnp.sum(stacked, axis=1).reshape((-1,) + harmonic.shape[1:])
        backward = jnp.einsum(
            "fc,fkml->ckml",
            mixing,
            summed_bands * beam[:, None, None, :],
            precision=HIGHEST_PRECISION,
        )
        applied = prior[:, None, None, :] * direction + backward
        totals = lax.psum(
            (
                jnp.sum(direction * applied),
                jnp.sum(residual * applied),
                jnp.sum(applied * applied),
                jnp.sum(residual * residual),
            ),
            ("blk", "comp"),
        )
        curvature, cross_term, square, norm_now = totals
        step_size = norm_now / curvature
        solution = solution + step_size * direction
        residual = residual - step_size * applied
        norm_next = norm_now - 2.0 * step_size * cross_term + step_size * step_size * square
        direction = residual + norm_next / norm_now * direction
    return (solution, residual)


def fits(mesh, rhs, legendre, beam, mixing, inv_noise, m_values):
    sizes = dict(mesh.shape)
    m_count = m_values.shape[0]
    cycles = legendre.shape[2]
    slots = cycles // (sizes["blk"] * sizes["lat"])
    channels = beam.shape[0]
    width = channels // sizes["comp"]
    comps = mixing.shape[1] // sizes["comp"]
    l_count = legendre.shape[1]
    return (
        sizes["comp"] == 2
        and sizes["groups"] == 2
        and sizes["lat"] == 2
        and m_count == sizes["blk"] == 4
        and 2 * m_count == SUBLANES
        and cycles * m_count == LANES
        and slots * m_count == cycles // sizes["lat"] == 16
        and comps == channels
        and SIDE_ROWS - comps >= SUBLANES
        and (SIDE_ROWS - comps) * (WIDE // LANES) >= channels
        and channels % (SIDE_ROWS - comps) == 0
        and l_count % (2 * WIDE) == 0
        and channels % SUBLANES == 0
        and width * SUBLANES + 3 <= LANES
        and 2 * POWERS * channels <= 2 * LANES
        and l_count % WIDE == 0
        and inv_noise.shape[2] % WIDE == 0
        and rhs.shape[1] == 2
        and MOMENTS <= 16
    )


def solution(mesh):
    in_specs = (
        P(("groups", "comp"), None, "blk", None),
        P("blk", None, "lat"),
        P(),
        P(None, "comp"),
        P("comp", None),
        P("comp", ("blk", "lat"), None),
        P("comp", ("blk", "lat")),
        P("lat"),
        P("lat"),
        P(),
    )
    out_specs = (P(("groups", "comp"), None, "blk", None), P(("groups", "comp"), None, "blk", None))

    def whole(rhs, legendre, beam, mixing, prior, inv_noise, mask_flags, cycle_len, cycle_slot, m_values):
        small = fits(mesh, rhs, legendre, beam, mixing, inv_noise, m_values)
        local = compact if small else distributed
        mapped = jax.shard_map(local, mesh=mesh, in_specs=in_specs, out_specs=out_specs, check_vma=False)
        return mapped(
            rhs, legendre, beam, mixing, prior, inv_noise, mask_flags, cycle_len, cycle_slot, m_values
        )

    return whole
```

```python
import functools
import math

import jax
import jax.numpy as jnp
from jax import lax
from jax.experimental import pallas as pl
from jax.experimental.pallas import tpu as pltpu
from jax.sharding import PartitionSpec as P

ITERS = 3
LANES = 128
SUBLANES = 8
WIDE = 512
SIDE_ROWS = 32
PIECES = 2
MOMENTS = 2 * ITERS
POWERS = 2 * ITERS - 1
HIGHEST_PRECISION = lax.Precision.HIGHEST
F32 = jnp.float32
BF16 = jnp.bfloat16


def nt_dot(a, b):
    return lax.dot_general(a, b, (((1,), (1,)), ((), ())), preferred_element_type=F32)


def nn_dot(a, b):
    return jnp.dot(a, b, preferred_element_type=F32)


def iota(shape, dim):
    return lax.broadcasted_iota(jnp.int32, shape, dim)


def halves(x):
    high = x.astype(BF16)
    return high, (x - high.astype(F32)).astype(BF16)


def plane_copies(outside, inside, sems, inward):
    copies = []
    width = inside.shape[2] // sems.shape[0]
    for piece in range(sems.shape[0]):
        for k in range(inside.shape[0]):
            lanes = pl.ds(piece * width, width)
            pair = (outside.at[:, k, 0, lanes], inside.at[k, :, lanes])
            source, target = pair if inward else pair[::-1]
            copies.append(pltpu.make_async_copy(source, target, sems.at[piece, k]))
    return copies


def half_turn_sine(u):
    square = u * u
    total = jnp.full_like(u, -(math.pi**11) / math.factorial(11))
    for power in (9, 7, 5, 3, 1):
        sign = 1.0 if power % 4 == 1 else -1.0
        total = total * square + sign * math.pi**power / math.factorial(power)
    return total * u


def project(rhs_ref, legendre_ref, beam_ref, mixing_ref, prior_ref):
    comp_count, l_count = prior_ref.shape
    channel_count = beam_ref.shape[0]
    band_cycles = legendre_ref.shape[0]
    mixing = mixing_ref[...].astype(BF16)
    width = 256
    moments = [jnp.zeros((comp_count, 2 * width), F32) for n in range(MOMENTS)]
    used = POWERS * 2 * channel_count
    images = jnp.zeros((band_cycles, 2 * LANES), F32)
    filler = jnp.zeros((2 * LANES - used, width), F32)
    for start in range(0, l_count, width):
        lanes = slice(start, start + width)
        vector = jnp.concatenate([rhs_ref[k, :, lanes] for k in range(2)], axis=1)
        prior = jnp.concatenate([prior_ref[:, lanes]] * 2, axis=1)
        powers = [vector]
        for n in range(1, POWERS):
            powers.append(prior * powers[-1])
        for n in range(MOMENTS):
            moments[n] = moments[n] + powers[n // 2] * powers[n - n // 2]
        beam = beam_ref[:, lanes]
        blended = []
        for power in powers:
            mixed = nn_dot(mixing, power.astype(BF16))
            blended += [mixed[:, :width] * beam, mixed[:, width:] * beam]
        blended = jnp.concatenate(blended + [filler], axis=0).astype(BF16)
        images = images + nt_dot(legendre_ref[:, lanes], blended)
    return images, moments


def gather_kernel(
    rhs_in, legendre_in, beam_in, mixing_in, prior_in, noise_in, mask_in, len_in, slot_in, m_in,
    out_ref, side_ref, slotted_ref,
    rhs_ref, legendre_ref, beam_ref, mixing_ref, prior_ref, noise_ref, mask_ref, len_ref, slot_ref, m_ref,
    gram_ref, sems, rhs_sems,
):
    sources = (slot_in, len_in, m_in, mask_in, mixing_in, prior_in, beam_in, legendre_in, noise_in)
    targets = (slot_ref, len_ref, m_ref, mask_ref, mixing_ref, prior_ref, beam_ref, legendre_ref, noise_ref)
    copies = [pltpu.make_async_copy(a, b, sems.at[i]) for i, (a, b) in enumerate(zip(sources, targets))]
    copies = plane_copies(rhs_in, rhs_ref, rhs_sems, True) + copies
    for copy in copies:
        copy.start()
    channel_width, cycle_count, pixel_count = noise_ref.shape
    comp_count, l_count = prior_ref.shape
    m_count = m_ref.shape[0]
    band_cycles = legendre_ref.shape[0]
    rows = 2 * m_count
    owner = lax.axis_index("blk")
    band = lax.axis_index("lat")
    bands = lax.axis_size("lat")

    for copy in copies[:-1]:
        copy.wait()
    slot_rows = iota((band_cycles, 1), 0)
    slot_column = jnp.zeros((band_cycles, 1), jnp.int32)
    for n in range(band_cycles):
        slot_column = jnp.where(slot_rows == n, slot_ref[n], slot_column)
    order = jnp.where(slot_column == iota((band_cycles, band_cycles), 1), 1.0, 0.0).astype(BF16)
    slotted_ref[...] = nn_dot(order, legendre_ref[...]).astype(BF16)
    images, moments = project(rhs_ref, slotted_ref, beam_ref, mixing_ref, prior_ref)
    count = cycle_count * m_count
    message_rows = iota((count, LANES), 0)
    totals = jnp.zeros((count, LANES), F32)
    for n in range(MOMENTS):
        total = jnp.sum(jnp.sum(moments[n], axis=0, keepdims=True), axis=1, keepdims=True)
        totals = jnp.where(message_rows == n, total, totals)
    copies[-1].wait()

    row_ids = iota((rows, 1), 0)
    m_column = jnp.zeros((rows, 1), F32)
    for i in range(m_count):
        m_column = jnp.where(row_ids % m_count == i, m_ref[i].astype(F32), m_column)
    quarter = jnp.where(row_ids < m_count, 0.0, 0.25).astype(F32)
    chunk = min(WIDE, pixel_count)
    lengths = [len_ref[slot_ref[owner * cycle_count + q]] for q in range(cycle_count)]
    doubles = [jnp.full((rows, 1), (2 * n).astype(F32), F32) for n in lengths]
    inverses = [1.0 / double for double in doubles]
    sums = [jnp.zeros((rows, LANES), F32) for q in range(cycle_count)]
    padding = jnp.zeros((LANES - channel_width * rows, chunk), F32)
    for start in range(0, pixel_count, chunk):
        pixels = iota((rows, chunk), 1) + start
        phases = m_column * (2 * pixels + 1).astype(F32)
        for q in range(cycle_count):
            rest = phases - jnp.floor(phases * inverses[q] + 0.5) * doubles[q]
            turns = rest * inverses[q] + quarter
            turns = turns - jnp.floor(turns + 0.5)
            sine = half_turn_sine(turns)
            table = jnp.where(pixels < lengths[q], 1.0 - 2.0 * sine * sine, 0.0).astype(BF16)
            wide = table.astype(F32)
            weighted = [noise_ref[f, q : q + 1, start : start + chunk] * wide for f in range(channel_width)]
            weighted = jnp.concatenate(weighted + [padding], axis=0).astype(BF16)
            sums[q] = sums[q] + nt_dot(table, weighted)
    spread = jnp.where(iota((channel_width, LANES), 1) // rows == iota((channel_width, LANES), 0), 1.0, 0.0)
    flags = nn_dot(mask_ref[...].astype(F32).astype(BF16), spread.astype(BF16))
    for q in range(cycle_count):
        gram = sums[q] * flags[q : q + 1]
        gram_ref[q * m_count : (q + 1) * m_count, :LANES] = gram[:m_count]
        gram_ref[q * m_count : (q + 1) * m_count, LANES:] = gram[m_count:]

    lanes = iota((count, LANES), 1)
    first = gram_ref[:, :LANES]
    base = channel_width * rows
    for piece in range(3):
        part = totals.astype(BF16).astype(F32)
        first = jnp.where(lanes == base + piece, part, first)
        totals = totals - part
    out_ref[:, :LANES] = first.astype(BF16)
    out_ref[:, LANES : 2 * LANES] = gram_ref[:, LANES:].astype(BF16)
    out_ref[:, 2 * LANES :] = images.astype(BF16)
    half = l_count // 2
    spare = side_ref.shape[0] // (half // WIDE) - comp_count
    for piece in range(half // WIDE):
        lanes = pl.ds(pl.multiple_of(band * half + piece * WIDE, WIDE), WIDE)
        block = [prior_ref[:, lanes]]
        strips = []
        for i in range(WIDE // LANES):
            begin = i * spare
            if piece == 0 and begin < mixing_ref.shape[0]:
                strip = jnp.concatenate(
                    [mixing_ref[begin : begin + spare, :], jnp.zeros((spare, LANES - comp_count), F32)], axis=1
                )
            else:
                strip = jnp.zeros((spare, LANES), F32)
            strips.append(strip)
        block.append(jnp.concatenate(strips, axis=1))
        side_ref[piece * (comp_count + spare) : (piece + 1) * (comp_count + spare), :] = jnp.concatenate(
            block, axis=0
        ).astype(BF16)


def widen(talls, expand):
    small = expand.shape[0]
    rows = small // expand.shape[1]
    wide = nt_dot(jnp.concatenate([tall.astype(BF16) for tall in talls], axis=0), expand)
    same_row = iota((small, small), 0) % rows == iota((small, small), 1) % rows
    return [jnp.where(same_row, wide[i * small : (i + 1) * small], 0.0).astype(BF16) for i in range(len(talls))]


def expander(small, count):
    rows = small // count
    return jnp.where(iota((small, count), 0) // rows == iota((small, count), 1), 1.0, 0.0).astype(BF16)


def iterate_kernel(
    near_ref, far_ref, near_side_ref, far_side_ref, near_legendre_ref, far_legendre_ref, beam_ref, own_mixing_ref,
    own_prior_ref, rhs_in,
    solution_out, residual_out, legendre_ref, once_ref, other_prior_ref, rhs_ref, solution_ref, residual_ref,
    rhs_sems, solution_sems, residual_sems, channel_width, m_count, block_count, side_rows,
):
    arrivals = plane_copies(rhs_in, rhs_ref, rhs_sems, True)
    for copy in arrivals:
        copy.start()
    departures = plane_copies(solution_out, solution_ref, solution_sems, False)
    departures = list(zip(departures, plane_copies(residual_out, residual_ref, residual_sems, False)))
    comp_count, l_count = own_prior_ref.shape
    channel_count = beam_ref.shape[0]
    rows = 2 * m_count
    count = near_ref.shape[0] // (block_count * 2)
    cycles = 2 * block_count * count
    small = channel_count * rows
    base = channel_width * rows
    owner = lax.axis_index("blk")
    comp = lax.axis_index("comp")
    band = lax.axis_index("lat")

    half = l_count // 2
    step = side_rows // (half // WIDE)
    for ref, place in ((near_side_ref, band), (far_side_ref, 1 - band)):
        for piece in range(half // WIDE):
            lanes = pl.ds(pl.multiple_of(place * half + piece * WIDE, WIDE), WIDE)
            block = ref[piece * step : (piece + 1) * step, :].astype(F32)
            other_prior_ref[:, lanes] = block[:comp_count]
    span = block_count * count
    own_rows = jnp.concatenate([near_ref[:span, :], far_ref[:span, :]], axis=0).astype(F32)
    other_rows = jnp.concatenate([near_ref[span : 2 * span, :], far_ref[span : 2 * span, :]], axis=0).astype(F32)

    pieces_sum = own_rows[:, :LANES] + other_rows[:, :LANES]
    scalars = []
    for n in range(MOMENTS):
        total = jnp.zeros((1, LANES), F32)
        for i in range(block_count):
            total = total + pieces_sum[i * count + n : i * count + n + 1, :]
        lane = iota((1, LANES), 1)
        keep = (lane >= base) & (lane < base + 3)
        scalars.append(jnp.sum(jnp.where(keep, total, 0.0), axis=1, keepdims=True))

    legendre_ref[:span, :] = near_legendre_ref[...]
    legendre_ref[span:, :] = far_legendre_ref[...]
    part = lax.axis_index("groups")

    def block_of(lanes):
        place = lanes // count % block_count
        return jnp.where(place >= 2, place ^ 1 ^ part, place) ^ owner

    slots = count // m_count
    lane_m = block_of(iota((small, cycles), 1))
    same_m = iota((small, cycles), 0) % m_count == lane_m
    given = iota((cycles, cycles), 0)
    wanted = iota((cycles, cycles), 1)
    pick = (
        (given // span == wanted // span)
        & (given // m_count % slots == wanted % slots)
        & (given % m_count == block_of(wanted))
        & (block_of(given) == wanted // slots % block_count)
    )
    pick = jnp.where(pick, 1.0, 0.0).astype(BF16)
    images = jnp.transpose((own_rows + other_rows)[:, 2 * LANES :])
    width = 2 * channel_count
    images = jnp.concatenate([images[n * width : (n + 1) * width] for n in range(POWERS)], axis=1)
    high, low = halves(images)
    spread_row = iota((small, width), 0)
    spread_lane = iota((small, width), 1)
    spread = (spread_row // rows == spread_lane % channel_count) & (
        spread_row % rows // m_count == spread_lane // channel_count
    )
    spread = jnp.where(spread, 1.0, 0.0).astype(BF16)
    images = nn_dot(jnp.concatenate([spread, spread], axis=1), jnp.concatenate([high, low], axis=0))
    y = [jnp.where(same_m, images[:, n * cycles : (n + 1) * cycles], 0.0) for n in range(POWERS)]

    own_gram = nn_dot(jnp.transpose(own_rows[:, : 2 * LANES]).astype(BF16), pick)
    other_gram = nn_dot(jnp.transpose(other_rows[:, : 2 * LANES]).astype(BF16), pick)
    first_gram = jnp.where(comp == 0, own_gram, other_gram)
    second_gram = jnp.where(comp == 0, other_gram, own_gram)
    grams = []
    for k in range(2):
        gram = jnp.concatenate(
            [first_gram[k * LANES : k * LANES + base], second_gram[k * LANES : k * LANES + base]], axis=0
        )
        grams.append(gram.reshape(channel_count, rows, cycles))
    first_lane = iota((2 * cycles, cycles), 0) % cycles
    second_lane = iota((2 * cycles, cycles), 1)
    group = (first_lane // span == second_lane // span) & (first_lane % count == second_lane % count)
    group = jnp.where(group, 1.0, 0.0).astype(BF16)

    def sky(image):
        image = image.reshape(channel_count, rows, cycles)
        cosine = jnp.sum(image[:, :m_count], axis=1, keepdims=True)
        sine = jnp.sum(image[:, m_count:], axis=1, keepdims=True)
        product = (grams[0] * cosine + grams[1] * sine).reshape(small, cycles)
        high, low = halves(product)
        result = nn_dot(jnp.concatenate([high, low], axis=1), group)
        return jnp.where(same_m, result, 0.0)

    block = near_side_ref[:step, :].astype(F32)[comp_count:]
    strips = [block[:, i * LANES : i * LANES + comp_count] for i in range(channel_count // (step - comp_count))]
    other = jnp.concatenate(strips, axis=0).astype(BF16)
    own_mixing = own_mixing_ref[...].astype(BF16)
    both = (nt_dot(own_mixing, own_mixing) + nt_dot(other, other)).astype(BF16)
    expand = expander(small, channel_count)
    def repeat(x):
        x = x.astype(F32)
        return jnp.broadcast_to(x[:, None, :], (channel_count, rows, x.shape[1])).reshape(small, x.shape[1])

    talls = [repeat(both), nt_dot(expand, own_mixing), nt_dot(expand, other), repeat(own_mixing), repeat(other)]
    square_matrix, *widened = widen(talls, expand)
    spreads, gathers = widened[:2], widened[2:]
    priors = (own_prior_ref, other_prior_ref)

    def dot(a, b):
        return jnp.sum(jnp.sum(a * b, axis=0, keepdims=True), axis=1, keepdims=True)

    def total(x):
        return jnp.sum(jnp.sum(x, axis=0, keepdims=True), axis=1, keepdims=True)

    def harmonic(z):
        table = legendre_ref[...]
        beam = beam_ref[...][:, None, :]
        value = nn_dot(z.astype(BF16), table).reshape(channel_count, rows, l_count) * beam
        value = value.reshape(small, l_count).astype(BF16)
        return value

    def analyse(values):
        table = legendre_ref[...]
        beam = beam_ref[...][:, None, :]
        shaped = [value.reshape(channel_count, rows, l_count) * beam for value in values]
        images = [nt_dot(value.reshape(small, l_count).astype(BF16), table) for value in shaped]
        return [jnp.where(same_m, image, 0.0) for image in images]

    def first_pass(z):
        value = harmonic(z)
        (plain,) = analyse([nn_dot(square_matrix, value)])
        second = jnp.zeros((rows, l_count), F32)
        third = jnp.zeros((rows, l_count), F32)
        for side in range(2):
            prior = priors[side][...][:, None, :]
            once = nn_dot(spreads[side], value).reshape(comp_count, rows, l_count) * prior
            square = once * once
            second = second + jnp.sum(square, axis=0)
            third = third + jnp.sum(square * prior, axis=0)
            once = once.reshape(small, l_count).astype(BF16)
            once_ref[side * small : (side + 1) * small, :] = once
        (primed,) = analyse([nn_dot(jnp.concatenate(gathers, axis=1), once_ref[...])])
        return plain, primed, total(second), total(third)

    def second_pass(z):
        value = harmonic(z)
        (plain,) = analyse([nn_dot(square_matrix, value)])
        cross = jnp.zeros((rows, l_count), F32)
        own = jnp.zeros((rows, l_count), F32)
        for side in range(2):
            prior = priors[side][...][:, None, :]
            vector = nn_dot(spreads[side], value).reshape(comp_count, rows, l_count)
            once = once_ref[side * small : (side + 1) * small, :].astype(F32).reshape(comp_count, rows, l_count)
            primed = vector * prior
            cross = cross + jnp.sum(primed * once, axis=0)
            own = own + jnp.sum(vector * primed, axis=0)
        return plain, total(cross), total(own)

    s = scalars
    z0 = sky(y[0])
    y_plain0, y_prime0, pp00, ppp00 = first_pass(z0)
    norm0 = s[0]
    step0 = norm0 / (s[1] + dot(y[0], z0))
    p00, uu00 = dot(z0, y_prime0), dot(z0, y_plain0)
    by0, by1, by2, by3, by4 = [dot(y[n], z0) for n in range(5)]
    norm1 = s[0] - 2.0 * step0 * (s[1] + by0) + step0 * step0 * (s[2] + 2.0 * by1 + uu00)
    ratio0 = norm1 / norm0
    y_r1 = y[0] - step0 * (y[1] + y_plain0)
    y_d1 = y_r1 + ratio0 * y[0]
    e0, e1, e2 = 1.0 + ratio0, -step0, -step0
    z1 = sky(y_d1)
    y_plain1, p2_01, p_11 = second_pass(z1)
    quadratic1 = (
        e0 * e0 * s[1] + 2.0 * e0 * e1 * s[2] + e1 * e1 * s[3]
        + 2.0 * e0 * e2 * by1 + 2.0 * e1 * e2 * by2 + e2 * e2 * p00
    )
    step1 = norm1 / (quadratic1 + dot(y_d1, z1))
    y_pd1 = e0 * y[1] + e1 * y[2] + e2 * y_prime0
    h0, h1, h2 = 1.0 + 0.0 * step1, -step0 - step1 * e0, -step1 * e1
    h3, h4, h5 = -step0, -step1 * e2, -step1
    b1y = [dot(y[n], z1) for n in range(4)]
    uu01, p01, uu11 = dot(z1, y_plain0), dot(z1, y_prime0), dot(z1, y_plain1)
    norm2 = (
        h0 * h0 * s[0] + 2.0 * h0 * h1 * s[1] + (h1 * h1 + 2.0 * h0 * h2) * s[2]
        + 2.0 * h1 * h2 * s[3] + h2 * h2 * s[4]
        + 2.0 * h3 * (h0 * by0 + h1 * by1 + h2 * by2)
        + 2.0 * h4 * (h0 * by1 + h1 * by2 + h2 * by3)
        + 2.0 * h5 * (h0 * b1y[0] + h1 * b1y[1] + h2 * b1y[2])
        + h3 * h3 * uu00 + 2.0 * h3 * h4 * p00 + h4 * h4 * pp00
        + 2.0 * h3 * h5 * uu01 + 2.0 * h4 * h5 * p01 + h5 * h5 * uu11
    )
    ratio1 = norm2 / norm1
    y_d2 = y_r1 - step1 * (y_pd1 + y_plain1) + ratio1 * y_d1
    z2 = sky(y_d2)
    h0, h1, h3 = h0 + ratio1 * e0, h1 + ratio1 * e1, h3 + ratio1 * e2
    quadratic2 = (
        h0 * h0 * s[1] + 2.0 * h0 * h1 * s[2] + (h1 * h1 + 2.0 * h0 * h2) * s[3]
        + 2.0 * h1 * h2 * s[4] + h2 * h2 * s[5]
        + 2.0 * h3 * (h0 * by1 + h1 * by2 + h2 * by3)
        + 2.0 * h4 * (h0 * by2 + h1 * by3 + h2 * by4)
        + 2.0 * h5 * (h0 * b1y[1] + h1 * b1y[2] + h2 * b1y[3])
        + h3 * h3 * p00 + 2.0 * h3 * h4 * pp00 + h4 * h4 * ppp00
        + 2.0 * h3 * h5 * p01 + 2.0 * h4 * h5 * p2_01 + h5 * h5 * p_11
    )
    step2 = norm2 / (quadratic2 + dot(y_d2, z2))

    mine_row = iota((width, small), 0)
    mine_lane = iota((width, small), 1)
    mine = (mine_lane // rows == mine_row % channel_count) & (
        mine_lane % rows == mine_row // channel_count * m_count + owner
    )
    mine = jnp.where(mine, 1.0, 0.0).astype(BF16)
    stacked = jnp.concatenate([z.astype(BF16) for z in (z0, z1, z2)], axis=1)
    stacked = nn_dot(mine, stacked).astype(BF16)
    stacked = jnp.concatenate([stacked[:, i * cycles : (i + 1) * cycles] for i in range(ITERS)], axis=0)
    for copy in arrivals:
        copy.wait()
    value = nn_dot(stacked, legendre_ref[...])
    value = [value[i * channel_count : (i + 1) * channel_count] * beam_ref[...] for i in range(2 * ITERS)]
    value = jnp.concatenate(value, axis=1).astype(BF16)
    vectors = lax.dot_general(own_mixing, value, (((0,), (0,)), ((), ())), preferred_element_type=F32)
    start, chunk = 0, l_count
    if True:
        for part in range(chunk // LANES):
            prior = own_prior_ref[:, start + part * LANES : start + (part + 1) * LANES]
            for k in range(2):
                lanes = slice(start + part * LANES, start + (part + 1) * LANES)
                u = []
                for i in range(ITERS):
                    begin = (2 * i + k) * chunk + part * LANES
                    u.append(vectors[:, begin : begin + LANES])
                b = rhs_ref[k, :, lanes]
                r1 = b - step0 * (prior * b + u[0])
                d1 = r1 + ratio0 * b
                r2 = r1 - step1 * (prior * d1 + u[1])
                d2 = r2 + ratio1 * d1
                solution_ref[k, :, lanes] = step0 * b + step1 * d1 + step2 * d2
                residual_ref[k, :, lanes] = r2 - step2 * (prior * d2 + u[2])
            place, rest = divmod(start + (part + 1) * LANES, l_count // PIECES)
            if rest == 0:
                for pair in departures[2 * (place - 1) : 2 * place]:
                    for copy in pair:
                        copy.start()
    for pair in departures:
        for copy in pair:
            copy.wait()


def swap(x, axis):
    return lax.ppermute(x, axis, [(0, 1), (1, 0)])


def hop(x, distance):
    return lax.ppermute(x, "blk", [(i, i ^ distance) for i in range(lax.axis_size("blk"))])


def compact(
    rhs, legendre, beam, mixing, prior, inv_noise, mask_flags, cycle_len, cycle_slot, m_values
):
    comp_count, parts, m_own, l_count = rhs.shape
    block_count = lax.axis_size("blk")
    m_count = m_values.shape[0]
    channel_width, cycle_count = mask_flags.shape
    channel_count = beam.shape[0]
    count = cycle_count * m_count
    vmem = pl.BlockSpec(memory_space=pltpu.VMEM)
    flat = rhs
    inside = (parts, comp_count, l_count)
    in_sems = pltpu.SemaphoreType.DMA((1, parts))
    out_sems = pltpu.SemaphoreType.DMA((PIECES, parts))
    half = l_count // 2
    side_rows = half // WIDE * SIDE_ROWS
    hbm = pl.BlockSpec(memory_space=pltpu.HBM)
    operands = (
        flat, jnp.transpose(legendre[0]), beam, mixing, prior, inv_noise, jnp.transpose(mask_flags),
        cycle_len, cycle_slot, m_values,
    )
    spaces = [pltpu.VMEM] * 7 + [pltpu.SMEM] * 3
    rows = 2 * m_count
    small = channel_count * rows
    message, side, table = pl.pallas_call(
        gather_kernel,
        out_shape=[
            pltpu.VMEM((count, WIDE), BF16),
            pltpu.VMEM((side_rows, WIDE), BF16),
            pltpu.VMEM(operands[1].shape, BF16),
        ],
        in_specs=[hbm] * len(operands),
        out_specs=[vmem] * 3,
        scratch_shapes=[pltpu.VMEM(inside, F32)]
        + [space(x.shape, x.dtype) for space, x in zip(spaces[1:], operands[1:])]
        + [
            pltpu.VMEM((count, 2 * LANES), F32),
            pltpu.SemaphoreType.DMA((len(operands),)),
            in_sems,
        ],
        compiler_params=pltpu.CompilerParams(vmem_limit_bytes=40 * 1024 * 1024),
        name="gather_kernel",
    )(*[pltpu.with_memory_space_constraint(x, pltpu.HBM) for x in operands])
    both = jnp.concatenate([message, table], axis=1)

    def split(x, distances):
        pairs = [
            (g * block_count + i, g * block_count + (i ^ distances[g])) for g in range(2) for i in range(block_count)
        ]
        return lax.ppermute(x, ("groups", "blk"), pairs)

    other_side = swap(side, "comp")
    first, second = hop(both, 1), split(both, (3, 2))
    hops = [first[:, :WIDE], second[:, :WIDE], split(message, (2, 3))]
    legs = [first[:, WIDE:], second[:, WIDE:], swap(second[:, WIDE:], "groups")]
    tables = jnp.concatenate([table] + legs, axis=0)
    far_tables = swap(tables, "lat")
    messages = jnp.concatenate([message] + hops, axis=0)
    crossing = swap(messages, "comp")
    near = jnp.concatenate([messages, crossing], axis=0)
    far = swap(near, "lat")
    far_side = swap(other_side, "lat")

    def kernel(*refs):
        iterate_kernel(*refs, channel_width, m_count, block_count, side_rows)

    cycles = 2 * block_count * count
    answers = pl.pallas_call(
        kernel,
        out_shape=[jax.ShapeDtypeStruct(rhs.shape, F32)] * 2,
        in_specs=[vmem] * 9 + [hbm],
        out_specs=[hbm] * 2,
        scratch_shapes=[
            pltpu.VMEM((cycles, l_count), BF16),
            pltpu.VMEM((2 * small, l_count), BF16),
            pltpu.VMEM(prior.shape, F32),
        ]
        + [pltpu.VMEM(inside, F32)] * 3
        + [in_sems, out_sems, out_sems],
        compiler_params=pltpu.CompilerParams(vmem_limit_bytes=48 * 1024 * 1024),
        name="iterate_kernel",
    )(near, far, other_side, far_side, tables, far_tables, beam, mixing, prior, pltpu.with_memory_space_constraint(flat, pltpu.HBM))
    return tuple(answers)


def cycle_table(m_values, length, pixel_count):
    pixels = jnp.arange(pixel_count, dtype=jnp.int32)
    phase_ids = m_values[:, None] * (2 * pixels[None, :] + 1) % (2 * length)
    angles = math.pi * phase_ids.astype(jnp.float32) / length.astype(jnp.float32)
    inside = (pixels < length)[None, :]
    cosine = jnp.where(inside, jnp.cos(angles), jnp.float32(0.0))
    sine_part = jnp.where(inside, -jnp.sin(angles), jnp.float32(0.0))
    return jnp.stack([cosine, sine_part]).astype(jnp.bfloat16)


def distributed(
    rhs, legendre, beam, mixing, prior, inv_noise, mask_flags, cycle_len, cycle_slot, m_values
):
    cycle_count = inv_noise.shape[1]
    pixel_count = inv_noise.shape[2]
    channel_width = inv_noise.shape[0]
    owner_index = lax.axis_index("blk")
    comp_index = lax.axis_index("comp")
    local_ids = lax.dynamic_slice_in_dim(cycle_slot, owner_index * cycle_count, cycle_count)
    local_lengths = cycle_len[local_ids]
    legendre_slot = legendre[:, :, cycle_slot]
    weights = mask_flags.astype(jnp.float32)
    own_beam = lax.dynamic_slice_in_dim(beam, comp_index * channel_width, channel_width, 0)
    stored = jax.vmap(cycle_table, in_axes=(None, 0, None))(m_values, local_lengths, pixel_count)
    solution = jnp.zeros_like(rhs)
    residual = rhs
    direction = rhs
    for iteration in range(ITERS):
        local_mix = jnp.einsum("fc,ckml->fkml", mixing, direction, precision=HIGHEST_PRECISION)
        summed = lax.psum(local_mix.astype(jnp.bfloat16), "comp").astype(jnp.float32)
        own_part = lax.dynamic_slice_in_dim(summed, comp_index * channel_width, channel_width, 0)
        blended = (own_part * own_beam[:, None, None, :]).astype(jnp.bfloat16)
        coeffs = jnp.einsum(
            "fkml,mlr->fkmr", blended, legendre_slot, preferred_element_type=jnp.float32
        ).astype(jnp.bfloat16)
        arrived = lax.all_to_all(coeffs, "blk", split_axis=3, concat_axis=2, tiled=True)
        sky_map = jnp.einsum("fkmq,qkmp->fqp", arrived, stored, preferred_element_type=jnp.float32)
        weighted = (weights[:, :, None] * inv_noise * sky_map).astype(jnp.bfloat16)
        projected = jnp.einsum(
            "fqp,qkmp->fkmq", weighted, stored, preferred_element_type=jnp.float32
        ).astype(jnp.bfloat16)
        returned = lax.all_to_all(projected, "blk", split_axis=2, concat_axis=3, tiled=True)
        harmonic = jnp.einsum(
            "fkms,mls->fkml", returned, legendre_slot, preferred_element_type=jnp.float32
        )
        everyone = lax.all_gather(
            harmonic.astype(jnp.bfloat16), ("comp", "lat"), axis=0, tiled=True
        ).astype(harmonic.dtype)
        stacked = everyone.reshape(
            (lax.axis_size("comp"), lax.axis_size("lat"), channel_width) + harmonic.shape[1:]
        )
        summed_bands = jnp.sum(stacked, axis=1).reshape((-1,) + harmonic.shape[1:])
        backward = jnp.einsum(
            "fc,fkml->ckml",
            mixing,
            summed_bands * beam[:, None, None, :],
            precision=HIGHEST_PRECISION,
        )
        applied = prior[:, None, None, :] * direction + backward
        totals = lax.psum(
            (
                jnp.sum(direction * applied),
                jnp.sum(residual * applied),
                jnp.sum(applied * applied),
                jnp.sum(residual * residual),
            ),
            ("blk", "comp"),
        )
        curvature, cross_term, square, norm_now = totals
        step_size = norm_now / curvature
        solution = solution + step_size * direction
        residual = residual - step_size * applied
        norm_next = norm_now - 2.0 * step_size * cross_term + step_size * step_size * square
        direction = residual + norm_next / norm_now * direction
    return (solution, residual)


def fits(mesh, rhs, legendre, beam, mixing, inv_noise, m_values):
    sizes = dict(mesh.shape)
    m_count = m_values.shape[0]
    cycles = legendre.shape[2]
    slots = cycles // (sizes["blk"] * sizes["lat"])
    channels = beam.shape[0]
    width = channels // sizes["comp"]
    comps = mixing.shape[1] // sizes["comp"]
    l_count = legendre.shape[1]
    return (
        sizes["comp"] == 2
        and sizes["groups"] == 2
        and sizes["lat"] == 2
        and m_count == sizes["blk"] == 4
        and 2 * m_count == SUBLANES
        and cycles * m_count == LANES
        and slots * m_count == cycles // sizes["lat"] == 16
        and comps == channels
        and SIDE_ROWS - comps >= SUBLANES
        and (SIDE_ROWS - comps) * (WIDE // LANES) >= channels
        and channels % (SIDE_ROWS - comps) == 0
        and l_count % (2 * WIDE) == 0
        and channels % SUBLANES == 0
        and width * SUBLANES + 3 <= LANES
        and 2 * POWERS * channels <= 2 * LANES
        and l_count % WIDE == 0
        and inv_noise.shape[2] % WIDE == 0
        and rhs.shape[1] == 2
        and MOMENTS <= 16
    )


def solution(mesh):
    in_specs = (
        P(("groups", "comp"), None, "blk", None),
        P("blk", None, "lat"),
        P(),
        P(None, "comp"),
        P("comp", None),
        P("comp", ("blk", "lat"), None),
        P("comp", ("blk", "lat")),
        P("lat"),
        P("lat"),
        P(),
    )
    out_specs = (P(("groups", "comp"), None, "blk", None), P(("groups", "comp"), None, "blk", None))

    def whole(rhs, legendre, beam, mixing, prior, inv_noise, mask_flags, cycle_len, cycle_slot, m_values):
        small = fits(mesh, rhs, legendre, beam, mixing, inv_noise, m_values)
        local = compact if small else distributed
        mapped = jax.shard_map(local, mesh=mesh, in_specs=in_specs, out_specs=out_specs, check_vma=False)
        return mapped(
            rhs, legendre, beam, mixing, prior, inv_noise, mask_flags, cycle_len, cycle_slot, m_values
        )

    return whole
```
